32 devices in a mesh: seq: 8 (over z, y), tensor: 4 (over x, core).
Axes of the slice: x: 2, y: 2, z: 4, core: 2. Of those that a mesh axis runs over, the one named last changes fastest.
Arguments:
- hidden_in: float32 [2048, 3840], P('seq'), may hold values from -6 to 6
- query_proj: float32 [3840, 4096], P(None, 'tensor'), may hold values from -0.09375 to 0.09375
- key_proj: float32 [3840, 2048], P(None, 'tensor'), may hold values from -0.09375 to 0.09375
- value_proj: float32 [3840, 2048], P(None, 'tensor'), may hold values from -0.09375 to 0.09375
- query_gain: float32 [256], replicated, may hold values from 0.1 to 1.9
- key_gain: float32 [256], replicated, may hold values from 0.1 to 1.9
- segment_ids: int32 [2048], replicated, may hold values from 0 to 3, never falling along the last dimension, each value on 1 to 1024 neighbouring positions
- grad_out: float32 [2048, 4096], P('seq', 'tensor'), may hold values from -6 to 6
Outputs:
- attended: float32 [2048, 4096], P('seq', 'tensor')
- grad_input: float32 [2048, 3840], P('seq', 'tensor')
- grad_query: float32 [3840, 4096], P('seq', 'tensor')
- grad_key: float32 [3840, 2048], P('seq', 'tensor')
- grad_value: float32 [3840, 2048], P('seq', 'tensor')
The draws below stay inside these ranges and needn't reach their ends.
Inputs may be any that keep to these rules, and one draw needn't show every extreme that they name: `segment_ids`: segment ids never fall along the transcript; each of the 4 documents holds 1 to 1024 tokens and one holds exactly 1024.
All inputs are finite; a program needn't handle non-finite values.
Results may differ from the reference program's by a relative error of at most 0.0003.
Values sent between devices are 32-bit elements; how exact they have to be, the bound alone decides.
No kernel may reach another device: no remote copies, remote signals or barrier semaphores. Data moves between devices by JAX's collectives and lax.ppermute only.
A program may use at most 192 MiB of HBM per device.

```python
import math
import jax
import jax.numpy as jnp
import numpy as np
from jax import lax

D = 3840
HEADS = 16
KV_HEADS = 8
HEAD_DIM = 256
WINDOW = 1024
TOK_DEV = 256
SEQ = 2048


def steps_of(own_key, extent, split, least, largest):
    level = 1.0
    for position, shards_of in split:
        steps = jax.random.uniform(jax.random.fold_in(jax.random.fold_in(own_key, 6), position), (shards_of,), jnp.float32, least / len(split), largest / len(split))
        level = level * jnp.repeat(jnp.exp(steps), extent[position] // shards_of).reshape((-1,) + (1,) * (len(extent) - 1 - position))
    return level


def length_profile(count, total, bound, lean):
    portions = [(1 << 20) // math.isqrt(standing ** lean) + 1 for standing in range(2, count + 1)]
    surplus, given = total - bound - (count - 1), [1] * (count - 1)
    while surplus > 0:
        candidates = [i for i in range(count - 1) if given[i] < bound]
        mass, left = sum([portions[i] for i in candidates]), surplus
        for i in candidates:
            more = min(bound - given[i], max(1, left * portions[i] // mass), surplus)
            given[i] = given[i] + more
            surplus = surplus - more
    return np.array([bound] + given)


def uneven(rng, count, total, most, lean):
    if count == 2:
        one = jax.random.randint(rng, (), max(1, total - most), min(most, total - 1) + 1)
        return jnp.stack([one, total - one])
    tallies = jnp.asarray(length_profile(count, total, most, lean), jnp.int32)
    twos = (count - 1) // 2
    source_of, sink = tallies[1:1 + 2 * twos:2], tallies[2:2 + 2 * twos:2]
    margin = jnp.minimum(source_of - 1, most - sink)
    passed = jax.random.randint(jax.random.fold_in(rng, 1), (twos,), 0, 1 << 20) % (margin + 1)
    tallies = tallies.at[1:1 + 2 * twos:2].set(source_of - passed).at[2:2 + 2 * twos:2].set(sink + passed)
    return tallies[jax.random.permutation(jax.random.fold_in(rng, 2), count)]


def gaussian(key, shape, scale, limit, split=(), kind=jnp.bfloat16):
    result = jax.random.normal(key, shape, jnp.float32) * scale
    if len(split) > 0:
        result = steps_of(key, shape, split, -0.22, 0.18) * result
    return jnp.clip(result, min=-limit, max=limit).astype(kind)


def setup_inputs(seed: int = 0) -> dict:
    key_of = jax.random.split(jax.random.key(seed), 9)
    hidden_in = gaussian(key_of[0], (SEQ, D), 1.0, 6.0, ((0, 8),), jnp.float32)
    query_proj = gaussian(key_of[1], (D, HEADS * HEAD_DIM), D ** -0.5, 0.09375, ((1, 4),), jnp.float32)
    key_proj = gaussian(key_of[2], (D, KV_HEADS * HEAD_DIM), D ** -0.5, 0.09375, ((1, 4),), jnp.float32)
    value_proj = gaussian(key_of[3], (D, KV_HEADS * HEAD_DIM), D ** -0.5, 0.09375, ((1, 4),), jnp.float32)
    query_gain = jnp.clip(1.0 + 0.18 * jax.random.normal(key_of[4], (HEAD_DIM,), jnp.float32), 0.1, 1.9)
    key_gain = jnp.clip(1.0 + 0.18 * jax.random.normal(key_of[5], (HEAD_DIM,), jnp.float32), 0.1, 1.9)
    segment_ids = jnp.searchsorted(jnp.cumsum(uneven(key_of[6], 4, SEQ, SEQ // 2, 1)), jnp.arange(SEQ), side="right").astype(jnp.int32)
    grad_out = gaussian(key_of[7], (SEQ, HEADS * HEAD_DIM), 1.0, 6.0, ((0, 8), (1, 4)), jnp.float32)
    return {"hidden_in": hidden_in, "query_proj": query_proj, "key_proj": key_proj, "value_proj": value_proj, "query_gain": query_gain, "key_gain": key_gain, "segment_ids": segment_ids, "grad_out": grad_out}


highest = lax.Precision.HIGHEST
epsilon = 1e-06

def rms_gain(vector, scaling):
    mean_sq = lax.optimization_barrier(jnp.mean(vector * vector, axis=-1, keepdims=True))
    return vector * lax.rsqrt(mean_sq + epsilon) * scaling

def rotate(vector, cosine, sines):
    middle = vector.shape[-1] // 2
    turned = jnp.concatenate([-vector[..., middle:], vector[..., :middle]], axis=-1)
    return vector * cosine + turned * sines

def rope_tables(positions, head_width):
    middle = head_width // 2
    exponent = 2.0 * jnp.arange(middle).astype(jnp.float32) / head_width
    frequency = 10000.0 ** (-exponent)
    angles = positions.astype(jnp.float32)[:, None] * frequency[None, :]
    angles = jnp.concatenate([angles, angles], axis=-1)
    return (jnp.cos(angles)[:, None, :], jnp.sin(angles)[:, None, :])

def forward(hidden_in, query_proj, key_proj, value_proj, query_gain, key_gain, segment_ids):
    per_kv = HEADS // KV_HEADS
    queries = jnp.dot(hidden_in, query_proj, precision=highest).reshape(SEQ, KV_HEADS, per_kv, HEAD_DIM)
    key_raw = jnp.dot(hidden_in, key_proj, precision=highest).reshape(SEQ, KV_HEADS, HEAD_DIM)
    values = jnp.dot(hidden_in, value_proj, precision=highest).reshape(SEQ, KV_HEADS, HEAD_DIM)
    cosine, sines = rope_tables(jnp.arange(SEQ).astype(jnp.int32), HEAD_DIM)
    q_rot = rotate(rms_gain(queries, query_gain), cosine[:, None], sines[:, None])
    k_rot = rotate(rms_gain(key_raw, key_gain), cosine, sines)
    k_pad = jnp.concatenate([jnp.zeros((WINDOW, KV_HEADS, HEAD_DIM), jnp.float32), k_rot], axis=0)
    v_pad = jnp.concatenate([jnp.zeros((WINDOW, KV_HEADS, HEAD_DIM), jnp.float32), values], axis=0)
    seg_pad = jnp.concatenate([jnp.full((WINDOW,), -1, jnp.int32), segment_ids.astype(jnp.int32)])
    factor = HEAD_DIM ** (-0.5)

    def one_block(first_row):
        q_block = lax.dynamic_slice_in_dim(q_rot, first_row, TOK_DEV, 0)
        k_block = lax.dynamic_slice_in_dim(k_pad, first_row, TOK_DEV + WINDOW, 0)
        v_block = lax.dynamic_slice_in_dim(v_pad, first_row, TOK_DEV + WINDOW, 0)
        query_seg = lax.dynamic_slice_in_dim(segment_ids.astype(jnp.int32), first_row, TOK_DEV, 0)
        key_seg = lax.dynamic_slice_in_dim(seg_pad, first_row, TOK_DEV + WINDOW, 0)
        query_pos = first_row + jnp.arange(TOK_DEV).astype(jnp.int32)
        key_pos = first_row - WINDOW + jnp.arange(TOK_DEV + WINDOW).astype(jnp.int32)
        distance = query_pos[:, None] - key_pos[None, :]
        allowed = (key_pos[None, :] >= 0) & (distance >= 0) & (distance < WINDOW) & (query_seg[:, None] == key_seg[None, :])
        scores = jnp.einsum('tkgd,skd->kgts', q_block, k_block, precision=highest) * factor
        weights = jnp.where(allowed, jnp.exp(scores), 0.0)
        shares = weights / lax.optimization_barrier(jnp.sum(weights, axis=-1, keepdims=True))
        return jnp.einsum('kgts,skd->tkgd', shares, v_block, precision=highest)
    starts = jnp.arange(SEQ // TOK_DEV).astype(jnp.int32) * TOK_DEV
    blocks = lax.map(one_block, starts)
    return blocks.reshape(SEQ, HEADS * HEAD_DIM)

def reference(hidden_in, query_proj, key_proj, value_proj, query_gain, key_gain, segment_ids, grad_out):

    def project_all(inputs, w_query, w_key, w_value):
        return forward(inputs, w_query, w_key, w_value, query_gain, key_gain, segment_ids)
    attended, pullback = jax.vjp(project_all, hidden_in, query_proj, key_proj, value_proj)
    grad_input, grad_query, grad_key, grad_value = pullback(grad_out)
    return (attended, grad_input, grad_query, grad_key, grad_value)
```

```python
import jax
import jax.numpy as jnp
from jax import lax
from jax.sharding import PartitionSpec as P

WINDOW = 1024
CHAIN = 4

fine = lax.Precision.HIGH
epsilon = 1e-06


def dot_nn(left, right):
    return lax.dot_general(left, right, (((1,), (0,)), ((), ())), precision=fine)


def dot_nt(left, right):
    return lax.dot_general(left, right, (((1,), (1,)), ((), ())), precision=fine)


def dot_tn(left, right):
    return lax.dot_general(left, right, (((0,), (0,)), ((), ())), precision=fine)


def rope_tables(positions, head_width):
    middle = head_width // 2
    exponent = 2.0 * jnp.arange(middle).astype(jnp.float32) / head_width
    frequency = 10000.0 ** (-exponent)
    angles = positions.astype(jnp.float32)[:, None] * frequency[None, :]
    return jnp.cos(angles), jnp.sin(angles)


def inverse_rms(vector):
    return lax.rsqrt(jnp.mean(vector * vector, axis=-1, keepdims=True) + epsilon)


def norm_rotate(vector, scaling, cosine, sine):
    middle = vector.shape[-1] // 2
    normed = vector * inverse_rms(vector) * scaling
    low, high = normed[:, :middle], normed[:, middle:]
    return jnp.concatenate([low * cosine - high * sine, high * cosine + low * sine], axis=1)


def norm_rotate_back(grad, vector, scaling, cosine, sine):
    middle = vector.shape[-1] // 2
    low, high = grad[:, :middle], grad[:, middle:]
    d_normed = jnp.concatenate([low * cosine + high * sine, high * cosine - low * sine], axis=1)
    d_normed = d_normed * scaling
    inverse = inverse_rms(vector)
    unit = vector * inverse
    return inverse * (d_normed - unit * jnp.mean(d_normed * unit, axis=-1, keepdims=True))


def local(hidden_in, query_proj, key_proj, value_proj, query_gain, key_gain, segment_ids, grad_out):
    rows_dev, width = hidden_in.shape
    head = query_gain.shape[0]
    kv_local = key_proj.shape[1] // head
    q_local = query_proj.shape[1] // head
    per_kv = q_local // kv_local
    count = lax.axis_size("seq")
    pair = count // CHAIN
    members = lax.axis_size("tensor")
    member = lax.axis_index("tensor")
    seq_index = lax.axis_index("seq")
    along = seq_index // pair
    across = seq_index % pair
    reach = (WINDOW - 1) // rows_dev + 1
    span = (reach + 1) * rows_dev

    def z_shift(block, step):
        route = [(i, i + step * pair) for i in range(count) if 0 <= i + step * pair < count]
        return lax.ppermute(block, "seq", route)

    def z_ring(block, step):
        return lax.ppermute(block, "seq", [(i, (i + step * pair) % count) for i in range(count)])

    def y_ring(block, step):
        route = [(i, i // pair * pair + (i + step) % pair) for i in range(count)]
        return lax.ppermute(block, "seq", route)

    def shifted(block, distance):
        route = [(i - distance, i) for i in range(count) if 0 <= i - distance < count]
        return lax.ppermute(block, "seq", route)

    slab = width // CHAIN
    part = width // count
    piece = rows_dev // members
    my_rows = lax.dynamic_slice_in_dim(hidden_in, member * piece, piece, 0)
    pieces = []
    for step in range(1, CHAIN):
        target = (along + step) % CHAIN
        pieces.append(z_ring(lax.dynamic_slice_in_dim(my_rows, target * slab, slab, 1), step))

    first_row = seq_index * rows_dev
    positions = first_row + jnp.arange(rows_dev, dtype=jnp.int32)
    cosine, sine = rope_tables(positions, head)

    def heads_of(array):
        return [array[:, h * head : (h + 1) * head] for h in range(array.shape[1] // head)]

    def joined(blocks):
        return jnp.concatenate(blocks, axis=1)

    key_raw = dot_nn(hidden_in, key_proj)
    k_rot = joined([norm_rotate(u, key_gain, cosine, sine) for u in heads_of(key_raw)])
    values = dot_nn(hidden_in, value_proj)

    def spread(own):
        if pair != 2 or reach != 4:
            return [shifted(own, distance) for distance in range(reach, 0, -1)] + [own]
        two = z_shift(own, 1)
        four = z_shift(two, 1)
        one = y_ring(jnp.where(across == 0, own, two), 1)
        three = y_ring(jnp.where(across == 0, two, four), 1)
        return [four, three, two, one, own]

    def collect(parts):
        if pair != 2 or reach != 4:
            total = parts[reach]
            for distance in range(1, reach + 1):
                total = total + shifted(parts[reach - distance], -distance)
            return total
        four, three, two, one, own = parts
        from_three = y_ring(three, 1)
        from_one = y_ring(one, 1)
        from_four = z_shift(four + jnp.where(across == 0, 0.0, from_three), -1)
        from_two = z_shift(two + jnp.where(across == 0, from_three, from_one) + from_four, -1)
        return own + jnp.where(across == 0, from_one, 0.0) + from_two

    key_window = jnp.concatenate(spread(k_rot), axis=0)
    value_window = jnp.concatenate(spread(values), axis=0)

    queries = dot_nn(hidden_in, query_proj)
    query_heads = heads_of(queries)
    grad_heads = heads_of(grad_out)
    q_rot = [norm_rotate(u, query_gain, cosine, sine) for u in query_heads]

    seg_pad = jnp.concatenate([jnp.full((reach * rows_dev,), -1, jnp.int32), segment_ids])
    key_seg = lax.dynamic_slice_in_dim(seg_pad, first_row, span, 0)
    query_seg = lax.dynamic_slice_in_dim(segment_ids, first_row, rows_dev, 0)
    key_pos = first_row - reach * rows_dev + jnp.arange(span, dtype=jnp.int32)
    distance = positions[:, None] - key_pos[None, :]
    allowed = (
        (key_pos[None, :] >= 0)
        & (distance >= 0)
        & (distance < WINDOW)
        & (query_seg[:, None] == key_seg[None, :])
    )
    allowed = jnp.concatenate([allowed] * per_kv, axis=0)
    factor = head ** (-0.5)

    attended, d_queries, d_krot, d_values = [], [], [], []
    for group in range(kv_local):
        mine = range(group * per_kv, (group + 1) * per_kv)
        q_group = jnp.concatenate([q_rot[h] for h in mine], axis=0)
        g_group = jnp.concatenate([grad_heads[h] for h in mine], axis=0)
        k_group = key_window[:, group * head : (group + 1) * head]
        v_group = value_window[:, group * head : (group + 1) * head]
        weights = jnp.where(allowed, jnp.exp(dot_nt(q_group, k_group) * factor), 0.0)
        shares = weights / jnp.sum(weights, axis=-1, keepdims=True)
        out = dot_nn(shares, v_group)
        d_shares = dot_nt(g_group, v_group)
        delta = jnp.sum(g_group * out, axis=-1, keepdims=True)
        d_scores = shares * (d_shares - delta) * factor
        d_krot.append(dot_tn(d_scores, q_group))
        d_values.append(dot_tn(shares, g_group))
        d_qrot = dot_nn(d_scores, k_group)
        for place, h in enumerate(mine):
            rows = slice(place * rows_dev, (place + 1) * rows_dev)
            attended.append(out[rows])
            d_queries.append(norm_rotate_back(d_qrot[rows], query_heads[h], query_gain, cosine, sine))

    def window_parts(blocks):
        return [
            joined([b[p * rows_dev : (p + 1) * rows_dev] for b in blocks]) for p in range(reach + 1)
        ]

    d_value = collect(window_parts(d_values))
    d_krot_own = collect(window_parts(d_krot))
    d_key = joined(
        [
            norm_rotate_back(d, u, key_gain, cosine, sine)
            for d, u in zip(heads_of(d_krot_own), heads_of(key_raw))
        ]
    )
    d_query = joined(d_queries)

    others = lax.all_gather(jnp.stack(pieces), "tensor", axis=1, tiled=True)
    lower = along < CHAIN // 2
    near = jnp.where(lower, others[2], others[0])
    far = jnp.where(lower, others[0], others[2])
    own_slab = lax.dynamic_slice_in_dim(hidden_in, along * slab, slab, 1)
    slabs = [own_slab, near, others[1], far]

    def part_of(block, step):
        return lax.dynamic_slice_in_dim(block, (across + step) % pair * part, part, 1)

    def weight_grad(own):
        up1, down1 = z_shift(own, 1), z_shift(own, -1)
        up2, down2 = z_shift(up1, 1), z_shift(down1, -1)
        up3, down3 = z_shift(up2, 1), z_shift(down2, -1)
        first = along == 0
        last = along == CHAIN - 1
        blocks = [
            own,
            jnp.where(lower, down1, up1),
            jnp.where(lower, down2, up2),
            jnp.where(first, down3, jnp.where(last, up3, jnp.where(lower, up1, down1))),
        ]
        arrived = None
        for step in range(pair - 1, -1, -1):
            term = None
            for slab_block, block in zip(slabs, blocks):
                product = dot_tn(part_of(slab_block, step), block)
                term = product if term is None else term + product
            if step:
                term = y_ring(term, step)
            arrived = term if arrived is None else arrived + term
        return arrived

    grad_query = weight_grad(d_query)
    grad_value = weight_grad(d_value)
    grad_key = weight_grad(d_key)
    input_term = dot_nt(d_query, query_proj) + dot_nt(d_value, value_proj) + dot_nt(d_key, key_proj)
    grad_input = lax.psum_scatter(input_term, "tensor", scatter_dimension=1, tiled=True)
    return (joined(attended), grad_input, grad_query, grad_key, grad_value)


def solution(mesh):
    return jax.shard_map(
        local,
        mesh=mesh,
        in_specs=(
            P("seq", None),
            P(None, "tensor"),
            P(None, "tensor"),
            P(None, "tensor"),
            P(),
            P(),
            P(),
            P("seq", "tensor"),
        ),
        out_specs=(
            P("seq", "tensor"),
            P("seq", "tensor"),
            P("seq", "tensor"),
            P("seq", "tensor"),
            P("seq", "tensor"),
        ),
        check_vma=False,
    )
```

```python
import jax
import jax.numpy as jnp
from jax import lax
from jax.sharding import PartitionSpec as P

WINDOW = 1024
CHAIN = 4

fine = lax.Precision.HIGH
epsilon = 1e-06


def dot_nn(left, right):
    return lax.dot_general(left, right, (((1,), (0,)), ((), ())), precision=fine)


def dot_nt(left, right):
    return lax.dot_general(left, right, (((1,), (1,)), ((), ())), precision=fine)


def dot_tn(left, right):
    return lax.dot_general(left, right, (((0,), (0,)), ((), ())), precision=fine)


def after(block, *earlier):
    return lax.optimization_barrier((block, earlier))[0]


def rope_tables(positions, head_width):
    middle = head_width // 2
    exponent = 2.0 * jnp.arange(middle).astype(jnp.float32) / head_width
    frequency = 10000.0 ** (-exponent)
    angles = positions.astype(jnp.float32)[:, None] * frequency[None, :]
    return jnp.cos(angles), jnp.sin(angles)


def inverse_rms(vector):
    return lax.rsqrt(jnp.mean(vector * vector, axis=-1, keepdims=True) + epsilon)


def norm_rotate(vector, scaling, cosine, sine):
    middle = vector.shape[-1] // 2
    normed = vector * inverse_rms(vector) * scaling
    low, high = normed[:, :middle], normed[:, middle:]
    return jnp.concatenate([low * cosine - high * sine, high * cosine + low * sine], axis=1)


def norm_rotate_back(grad, vector, scaling, cosine, sine):
    middle = vector.shape[-1] // 2
    low, high = grad[:, :middle], grad[:, middle:]
    d_normed = jnp.concatenate([low * cosine + high * sine, high * cosine - low * sine], axis=1)
    d_normed = d_normed * scaling
    inverse = inverse_rms(vector)
    unit = vector * inverse
    return inverse * (d_normed - unit * jnp.mean(d_normed * unit, axis=-1, keepdims=True))


def local(hidden_in, query_proj, key_proj, value_proj, query_gain, key_gain, segment_ids, grad_out):
    rows_dev, width = hidden_in.shape
    head = query_gain.shape[0]
    kv_local = key_proj.shape[1] // head
    q_local = query_proj.shape[1] // head
    per_kv = q_local // kv_local
    count = lax.axis_size("seq")
    pair = count // CHAIN
    members = lax.axis_size("tensor")
    member = lax.axis_index("tensor")
    seq_index = lax.axis_index("seq")
    along = seq_index // pair
    across = seq_index % pair
    reach = (WINDOW - 1) // rows_dev + 1
    span = (reach + 1) * rows_dev

    def z_shift(block, step):
        route = [(i, i + step * pair) for i in range(count) if 0 <= i + step * pair < count]
        return lax.ppermute(block, "seq", route)

    def z_ring(block, step):
        return lax.ppermute(block, "seq", [(i, (i + step * pair) % count) for i in range(count)])

    def y_ring(block, step):
        route = [(i, i // pair * pair + (i + step) % pair) for i in range(count)]
        return lax.ppermute(block, "seq", route)

    def shifted(block, distance):
        route = [(i - distance, i) for i in range(count) if 0 <= i - distance < count]
        return lax.ppermute(block, "seq", route)

    slab = width // CHAIN
    part = width // count
    piece = rows_dev // members

    first_row = seq_index * rows_dev
    positions = first_row + jnp.arange(rows_dev, dtype=jnp.int32)
    cosine, sine = rope_tables(positions, head)

    def heads_of(array):
        return [array[:, h * head : (h + 1) * head] for h in range(array.shape[1] // head)]

    def joined(blocks):
        return jnp.concatenate(blocks, axis=1)

    key_raw = dot_nn(hidden_in, key_proj)
    k_rot = joined([norm_rotate(u, key_gain, cosine, sine) for u in heads_of(key_raw)])
    values = dot_nn(after(hidden_in, k_rot), value_proj)

    def spread(own):
        if pair != 2 or reach != 4:
            return [shifted(own, distance) for distance in range(reach, 0, -1)] + [own]
        two = z_shift(own, 1)
        four = z_shift(two, 1)
        one = y_ring(jnp.where(across == 0, own, two), 1)
        three = y_ring(jnp.where(across == 0, two, four), 1)
        return [four, three, two, one, own]

    def collect(parts):
        if pair != 2 or reach != 4:
            total = parts[reach]
            for distance in range(1, reach + 1):
                total = total + shifted(parts[reach - distance], -distance)
            return total
        four, three, two, one, own = parts
        from_three = y_ring(three, 1)
        from_one = y_ring(one, 1)
        from_four = z_shift(four + jnp.where(across == 0, 0.0, from_three), -1)
        from_two = z_shift(two + jnp.where(across == 0, from_three, from_one) + from_four, -1)
        return own + jnp.where(across == 0, from_one, 0.0) + from_two

    key_blocks = spread(k_rot)
    value_blocks = spread(values)
    key_window = jnp.concatenate(key_blocks, axis=0)
    value_window = jnp.concatenate(value_blocks, axis=0)

    my_rows = lax.dynamic_slice_in_dim(hidden_in, member * piece, piece, 0)
    my_rows = after(my_rows, key_blocks[0], value_blocks[0])
    pieces = []
    for step in range(1, CHAIN):
        target = (along + step) % CHAIN
        pieces.append(z_ring(lax.dynamic_slice_in_dim(my_rows, target * slab, slab, 1), step))

    queries = dot_nn(after(hidden_in, values), query_proj)
    query_heads = heads_of(queries)
    grad_heads = heads_of(grad_out)
    q_rot = [norm_rotate(u, query_gain, cosine, sine) for u in query_heads]

    seg_pad = jnp.concatenate([jnp.full((reach * rows_dev,), -1, jnp.int32), segment_ids])
    key_seg = lax.dynamic_slice_in_dim(seg_pad, first_row, span, 0)
    query_seg = lax.dynamic_slice_in_dim(segment_ids, first_row, rows_dev, 0)
    key_pos = first_row - reach * rows_dev + jnp.arange(span, dtype=jnp.int32)
    distance = positions[:, None] - key_pos[None, :]
    allowed = (
        (key_pos[None, :] >= 0)
        & (distance >= 0)
        & (distance < WINDOW)
        & (query_seg[:, None] == key_seg[None, :])
    )
    allowed = jnp.concatenate([allowed] * per_kv, axis=0)
    factor = head ** (-0.5)

    attended, d_queries, d_krot, d_values = [], [], [], []
    for group in range(kv_local):
        mine = range(group * per_kv, (group + 1) * per_kv)
        q_group = jnp.concatenate([q_rot[h] for h in mine], axis=0)
        g_group = jnp.concatenate([grad_heads[h] for h in mine], axis=0)
        k_group = key_window[:, group * head : (group + 1) * head]
        v_group = value_window[:, group * head : (group + 1) * head]
        weights = jnp.where(allowed, jnp.exp(dot_nt(q_group, k_group) * factor), 0.0)
        shares = weights / jnp.sum(weights, axis=-1, keepdims=True)
        out = dot_nn(shares, v_group)
        d_shares = dot_nt(g_group, v_group)
        delta = jnp.sum(g_group * out, axis=-1, keepdims=True)
        d_scores = shares * (d_shares - delta) * factor
        d_krot.append(dot_tn(d_scores, q_group))
        d_values.append(dot_tn(shares, g_group))
        d_qrot = dot_nn(d_scores, k_group)
        for place, h in enumerate(mine):
            rows = slice(place * rows_dev, (place + 1) * rows_dev)
            attended.append(out[rows])
            d_queries.append(norm_rotate_back(d_qrot[rows], query_heads[h], query_gain, cosine, sine))

    def window_parts(blocks):
        return [
            joined([b[p * rows_dev : (p + 1) * rows_dev] for b in blocks]) for p in range(reach + 1)
        ]

    value_parts = window_parts(d_values)
    key_parts = window_parts(d_krot)
    d_query = after(joined(d_queries), pieces)

    class Chain:
        def __init__(self):
            self.sent = []

        def send(self, block, step):
            if len(self.sent) >= 2:
                block = after(block, self.sent[-2])
            got = z_shift(block, step)
            self.sent.append(got)
            return got

    up, down = Chain(), Chain()

    def upward(block):
        return up.send(block, 1)

    def downward(block):
        return down.send(block, -1)

    q_up1 = upward(d_query)
    q_down1 = downward(d_query)
    if pair == 2 and reach == 4:
        stage = []
        for four, three, two, one, own in (value_parts, key_parts):
            stage.append((four, two, own, y_ring(three, 1), y_ring(one, 1)))
        held = []
        for four, two, own, from_three, from_one in stage:
            got = downward(four + jnp.where(across == 0, 0.0, from_three))
            held.append((two + jnp.where(across == 0, from_three, from_one), own, from_one, got))
        q_up2 = upward(q_up1)
        totals = []
        for two, own, from_one, got in held:
            totals.append(own + jnp.where(across == 0, from_one, 0.0) + downward(two + got))
        q_up3 = upward(q_up2)
        d_value, d_krot_own = totals
    else:
        d_value, d_krot_own = collect(value_parts), collect(key_parts)
        q_up2 = upward(q_up1)
        q_up3 = upward(q_up2)
    q_down2 = downward(q_down1)
    d_key = joined(
        [
            norm_rotate_back(d, u, key_gain, cosine, sine)
            for d, u in zip(heads_of(d_krot_own), heads_of(key_raw))
        ]
    )
    v_up1, v_down1 = upward(d_value), downward(d_value)
    q_down3 = downward(q_down2)
    k_up1, k_down1 = upward(d_key), downward(d_key)
    v_up2, v_down2 = upward(v_up1), downward(v_down1)
    k_up2, k_down2 = upward(k_up1), downward(k_down1)
    v_up3, v_down3 = upward(v_up2), downward(v_down2)
    k_up3, k_down3 = upward(k_up2), downward(k_down2)

    others = lax.all_gather(jnp.stack(pieces), "tensor", axis=1, tiled=True)
    lower = along < CHAIN // 2
    near = jnp.where(lower, others[2], others[0])
    far = jnp.where(lower, others[0], others[2])
    own_slab = lax.dynamic_slice_in_dim(hidden_in, along * slab, slab, 1)
    slabs = [own_slab, near, others[1], far]

    def part_of(block, step):
        return lax.dynamic_slice_in_dim(block, (across + step) % pair * part, part, 1)

    def weight_grad(own, up1, up2, up3, down1, down2, down3):
        first = along == 0
        last = along == CHAIN - 1
        blocks = [
            own,
            jnp.where(lower, down1, up1),
            jnp.where(lower, down2, up2),
            jnp.where(first, down3, jnp.where(last, up3, jnp.where(lower, up1, down1))),
        ]
        arrived = None
        for step in range(pair - 1, -1, -1):
            term = None
            for slab_block, block in zip(slabs, blocks):
                product = dot_tn(part_of(slab_block, step), block)
                term = product if term is None else term + product
            if step:
                term = y_ring(term, step)
            arrived = term if arrived is None else arrived + term
        return arrived

    grad_query = weight_grad(d_query, q_up1, q_up2, q_up3, q_down1, q_down2, q_down3)
    grad_value = weight_grad(d_value, v_up1, v_up2, v_up3, v_down1, v_down2, v_down3)
    grad_key = weight_grad(d_key, k_up1, k_up2, k_up3, k_down1, k_down2, k_down3)
    input_term = dot_nt(d_query, query_proj) + dot_nt(d_value, value_proj) + dot_nt(d_key, key_proj)
    grad_input = lax.psum_scatter(input_term, "tensor", scatter_dimension=1, tiled=True)
    return (joined(attended), grad_input, grad_query, grad_key, grad_value)


def solution(mesh):
    return jax.shard_map(
        local,
        mesh=mesh,
        in_specs=(
            P("seq", None),
            P(None, "tensor"),
            P(None, "tensor"),
            P(None, "tensor"),
            P(),
            P(),
            P(),
            P("seq", "tensor"),
        ),
        out_specs=(
            P("seq", "tensor"),
            P("seq", "tensor"),
            P("seq", "tensor"),
            P("seq", "tensor"),
            P("seq", "tensor"),
        ),
        check_vma=False,
    )
```

```python
import jax
import jax.numpy as jnp
from jax import lax
from jax.sharding import Mesh, PartitionSpec as P

WINDOW = 1024
CHAIN = 4
CORES = 2

fine = lax.Precision.HIGH
epsilon = 1e-06


def dot_nn(left, right):
    return lax.dot_general(left, right, (((1,), (0,)), ((), ())), precision=fine)


def dot_nt(left, right):
    return lax.dot_general(left, right, (((1,), (1,)), ((), ())), precision=fine)


def dot_tn(left, right):
    return lax.dot_general(left, right, (((0,), (0,)), ((), ())), precision=fine)


def after(block, *earlier):
    return lax.optimization_barrier((block, earlier))[0]


def rope_tables(positions, head_width):
    middle = head_width // 2
    exponent = 2.0 * jnp.arange(middle).astype(jnp.float32) / head_width
    frequency = 10000.0 ** (-exponent)
    angles = positions.astype(jnp.float32)[:, None] * frequency[None, :]
    return jnp.cos(angles), jnp.sin(angles)


def inverse_rms(vector):
    return lax.rsqrt(jnp.mean(vector * vector, axis=-1, keepdims=True) + epsilon)


def norm_rotate(vector, scaling, cosine, sine):
    middle = vector.shape[-1] // 2
    normed = vector * inverse_rms(vector) * scaling
    low, high = normed[:, :middle], normed[:, middle:]
    return jnp.concatenate([low * cosine - high * sine, high * cosine + low * sine], axis=1)


def norm_rotate_back(grad, vector, scaling, cosine, sine):
    middle = vector.shape[-1] // 2
    low, high = grad[:, :middle], grad[:, middle:]
    d_normed = jnp.concatenate([low * cosine + high * sine, high * cosine - low * sine], axis=1)
    d_normed = d_normed * scaling
    inverse = inverse_rms(vector)
    unit = vector * inverse
    return inverse * (d_normed - unit * jnp.mean(d_normed * unit, axis=-1, keepdims=True))


def local(hidden_in, query_proj, key_proj, value_proj, query_gain, key_gain, segment_ids, grad_out):
    rows_dev, width = hidden_in.shape
    head = query_gain.shape[0]
    kv_local = key_proj.shape[1] // head
    q_local = query_proj.shape[1] // head
    per_kv = q_local // kv_local
    pair = lax.axis_size("y")
    count = CHAIN * pair
    members = lax.axis_size("tensor")
    member = lax.axis_index("tensor")
    along = lax.axis_index("z")
    across = lax.axis_index("y")
    seq_index = along * pair + across
    reach = (WINDOW - 1) // rows_dev + 1
    span = (reach + 1) * rows_dev

    def z_shift(block, step):
        route = [(i, i + step) for i in range(CHAIN) if 0 <= i + step < CHAIN]
        return lax.ppermute(block, "z", route)

    def y_ring(block, step):
        return lax.ppermute(block, "y", [(i, (i + step) % pair) for i in range(pair)])

    def shifted(block, distance):
        route = [(i - distance, i) for i in range(count) if 0 <= i - distance < count]
        return lax.ppermute(block, ("z", "y"), route)

    slab = width // CHAIN
    part = width // count
    piece = rows_dev // members

    first_row = seq_index * rows_dev
    positions = first_row + jnp.arange(rows_dev, dtype=jnp.int32)
    cosine, sine = rope_tables(positions, head)

    def heads_of(array):
        return [array[:, h * head : (h + 1) * head] for h in range(array.shape[1] // head)]

    def joined(blocks):
        return jnp.concatenate(blocks, axis=1)

    short = pair == 2 and reach == 4

    def spread_later(own, two):
        four = z_shift(two, 1)
        one = y_ring(jnp.where(across == 0, own, two), 1)
        three = y_ring(jnp.where(across == 0, two, four), 1)
        return [four, three, two, one, own]

    key_raw = dot_nn(hidden_in, key_proj)
    k_rot = joined([norm_rotate(u, key_gain, cosine, sine) for u in heads_of(key_raw)])
    values = dot_nn(after(hidden_in, k_rot), value_proj)
    if short:
        key_two = z_shift(k_rot, 1)
        value_two = z_shift(values, 1)
        key_blocks = spread_later(k_rot, key_two)
        queries = dot_nn(after(hidden_in, key_two, values), query_proj)
        value_blocks = spread_later(values, value_two)
    else:
        key_blocks = [shifted(k_rot, d) for d in range(reach, 0, -1)] + [k_rot]
        value_blocks = [shifted(values, d) for d in range(reach, 0, -1)] + [values]
        queries = dot_nn(hidden_in, query_proj)
    key_window = jnp.concatenate(key_blocks, axis=0)
    value_window = jnp.concatenate(value_blocks, axis=0)

    my_rows = lax.dynamic_slice_in_dim(hidden_in, member * piece, piece, 0)
    my_rows = after(my_rows, key_blocks[0], value_blocks[0])
    pieces = lax.all_to_all(my_rows, "z", 1, 0, tiled=True).reshape(CHAIN, piece, slab)
    hidden_slab = lax.all_gather(pieces, "tensor", axis=1, tiled=True)
    hidden_slab = hidden_slab.reshape(CHAIN * rows_dev, slab)

    query_heads = heads_of(queries)
    grad_heads = heads_of(grad_out)
    q_rot = [norm_rotate(u, query_gain, cosine, sine) for u in query_heads]
    seg_pad = jnp.concatenate([jnp.full((reach * rows_dev,), -1, jnp.int32), segment_ids])
    key_seg = lax.dynamic_slice_in_dim(seg_pad, first_row, span, 0)
    query_seg = lax.dynamic_slice_in_dim(segment_ids, first_row, rows_dev, 0)
    key_pos = first_row - reach * rows_dev + jnp.arange(span, dtype=jnp.int32)
    distance = positions[:, None] - key_pos[None, :]
    allowed = (
        (key_pos[None, :] >= 0)
        & (distance >= 0)
        & (distance < WINDOW)
        & (query_seg[:, None] == key_seg[None, :])
    )
    allowed = jnp.concatenate([allowed] * per_kv, axis=0)
    factor = head ** (-0.5)

    attended, d_queries, d_krot, d_values = [], [], [], []
    for group in range(kv_local):
        mine = range(group * per_kv, (group + 1) * per_kv)
        q_group = jnp.concatenate([q_rot[h] for h in mine], axis=0)
        g_group = jnp.concatenate([grad_heads[h] for h in mine], axis=0)
        k_group = key_window[:, group * head : (group + 1) * head]
        v_group = value_window[:, group * head : (group + 1) * head]
        weights = jnp.where(allowed, jnp.exp(dot_nt(q_group, k_group) * factor), 0.0)
        shares = weights / jnp.sum(weights, axis=-1, keepdims=True)
        out = dot_nn(shares, v_group)
        d_shares = dot_nt(g_group, v_group)
        delta = jnp.sum(g_group * out, axis=-1, keepdims=True)
        d_scores = shares * (d_shares - delta) * factor
        d_krot.append(dot_tn(d_scores, q_group))
        d_values.append(dot_tn(shares, g_group))
        d_qrot = dot_nn(d_scores, k_group)
        for place, h in enumerate(mine):
            rows = slice(place * rows_dev, (place + 1) * rows_dev)
            attended.append(out[rows])
            d_queries.append(norm_rotate_back(d_qrot[rows], query_heads[h], query_gain, cosine, sine))

    def window_parts(blocks):
        return [
            joined([b[p * rows_dev : (p + 1) * rows_dev] for b in blocks]) for p in range(reach + 1)
        ]

    d_query = after(joined(d_queries), hidden_slab)
    value_parts = after(window_parts(d_values), d_query)
    key_parts = after(window_parts(d_krot), d_query)

    def z_all(block):
        return lax.all_gather(block, "z", axis=0, tiled=True)

    def weight_grad(gathered):
        total = None
        for step in range(pair - 1, -1, -1):
            columns = lax.dynamic_slice_in_dim(hidden_slab, (across + step) % pair * part, part, 1)
            term = dot_tn(columns, gathered)
            if step:
                term = y_ring(term, step)
            total = term if total is None else total + term
        return total

    query_all = z_all(d_query)
    if short:
        stage, held, totals = [], [], []
        for four, three, two, one, own in (value_parts, key_parts):
            stage.append((four, two, own, y_ring(three, 1), y_ring(one, 1)))
        for four, two, own, from_three, from_one in stage:
            got = z_shift(four + jnp.where(across == 0, 0.0, from_three), -1)
            held.append((two + jnp.where(across == 0, from_three, from_one), own, from_one, got))
        for two, own, from_one, got in held:
            totals.append(own + jnp.where(across == 0, from_one, 0.0) + z_shift(two + got, -1))
    else:
        totals = []
        for parts in (value_parts, key_parts):
            total = parts[reach]
            for distance in range(1, reach + 1):
                total = total + shifted(parts[reach - distance], -distance)
            totals.append(total)
    d_value, d_krot_own = totals
    value_all = z_all(after(d_value, query_all))
    d_key = joined(
        [
            norm_rotate_back(d, u, key_gain, cosine, sine)
            for d, u in zip(heads_of(d_krot_own), heads_of(key_raw))
        ]
    )
    key_all = z_all(after(d_key, value_all))

    d_query = after(d_query, d_key, query_all)
    input_term = dot_nt(d_query, query_proj) + dot_nt(d_value, value_proj) + dot_nt(d_key, key_proj)
    chips = members // CORES
    chip, core = member // CORES, member % CORES
    strip = width // members

    def strip_of(index):
        return lax.dynamic_slice_in_dim(input_term, index * strip, strip, 1)

    def to_core(block):
        return lax.ppermute(block, "tensor", [(i, i ^ 1) for i in range(members)])

    def to_chip(block, step):
        route = [(i, (i + step * CORES) % members) for i in range(members)]
        return lax.ppermute(block, "tensor", route)

    turns = [(chip + step) % chips for step in range(chips)]
    theirs = to_core(jnp.stack([strip_of(c * CORES + 1 - core) for c in turns]))
    sums = [strip_of(c * CORES + core) + theirs[i] for i, c in enumerate(turns)]
    grad_input = sums[0]
    for step in range(1, chips):
        grad_input = grad_input + to_chip(sums[step], step)

    grad_query = weight_grad(query_all)
    grad_value = weight_grad(value_all)
    grad_key = weight_grad(key_all)
    return (joined(attended), grad_input, grad_query, grad_key, grad_value)


def solution(mesh):
    seq, members = mesh.devices.shape
    split = Mesh(mesh.devices.reshape(CHAIN, seq // CHAIN, members), ("z", "y", "tensor"))
    tokens = ("z", "y")
    return jax.shard_map(
        local,
        mesh=split,
        in_specs=(
            P(tokens, None),
            P(None, "tensor"),
            P(None, "tensor"),
            P(None, "tensor"),
            P(),
            P(),
            P(),
            P(tokens, "tensor"),
        ),
        out_specs=(
            P(tokens, "tensor"),
            P(tokens, "tensor"),
            P(tokens, "tensor"),
            P(tokens, "tensor"),
            P(tokens, "tensor"),
        ),
        check_vma=False,
    )
```

```python
import functools

import jax
import jax.numpy as jnp
from jax import lax
from jax.experimental import pallas as pl
from jax.experimental.pallas import tpu as pltpu
from jax.sharding import Mesh, PartitionSpec as P

WINDOW = 1024
CHAIN = 4
CORES = 2

fine = lax.Precision.HIGH
epsilon = 1e-06


def dot_nn(left, right):
    return lax.dot_general(left, right, (((1,), (0,)), ((), ())), precision=fine)


def dot_nt(left, right):
    return lax.dot_general(left, right, (((1,), (1,)), ((), ())), precision=fine)


def dot_tn(left, right):
    return lax.dot_general(left, right, (((0,), (0,)), ((), ())), precision=fine)


def after(block, *earlier):
    return lax.optimization_barrier((block, earlier))[0]


def rope_tables(positions, head_width):
    middle = head_width // 2
    exponent = 2.0 * jnp.arange(middle).astype(jnp.float32) / head_width
    frequency = 10000.0 ** (-exponent)
    angles = positions.astype(jnp.float32)[:, None] * frequency[None, :]
    return jnp.cos(angles), jnp.sin(angles)


def inverse_rms(vector):
    return lax.rsqrt(jnp.mean(vector * vector, axis=-1, keepdims=True) + epsilon)


def norm_rotate(vector, scaling, cosine, sine):
    middle = vector.shape[-1] // 2
    normed = vector * inverse_rms(vector) * scaling
    low, high = normed[:, :middle], normed[:, middle:]
    return jnp.concatenate([low * cosine - high * sine, high * cosine + low * sine], axis=1)


def norm_rotate_back(grad, vector, scaling, cosine, sine):
    middle = vector.shape[-1] // 2
    low, high = grad[:, :middle], grad[:, middle:]
    d_normed = jnp.concatenate([low * cosine + high * sine, high * cosine - low * sine], axis=1)
    d_normed = d_normed * scaling
    inverse = inverse_rms(vector)
    unit = vector * inverse
    return inverse * (d_normed - unit * jnp.mean(d_normed * unit, axis=-1, keepdims=True))


def halves(array):
    high = array.astype(jnp.bfloat16)
    return high, (array - high.astype(jnp.float32)).astype(jnp.bfloat16)


def three(left, right, left_dim, right_dim):
    def once(a, b):
        return lax.dot_general(
            a, b, (((left_dim,), (right_dim,)), ((), ())), preferred_element_type=jnp.float32
        )

    return once(left[0], right[0]) + (once(left[0], right[1]) + once(left[1], right[0]))


def attention_kernel(blocks, per_kv, *refs):
    query_ref, grad_ref, gain_ref, cos_ref, sin_ref, seg_ref, key_seg_ref = refs[:7]
    kv_refs = refs[7 : 7 + blocks]
    out_ref, d_query_ref = refs[7 + blocks : 9 + blocks]
    d_kv_refs = refs[9 + blocks : 9 + 2 * blocks]
    weight_ref, d_share_ref, share_high, share_low, score_high, score_low = refs[9 + 2 * blocks :]
    rows = query_ref.shape[0]
    head = gain_ref.shape[1]
    factor = head ** (-0.5)
    gain, cosine, sine = gain_ref[...], cos_ref[...], sin_ref[...]
    raw = [query_ref[:, h * head : (h + 1) * head] for h in range(per_kv)]
    q_rot = halves(
        jnp.concatenate([norm_rotate(u, gain, cosine, sine) for u in raw], axis=0)
    )
    grad = halves(
        jnp.concatenate([grad_ref[:, h * head : (h + 1) * head] for h in range(per_kv)], axis=0)
    )
    total = jnp.zeros((1, per_kv * rows), jnp.float32)
    mixed = jnp.zeros((1, per_kv * rows), jnp.float32)
    seg = jnp.concatenate([seg_ref[...]] * per_kv, axis=1)
    turned_keys, turned_values = [], []
    lane = lax.broadcasted_iota(jnp.int32, (rows, rows), 1)
    lane = jnp.concatenate([lane] * per_kv, axis=1)
    row = lax.broadcasted_iota(jnp.int32, (rows, per_kv * rows), 0)
    for j in range(blocks):
        place = slice(j * rows, (j + 1) * rows)
        key, value = kv_refs[j][:, :head], kv_refs[j][:, head:]
        turned_keys.append(key.T)
        turned_values.append(value.T)
        scores = three(halves(key), q_rot, 1, 1) * factor
        distance = (blocks - 1 - j) * rows + lane - row
        allowed = (distance >= 0) & (distance < WINDOW) & (key_seg_ref[place, :] == seg)
        weights = jnp.where(allowed, jnp.exp(scores), 0.0)
        d_shares = three(halves(value), grad, 1, 1)
        weight_ref[place, :] = weights
        d_share_ref[place, :] = d_shares
        total = total + jnp.sum(weights, axis=0, keepdims=True)
        mixed = mixed + jnp.sum(weights * d_shares, axis=0, keepdims=True)
    scale = 1.0 / total
    delta = mixed * scale
    for j in range(blocks):
        place = slice(j * rows, (j + 1) * rows)
        shares = weight_ref[place, :] * scale
        d_scores = shares * (d_share_ref[place, :] - delta) * factor
        share_pair = halves(shares)
        score_pair = halves(d_scores)
        share_high[place, :], share_low[place, :] = share_pair
        score_high[place, :], score_low[place, :] = score_pair
        d_kv_refs[j][:, :head] = three(score_pair, q_rot, 1, 0)
        d_kv_refs[j][:, head:] = three(share_pair, grad, 1, 0)
    turned_out = three(
        halves(jnp.concatenate(turned_values, axis=1)), (share_high[...], share_low[...]), 1, 0
    )
    turned_query = three(
        halves(jnp.concatenate(turned_keys, axis=1)), (score_high[...], score_low[...]), 1, 0
    )
    for h in range(per_kv):
        place = slice(h * rows, (h + 1) * rows)
        columns = slice(h * head, (h + 1) * head)
        out_ref[:, columns] = turned_out[:, place].T
        d_query_ref[:, columns] = norm_rotate_back(
            turned_query[:, place].T, raw[h], gain, cosine, sine
        )


def attention(queries, grads, gain, cosine, sine, query_seg, key_seg, window, per_kv):
    rows, width = queries.shape
    blocks = len(window)
    span = blocks * rows
    flat = jax.ShapeDtypeStruct((rows, width), jnp.float32)
    part = jax.ShapeDtypeStruct(window[0].shape, jnp.float32)
    wide = per_kv * rows
    results = pl.pallas_call(
        functools.partial(attention_kernel, blocks, per_kv),
        out_shape=[flat, flat] + [part] * blocks,
        scratch_shapes=[
            pltpu.VMEM((span, wide), jnp.float32),
            pltpu.VMEM((span, wide), jnp.float32),
            pltpu.VMEM((span, wide), jnp.bfloat16),
            pltpu.VMEM((span, wide), jnp.bfloat16),
            pltpu.VMEM((span, wide), jnp.bfloat16),
            pltpu.VMEM((span, wide), jnp.bfloat16),
        ],
        compiler_params=pltpu.CompilerParams(vmem_limit_bytes=40 * 1024 * 1024),
        cost_estimate=pl.CostEstimate(
            flops=36 * span * wide * gain.shape[1],
            bytes_accessed=4 * (4 * rows * width + 4 * span * gain.shape[1]),
            transcendentals=span * wide,
        ),
    )(queries, grads, gain, cosine, sine, query_seg, key_seg, *window)
    return results[0], results[1], results[2:]


def local(hidden_in, query_proj, key_proj, value_proj, query_gain, key_gain, segment_ids, grad_out):
    rows_dev, width = hidden_in.shape
    head = query_gain.shape[0]
    kv_local = key_proj.shape[1] // head
    per_kv = query_proj.shape[1] // key_proj.shape[1]
    pair = lax.axis_size("y")
    count = CHAIN * pair
    members = lax.axis_size("tensor")
    member = lax.axis_index("tensor")
    along = lax.axis_index("z")
    across = lax.axis_index("y")
    seq_index = along * pair + across
    reach = (WINDOW - 1) // rows_dev + 1
    span = (reach + 1) * rows_dev
    slab = width // CHAIN
    part = width // count
    piece = rows_dev // members
    groups = range(kv_local)
    short = pair == 2 and reach == 4

    def z_shift(block, step):
        route = [(i, i + step) for i in range(CHAIN) if 0 <= i + step < CHAIN]
        return lax.ppermute(block, "z", route)

    def z_ring(block, step):
        return lax.ppermute(block, "z", [(i, (i + step) % CHAIN) for i in range(CHAIN)])

    def y_ring(block, step):
        return lax.ppermute(block, "y", [(i, (i + step) % pair) for i in range(pair)])

    def shifted(block, distance):
        route = [(i - distance, i) for i in range(count) if 0 <= i - distance < count]
        return lax.ppermute(block, ("z", "y"), route)

    first_row = seq_index * rows_dev
    positions = first_row + jnp.arange(rows_dev, dtype=jnp.int32)
    cosine, sine = rope_tables(positions, head)
    seg_pad = jnp.concatenate([jnp.full((reach * rows_dev,), -1, jnp.int32), segment_ids])
    key_seg = lax.dynamic_slice_in_dim(seg_pad, first_row, span, 0)[:, None]
    query_seg = lax.dynamic_slice_in_dim(segment_ids, first_row, rows_dev, 0)[None, :]

    def kv_columns(array, group):
        return array[:, group * head : (group + 1) * head]

    def q_columns(array, group):
        return array[:, group * per_kv * head : (group + 1) * per_kv * head]

    key_raw, own, two, queries = [], [], [], []
    for group in groups:
        source = after(hidden_in, own[-1]) if own else hidden_in
        key_raw.append(dot_nn(source, kv_columns(key_proj, group)))
        values = dot_nn(source, kv_columns(value_proj, group))
        k_rot = norm_rotate(key_raw[group], key_gain, cosine, sine)
        own.append(jnp.concatenate([k_rot, values], axis=1))
        if short:
            two.append(z_shift(own[group], 1))
    for group in groups:
        earlier = [own[-1]] + queries[-1:] + (two[: group] if short else [])
        queries.append(dot_nn(after(hidden_in, *earlier), q_columns(query_proj, group)))

    windows = []
    for group in groups:
        if short:
            ahead = windows[-1][:4] if windows else []
            four = z_shift(after(two[group], *two[:group]), 1)
            near = jnp.where(across == 0, own[group], two[group])
            one = y_ring(after(near, *ahead[:1]), 1)
            far = jnp.where(across == 0, two[group], four)
            three_back = y_ring(after(far, *ahead[3:]), 1)
            windows.append([four, three_back, two[group], one, own[group]])
        else:
            windows.append([shifted(own[group], d) for d in range(reach, 0, -1)] + [own[group]])

    my_rows = lax.dynamic_slice_in_dim(hidden_in, member * piece, piece, 0)
    my_rows = after(my_rows, *[w[0] for w in windows])
    pieces = []
    for step in range(CHAIN - 1, 0, -1):
        target = (along + step) % CHAIN
        pieces.append(z_ring(lax.dynamic_slice_in_dim(my_rows, target * slab, slab, 1), step))
    chips = members // CORES
    chip, core = member // CORES, member % CORES

    def to_core(block):
        return lax.ppermute(block, "tensor", [(i, i ^ 1) for i in range(members)])

    def to_chip(block, step):
        route = [(i, (i + step * CORES) % members) for i in range(members)]
        return lax.ppermute(block, "tensor", route)

    def in_order(blocks, index, axis):
        size = blocks[0].shape[axis]
        both = jnp.concatenate(blocks + blocks[:-1], axis=axis)
        start = (len(blocks) - 1 - index) * size
        return lax.dynamic_slice_in_dim(both, start, len(blocks) * size, axis)

    mine = jnp.stack(pieces)
    chip_rows = in_order([to_core(mine), mine], core, 1)
    arrivals = [to_chip(chip_rows, step) for step in range(chips - 1, 0, -1)]
    others = in_order(arrivals + [chip_rows], chip, 1)
    own_slab = lax.dynamic_slice_in_dim(hidden_in, along * slab, slab, 1)
    slabs = [others[i] for i in range(CHAIN - 1)] + [own_slab]

    attended, d_query, parts = [], [], []
    for group in groups:
        out, d_q, d_kv = attention(
            after(queries[group], *attended),
            q_columns(grad_out, group),
            query_gain[None, :],
            cosine,
            sine,
            query_seg,
            key_seg,
            windows[group],
            per_kv,
        )
        attended.append(out)
        d_query.append(d_q)
        parts.append(d_kv)

    def z_all(block):
        return lax.all_gather(block, "z", axis=0, tiled=True)

    query_all = [z_all(d) for d in d_query]

    totals = []
    for group in groups:
        if short:
            four, three_back, two_back, one, mine = parts[group]
            from_three = y_ring(three_back, 1)
            from_one = y_ring(one, 1)
            got = z_shift(four + jnp.where(across == 0, 0.0, from_three), -1)
            middle = two_back + jnp.where(across == 0, from_three, from_one) + got
            total = mine + jnp.where(across == 0, from_one, 0.0) + z_shift(middle, -1)
        else:
            total = parts[group][reach]
            for distance in range(1, reach + 1):
                total = total + shifted(parts[group][reach - distance], -distance)
        totals.append(total)

    joined_query = jnp.concatenate(d_query, axis=1)
    input_term = dot_nt(joined_query, query_proj)
    d_kv = []
    for group in groups:
        d_key = norm_rotate_back(totals[group][:, :head], key_raw[group], key_gain, cosine, sine)
        d_kv.append(jnp.concatenate([d_key, totals[group][:, head:]], axis=1))

    ordered = in_order(slabs, along, 0)

    def columns_of(block, step):
        return lax.dynamic_slice_in_dim(block, (across + step) % pair * part, part, 1)

    def term_of(pairs, step):
        term = None
        for columns, block in pairs:
            product = dot_tn(columns_of(columns, step), block)
            term = product if term is None else term + product
        return term

    def weight_grad(pairs):
        sent = [term_of(pairs, step) for step in range(pair - 1, 0, -1)]
        return [y_ring(term, pair - 1 - i) for i, term in enumerate(sent)]

    query_sent = [weight_grad([(ordered, gathered)]) for gathered in query_all]

    rings = [[d] for d in d_kv]
    rings[0][0] = after(rings[0][0], query_all[0], input_term)
    for hop in range(1, CHAIN):
        for group in groups:
            block = rings[group][-1]
            if hop == CHAIN - 1 and group == 0:
                block = after(block, query_all[-1])
            if hop == CHAIN - 1 and group == kv_local - 1:
                block = after(block, query_sent[0])
            rings[group].append(z_ring(block, 1))

    grad_query, grad_kv = [], []
    for gathered, sent in zip(query_all, query_sent):
        total = term_of([(ordered, gathered)], 0)
        for term in sent:
            total = total + term
        grad_query.append(total)
    for group in groups:
        pairs = [(slabs[CHAIN - 1 - hop], rings[group][hop]) for hop in range(CHAIN)]
        sent = weight_grad(pairs)
        total = term_of(pairs, 0)
        for term in sent:
            total = total + term
        grad_kv.append(total)

    later = [after(d, rings[0][1]) for d in d_kv]
    d_keys = jnp.concatenate([d[:, :head] for d in later], axis=1)
    d_values = jnp.concatenate([d[:, head:] for d in later], axis=1)
    input_term = input_term + dot_nt(d_keys, key_proj) + dot_nt(d_values, value_proj)
    strip = width // members

    def strip_of(index):
        return lax.dynamic_slice_in_dim(input_term, index * strip, strip, 1)

    turns = [(chip + step) % chips for step in range(chips)]
    theirs = to_core(jnp.stack([strip_of(c * CORES + 1 - core) for c in turns]))
    sums = [strip_of(c * CORES + core) + theirs[i] for i, c in enumerate(turns)]
    grad_input = sums[0]
    for step in range(1, chips):
        grad_input = grad_input + to_chip(sums[step], step)

    return (
        jnp.concatenate(attended, axis=1),
        grad_input,
        jnp.concatenate(grad_query, axis=1),
        jnp.concatenate([g[:, :head] for g in grad_kv], axis=1),
        jnp.concatenate([g[:, head:] for g in grad_kv], axis=1),
    )


def solution(mesh):
    seq, members = mesh.devices.shape
    split = Mesh(mesh.devices.reshape(CHAIN, seq // CHAIN, members), ("z", "y", "tensor"))
    tokens = ("z", "y")
    return jax.shard_map(
        local,
        mesh=split,
        in_specs=(
            P(tokens, None),
            P(None, "tensor"),
            P(None, "tensor"),
            P(None, "tensor"),
            P(),
            P(),
            P(),
            P(tokens, "tensor"),
        ),
        out_specs=(
            P(tokens, "tensor"),
            P(tokens, "tensor"),
            P(tokens, "tensor"),
            P(tokens, "tensor"),
            P(tokens, "tensor"),
        ),
        check_vma=False,
    )
```

```python
import functools

import jax
import jax.numpy as jnp
from jax import lax
from jax.experimental import pallas as pl
from jax.experimental.pallas import tpu as pltpu
from jax.sharding import Mesh, PartitionSpec as P

WINDOW = 1024
CHAIN = 4
CORES = 2

MIB = 1024 * 1024
epsilon = 1e-06


def after(block, *earlier):
    return lax.optimization_barrier((block, earlier))[0]


def rope_tables(positions, head_width):
    middle = head_width // 2
    exponent = 2.0 * jnp.arange(middle).astype(jnp.float32) / head_width
    frequency = 10000.0 ** (-exponent)
    angles = positions.astype(jnp.float32)[:, None] * frequency[None, :]
    return jnp.cos(angles), jnp.sin(angles)


def inverse_rms(vector):
    return lax.rsqrt(jnp.mean(vector * vector, axis=-1, keepdims=True) + epsilon)


def norm_rotate(vector, scaling, cosine, sine):
    middle = vector.shape[-1] // 2
    normed = vector * inverse_rms(vector) * scaling
    low, high = normed[:, :middle], normed[:, middle:]
    return jnp.concatenate([low * cosine - high * sine, high * cosine + low * sine], axis=1)


def norm_rotate_back(grad, vector, scaling, cosine, sine):
    middle = vector.shape[-1] // 2
    low, high = grad[:, :middle], grad[:, middle:]
    d_normed = jnp.concatenate([low * cosine + high * sine, high * cosine - low * sine], axis=1)
    d_normed = d_normed * scaling
    inverse = inverse_rms(vector)
    unit = vector * inverse
    return inverse * (d_normed - unit * jnp.mean(d_normed * unit, axis=-1, keepdims=True))


def halves(array):
    high = array.astype(jnp.bfloat16)
    return high, (array - high.astype(jnp.float32)).astype(jnp.bfloat16)


def three(left, right, left_dim, right_dim):
    def once(a, b):
        return lax.dot_general(
            a, b, (((left_dim,), (right_dim,)), ((), ())), preferred_element_type=jnp.float32
        )

    return once(left[0], right[0]) + (once(left[0], right[1]) + once(left[1], right[0]))


def attention_kernel(blocks, per_kv, *refs):
    query_ref, grad_ref, gain_ref, cos_ref, sin_ref, seg_ref, key_seg_ref = refs[:7]
    kv_refs = refs[7 : 7 + blocks]
    out_ref, d_query_ref = refs[7 + blocks : 9 + blocks]
    d_kv_refs = refs[9 + blocks : 9 + 2 * blocks]
    weight_ref, d_share_ref, share_high, share_low, score_high, score_low = refs[9 + 2 * blocks :]
    rows = query_ref.shape[0]
    head = gain_ref.shape[1]
    factor = head ** (-0.5)
    gain, cosine, sine = gain_ref[...], cos_ref[...], sin_ref[...]
    raw = [query_ref[:, h * head : (h + 1) * head] for h in range(per_kv)]
    q_rot = halves(
        jnp.concatenate([norm_rotate(u, gain, cosine, sine) for u in raw], axis=0)
    )
    grad = halves(
        jnp.concatenate([grad_ref[:, h * head : (h + 1) * head] for h in range(per_kv)], axis=0)
    )
    total = jnp.zeros((1, per_kv * rows), jnp.float32)
    mixed = jnp.zeros((1, per_kv * rows), jnp.float32)
    seg = jnp.concatenate([seg_ref[...]] * per_kv, axis=1)
    turned_keys, turned_values = [], []
    lane = lax.broadcasted_iota(jnp.int32, (rows, rows), 1)
    lane = jnp.concatenate([lane] * per_kv, axis=1)
    row = lax.broadcasted_iota(jnp.int32, (rows, per_kv * rows), 0)
    for j in range(blocks):
        place = slice(j * rows, (j + 1) * rows)
        key, value = kv_refs[j][:, :head], kv_refs[j][:, head:]
        turned_keys.append(key.T)
        turned_values.append(value.T)
        scores = three(halves(key), q_rot, 1, 1) * factor
        distance = (blocks - 1 - j) * rows + lane - row
        allowed = (distance >= 0) & (distance < WINDOW) & (key_seg_ref[place, :] == seg)
        weights = jnp.where(allowed, jnp.exp(scores), 0.0)
        d_shares = three(halves(value), grad, 1, 1)
        weight_ref[place, :] = weights
        d_share_ref[place, :] = d_shares
        total = total + jnp.sum(weights, axis=0, keepdims=True)
        mixed = mixed + jnp.sum(weights * d_shares, axis=0, keepdims=True)
    scale = 1.0 / total
    delta = mixed * scale
    for j in range(blocks):
        place = slice(j * rows, (j + 1) * rows)
        shares = weight_ref[place, :] * scale
        d_scores = shares * (d_share_ref[place, :] - delta) * factor
        share_pair = halves(shares)
        score_pair = halves(d_scores)
        share_high[place, :], share_low[place, :] = share_pair
        score_high[place, :], score_low[place, :] = score_pair
        d_kv_refs[j][:, :head] = three(score_pair, q_rot, 1, 0)
        d_kv_refs[j][:, head:] = three(share_pair, grad, 1, 0)
    turned_out = three(
        halves(jnp.concatenate(turned_values, axis=1)), (share_high[...], share_low[...]), 1, 0
    )
    turned_query = three(
        halves(jnp.concatenate(turned_keys, axis=1)), (score_high[...], score_low[...]), 1, 0
    )
    for h in range(per_kv):
        place = slice(h * rows, (h + 1) * rows)
        columns = slice(h * head, (h + 1) * head)
        out_ref[:, columns] = turned_out[:, place].T
        d_query_ref[:, columns] = norm_rotate_back(
            turned_query[:, place].T, raw[h], gain, cosine, sine
        )


def attention(queries, grads, gain, cosine, sine, query_seg, key_seg, window, per_kv):
    rows, width = queries.shape
    blocks = len(window)
    span = blocks * rows
    flat = jax.ShapeDtypeStruct((rows, width), jnp.float32)
    part = jax.ShapeDtypeStruct(window[0].shape, jnp.float32)
    wide = per_kv * rows
    results = pl.pallas_call(
        functools.partial(attention_kernel, blocks, per_kv),
        out_shape=[flat, flat] + [part] * blocks,
        scratch_shapes=[
            pltpu.VMEM((span, wide), jnp.float32),
            pltpu.VMEM((span, wide), jnp.float32),
            pltpu.VMEM((span, wide), jnp.bfloat16),
            pltpu.VMEM((span, wide), jnp.bfloat16),
            pltpu.VMEM((span, wide), jnp.bfloat16),
            pltpu.VMEM((span, wide), jnp.bfloat16),
        ],
        compiler_params=pltpu.CompilerParams(vmem_limit_bytes=40 * 1024 * 1024),
        cost_estimate=pl.CostEstimate(
            flops=36 * span * wide * gain.shape[1],
            bytes_accessed=4 * (4 * rows * width + 4 * span * gain.shape[1]),
            transcendentals=span * wide,
        ),
    )(queries, grads, gain, cosine, sine, query_seg, key_seg, *window)
    return results[0], results[1], results[2:]


def project_kernel(normed, source_ref, *refs):
    if normed:
        key_ref, value_ref, gain_ref, cos_ref, sin_ref, raw_ref, packed_ref, total_ref = refs
        weight_refs = (key_ref, value_ref)
    else:
        weight_ref, raw_ref, total_ref = refs
        weight_refs = (weight_ref,)
    step = pl.program_id(0)
    source = halves(source_ref[...])
    start = 0
    for ref in weight_refs:
        columns = slice(start, start + ref.shape[1])
        start += ref.shape[1]
        product = three(source, halves(ref[...]), 1, 0)

        @pl.when(step == 0)
        def _():
            total_ref[:, columns] = product

        @pl.when(step > 0)
        def _():
            total_ref[:, columns] += product

    @pl.when(step == pl.num_programs(0) - 1)
    def _():
        if normed:
            head = gain_ref.shape[1]
            raw = total_ref[:, :head]
            raw_ref[...] = raw
            packed_ref[:, :head] = norm_rotate(raw, gain_ref[...], cos_ref[...], sin_ref[...])
            packed_ref[:, head:] = total_ref[:, head:]
        else:
            raw_ref[...] = total_ref[...]


def project(source, weights, group, columns, extra):
    rows, width = source.shape
    tile = width // 5
    normed = len(weights) > 1
    wide = columns * len(weights)
    whole = [pl.BlockSpec(e.shape, lambda k: (0, 0)) for e in extra]
    outs = [jax.ShapeDtypeStruct((rows, columns), jnp.float32)]
    if normed:
        outs.append(jax.ShapeDtypeStruct((rows, wide), jnp.float32))
    return pl.pallas_call(
        functools.partial(project_kernel, normed),
        grid=(5,),
        out_shape=outs,
        in_specs=[pl.BlockSpec((rows, tile), lambda k: (0, k))]
        + [pl.BlockSpec((tile, columns), lambda k: (k, group))] * len(weights)
        + whole,
        out_specs=[pl.BlockSpec(o.shape, lambda k: (0, 0)) for o in outs],
        scratch_shapes=[pltpu.VMEM((rows, wide), jnp.float32)],
        compiler_params=pltpu.CompilerParams(vmem_limit_bytes=24 * MIB),
        cost_estimate=pl.CostEstimate(
            flops=6 * rows * width * wide,
            bytes_accessed=4 * width * (rows + wide),
            transcendentals=0,
        ),
    )(source, *weights, *extra)


def settle_kernel(mine_ref, one_ref, far_ref, keep_ref, raw_ref, gain_ref, cos_ref, sin_ref, out_ref):
    head = gain_ref.shape[1]
    total = mine_ref[...] + one_ref[...] * keep_ref[...] + far_ref[...]
    out_ref[:, :head] = norm_rotate_back(
        total[:, :head], raw_ref[...], gain_ref[...], cos_ref[...], sin_ref[...]
    )
    out_ref[:, head:] = total[:, head:]


def settle(mine, one, far, keep, raw, gain, cosine, sine):
    return pl.pallas_call(
        settle_kernel,
        out_shape=jax.ShapeDtypeStruct(mine.shape, jnp.float32),
        compiler_params=pltpu.CompilerParams(vmem_limit_bytes=16 * MIB),
        cost_estimate=pl.CostEstimate(
            flops=12 * mine.size, bytes_accessed=18 * mine.size, transcendentals=0
        ),
    )(mine, one, far, keep, raw, gain, cosine, sine)


def turn_kernel(place_ref, others_ref, own_ref, high_ref, low_ref):
    step = pl.program_id(0)

    @pl.when(step < CHAIN - 1)
    def _():
        high_ref[0], low_ref[0] = halves(others_ref[0])

    @pl.when(step == CHAIN - 1)
    def _():
        high_ref[0], low_ref[0] = halves(own_ref[...])


def turn(place, others, own):
    slab, rows = own.shape
    half = jax.ShapeDtypeStruct((CHAIN, slab, rows), jnp.bfloat16)
    out_spec = pl.BlockSpec((1, slab, rows), lambda i, p: ((p[0] + 1 + i) % CHAIN, 0, 0))
    return pl.pallas_call(
        turn_kernel,
        grid_spec=pltpu.PrefetchScalarGridSpec(
            num_scalar_prefetch=1,
            grid=(CHAIN,),
            in_specs=[
                pl.BlockSpec((1, slab, rows), lambda i, p: (jnp.minimum(i, CHAIN - 2), 0, 0)),
                pl.BlockSpec((slab, rows), lambda i, p: (0, 0)),
            ],
            out_specs=[out_spec, out_spec],
        ),
        out_shape=[half, half],
        compiler_params=pltpu.CompilerParams(vmem_limit_bytes=24 * MIB),
        cost_estimate=pl.CostEstimate(
            flops=8 * CHAIN * rows * slab,
            bytes_accessed=8 * CHAIN * rows * slab,
            transcendentals=0,
        ),
    )(place, others, own)


def product_kernel(ringed, place_ref, high_ref, low_ref, *refs):
    blocks, out_ref = refs[:-1], refs[-1]
    rows = high_ref.shape[2]
    total = None
    for i in range(CHAIN):
        if ringed:
            slot = lax.rem(place_ref[0] + (CHAIN - i), CHAIN)
            block = blocks[i][...]
        else:
            slot = i
            block = blocks[0][i * rows : (i + 1) * rows, :]
        term = three((high_ref[slot], low_ref[slot]), halves(block), 1, 0)
        total = term if total is None else total + term
    out_ref[...] = total


def product(place, step, turned, blocks, pair):
    high, low = turned
    part = high.shape[1] // pair
    rows = high.shape[2]
    columns = blocks[0].shape[1]
    spec = pl.BlockSpec((CHAIN, part, rows), lambda i, p: (0, (p[1] + step) % pair, 0))
    return pl.pallas_call(
        functools.partial(product_kernel, len(blocks) > 1),
        grid_spec=pltpu.PrefetchScalarGridSpec(
            num_scalar_prefetch=1,
            grid=(1,),
            in_specs=[spec, spec] + [pl.BlockSpec(b.shape, lambda i, p: (0, 0)) for b in blocks],
            out_specs=pl.BlockSpec((part, columns), lambda i, p: (0, 0)),
        ),
        out_shape=jax.ShapeDtypeStruct((part, columns), jnp.float32),
        compiler_params=pltpu.CompilerParams(vmem_limit_bytes=28 * MIB),
        cost_estimate=pl.CostEstimate(
            flops=6 * CHAIN * rows * part * columns,
            bytes_accessed=4 * CHAIN * rows * (part + columns) + 4 * part * columns,
            transcendentals=0,
        ),
    )(place, high, low, *blocks)


def strip_kernel(groups, per_kv, strips_ref, query_ref, key_ref, value_ref, *refs):
    d_query_refs, d_kv_refs = refs[:groups], refs[groups : 2 * groups]
    out_ref = refs[2 * groups]
    head = d_kv_refs[0].shape[1] // 2
    total = None
    for group in range(groups):
        columns = slice(group * head, (group + 1) * head)
        wide = slice(group * per_kv * head, (group + 1) * per_kv * head)
        for left, right in (
            (d_query_refs[group][...], query_ref[:, wide]),
            (d_kv_refs[group][:, :head], key_ref[:, columns]),
            (d_kv_refs[group][:, head:], value_ref[:, columns]),
        ):
            term = three(halves(right), halves(left), 1, 1)
            total = term if total is None else total + term
    out_ref[0] = total


def input_strips(strips, strip, d_query, d_kv, weights):
    count = strips.shape[0]
    rows = d_query[0].shape[0]
    groups = len(d_query)
    per_kv = 2 * d_query[0].shape[1] // d_kv[0].shape[1]
    wide = sum(w.shape[1] for w in weights)
    whole = [pl.BlockSpec(d.shape, lambda i, p: (0, 0)) for d in d_query + d_kv]
    return pl.pallas_call(
        functools.partial(strip_kernel, groups, per_kv),
        grid_spec=pltpu.PrefetchScalarGridSpec(
            num_scalar_prefetch=1,
            grid=(count,),
            in_specs=[pl.BlockSpec((strip, w.shape[1]), lambda i, p: (p[i], 0)) for w in weights]
            + whole,
            out_specs=pl.BlockSpec((1, strip, rows), lambda i, p: (i, 0, 0)),
        ),
        out_shape=jax.ShapeDtypeStruct((count, strip, rows), jnp.float32),
        compiler_params=pltpu.CompilerParams(vmem_limit_bytes=48 * MIB),
        cost_estimate=pl.CostEstimate(
            flops=6 * count * rows * strip * wide,
            bytes_accessed=4 * count * strip * (wide + rows),
            transcendentals=0,
        ),
    )(strips, *weights, *d_query, *d_kv)


def local(hidden_in, query_proj, key_proj, value_proj, query_gain, key_gain, segment_ids, grad_out):
    rows_dev, width = hidden_in.shape
    head = query_gain.shape[0]
    kv_local = key_proj.shape[1] // head
    per_kv = query_proj.shape[1] // key_proj.shape[1]
    pair = lax.axis_size("y")
    count = CHAIN * pair
    members = lax.axis_size("tensor")
    member = lax.axis_index("tensor")
    along = lax.axis_index("z")
    across = lax.axis_index("y")
    seq_index = along * pair + across
    reach = (WINDOW - 1) // rows_dev + 1
    span = (reach + 1) * rows_dev
    slab = width // CHAIN
    part = width // count
    piece = slab // members
    groups = range(kv_local)
    short = pair == 2 and reach == 4

    def z_shift(block, step):
        route = [(i, i + step) for i in range(CHAIN) if 0 <= i + step < CHAIN]
        return lax.ppermute(block, "z", route)

    def z_ring(block, step):
        return lax.ppermute(block, "z", [(i, (i + step) % CHAIN) for i in range(CHAIN)])

    def y_ring(block, step):
        return lax.ppermute(block, "y", [(i, (i + step) % pair) for i in range(pair)])

    def shifted(block, distance):
        route = [(i - distance, i) for i in range(count) if 0 <= i - distance < count]
        return lax.ppermute(block, ("z", "y"), route)

    first_row = seq_index * rows_dev
    positions = first_row + jnp.arange(rows_dev, dtype=jnp.int32)
    cosine, sine = rope_tables(positions, head)
    seg_pad = jnp.concatenate([jnp.full((reach * rows_dev,), -1, jnp.int32), segment_ids])
    key_seg = lax.dynamic_slice_in_dim(seg_pad, first_row, span, 0)[:, None]
    query_seg = lax.dynamic_slice_in_dim(segment_ids, first_row, rows_dev, 0)[None, :]

    def q_columns(array, group):
        return array[:, group * per_kv * head : (group + 1) * per_kv * head]

    key_raw, own, two, queries = [], [], [], []
    tables = (key_gain[None, :], cosine, sine)
    for group in groups:
        source = after(hidden_in, own[-1]) if own else hidden_in
        raw, packed = project(source, (key_proj, value_proj), group, head, tables)
        key_raw.append(raw)
        own.append(packed)
        if short:
            two.append(z_shift(own[group], 1))
    for group in groups:
        earlier = [own[-1]] + queries[-1:]
        source = after(hidden_in, *earlier)
        queries.append(project(source, (query_proj,), group, per_kv * head, ())[0])

    windows = []
    for group in groups:
        if short:
            ahead = windows[-1][:4] if windows else []
            four = z_shift(after(two[group], *two[:group], own[-1]), 1)
            near = jnp.where(across == 0, own[group], two[group])
            one = y_ring(after(near, *ahead[:1]), 1)
            far = jnp.where(across == 0, two[group], four)
            three_back = y_ring(after(far, *queries, *ahead[3:]), 1)
            windows.append([four, three_back, two[group], one, own[group]])
        else:
            windows.append([shifted(own[group], d) for d in range(reach, 0, -1)] + [own[group]])

    hidden_rows = after(hidden_in, *queries).T
    ready = after(hidden_rows, *[w[0] for w in windows])
    pieces = []
    for step in range(CHAIN - 1, 0, -1):
        target = (along + step) % CHAIN
        start = target * slab + member * piece
        pieces.append(z_ring(lax.dynamic_slice_in_dim(ready, start, piece, 0), step))
    chips = members // CORES
    chip, core = member // CORES, member % CORES

    def to_core(block):
        return lax.ppermute(block, "tensor", [(i, i ^ 1) for i in range(members)])

    def to_chip(block, step):
        route = [(i, (i + step * CORES) % members) for i in range(members)]
        return lax.ppermute(block, "tensor", route)

    def in_order(blocks, index, axis):
        size = blocks[0].shape[axis]
        both = jnp.concatenate(blocks + blocks[:-1], axis=axis)
        start = (len(blocks) - 1 - index) * size
        return lax.dynamic_slice_in_dim(both, start, len(blocks) * size, axis)

    mine = jnp.stack(pieces)
    chip_rows = in_order([to_core(mine), mine], core, 1)
    arrivals = [to_chip(chip_rows, step) for step in range(chips - 1, 0, -1)]
    others = in_order(arrivals + [chip_rows], chip, 1)
    own_slab = lax.dynamic_slice_in_dim(hidden_rows, along * slab, slab, 0)
    place = jnp.stack([along, across]).astype(jnp.int32)
    turned = turn(place, others, own_slab)

    attended, d_query, parts = [], [], []
    for group in groups:
        out, d_q, d_kv = attention(
            after(queries[group], *attended, *queries),
            q_columns(grad_out, group),
            query_gain[None, :],
            cosine,
            sine,
            query_seg,
            key_seg,
            windows[group],
            per_kv,
        )
        attended.append(out)
        d_query.append(d_q)
        parts.append(d_kv)

    def z_all(block):
        return lax.all_gather(block, "z", axis=0, tiled=True)

    query_all = [z_all(d) for d in d_query]

    d_kv = []
    keep = jnp.where(across == 0, 1.0, 0.0).reshape(1, 1).astype(jnp.float32)
    for group in groups:
        if short:
            four, three_back, two_back, one, mine = parts[group]
            from_three = y_ring(three_back, 1)
            from_one = y_ring(one, 1)
            got = z_shift(four + jnp.where(across == 0, 0.0, from_three), -1)
            far = z_shift(two_back + jnp.where(across == 0, from_three, from_one) + got, -1)
        else:
            mine = parts[group][reach]
            far = jnp.zeros_like(mine)
            for distance in range(1, reach + 1):
                far = far + shifted(parts[group][reach - distance], -distance)
            from_one = jnp.zeros_like(mine)
        d_kv.append(settle(mine, from_one, far, keep, key_raw[group], *tables))

    def terms(blocks):
        return [product(place, step, turned, blocks, pair) for step in range(pair - 1, 0, -1)]

    def exchange(sent):
        return [y_ring(term, pair - 1 - i) for i, term in enumerate(sent)]

    def finish(blocks, arrived):
        total = product(place, 0, turned, blocks, pair)
        for term in arrived:
            total = total + term
        return total

    query_terms = [terms([gathered]) for gathered in query_all]
    query_sent = [exchange(t) for t in query_terms]

    rings = [[d] for d in d_kv]
    for hop in range(1, CHAIN):
        for group in groups:
            block = rings[group][-1]
            if hop == 2 and group == 0:
                block = after(block, query_terms[0])
            if hop == CHAIN - 1 and group == kv_local - 1:
                block = after(block, query_terms[-1])
            rings[group].append(z_ring(block, 1))

    strip = width // members
    turns = [(chip + step) % chips for step in range(chips)]
    weights = (query_proj, key_proj, value_proj)
    theirs_at = jnp.stack([c * CORES + 1 - core for c in turns]).astype(jnp.int32)
    mine_at = jnp.stack([c * CORES + core for c in turns]).astype(jnp.int32)
    kv_later = [after(d, rings[0][1]) for d in d_kv]
    theirs = input_strips(theirs_at, strip, d_query, kv_later, weights)
    from_core = to_core(theirs)
    kv_later = [after(d, theirs) for d in d_kv]
    sums = input_strips(mine_at, strip, d_query, kv_later, weights) + from_core
    grad_input = sums[0]
    for step in range(1, chips):
        grad_input = grad_input + to_chip(sums[step], step)

    grad_query = [finish([g], sent) for g, sent in zip(query_all, query_sent)]
    kv_terms = []
    for group in groups:
        kv_terms.append(terms(rings[group]))
    grad_kv = [finish(rings[group], exchange(kv_terms[group])) for group in groups]

    return (
        jnp.concatenate(attended, axis=1),
        grad_input.T,
        jnp.concatenate(grad_query, axis=1),
        jnp.concatenate([g[:, :head] for g in grad_kv], axis=1),
        jnp.concatenate([g[:, head:] for g in grad_kv], axis=1),
    )


def solution(mesh):
    seq, members = mesh.devices.shape
    split = Mesh(mesh.devices.reshape(CHAIN, seq // CHAIN, members), ("z", "y", "tensor"))
    tokens = ("z", "y")
    return jax.shard_map(
        local,
        mesh=split,
        in_specs=(
            P(tokens, None),
            P(None, "tensor"),
            P(None, "tensor"),
            P(None, "tensor"),
            P(),
            P(),
            P(),
            P(tokens, "tensor"),
        ),
        out_specs=(
            P(tokens, "tensor"),
            P(tokens, "tensor"),
            P(tokens, "tensor"),
            P(tokens, "tensor"),
            P(tokens, "tensor"),
        ),
        check_vma=False,
    )
```

```python
import functools

import jax
import jax.numpy as jnp
from jax import lax
from jax.experimental import pallas as pl
from jax.experimental.pallas import tpu as pltpu
from jax.sharding import Mesh, PartitionSpec as P

WINDOW = 1024
CHAIN = 4
CORES = 2

MIB = 1024 * 1024
SOON = pl.CostEstimate(flops=1024, bytes_accessed=1024, transcendentals=0)
epsilon = 1e-06


def after(block, *earlier):
    return lax.optimization_barrier((block, earlier))[0]


def rope_tables(positions, head_width):
    middle = head_width // 2
    exponent = 2.0 * jnp.arange(middle).astype(jnp.float32) / head_width
    frequency = 10000.0 ** (-exponent)
    angles = positions.astype(jnp.float32)[:, None] * frequency[None, :]
    return jnp.cos(angles), jnp.sin(angles)


def inverse_rms(vector):
    return lax.rsqrt(jnp.mean(vector * vector, axis=-1, keepdims=True) + epsilon)


def norm_rotate(vector, scaling, cosine, sine):
    middle = vector.shape[-1] // 2
    normed = vector * inverse_rms(vector) * scaling
    low, high = normed[:, :middle], normed[:, middle:]
    return jnp.concatenate([low * cosine - high * sine, high * cosine + low * sine], axis=1)


def norm_rotate_back(grad, vector, scaling, cosine, sine):
    middle = vector.shape[-1] // 2
    low, high = grad[:, :middle], grad[:, middle:]
    d_normed = jnp.concatenate([low * cosine + high * sine, high * cosine - low * sine], axis=1)
    d_normed = d_normed * scaling
    inverse = inverse_rms(vector)
    unit = vector * inverse
    return inverse * (d_normed - unit * jnp.mean(d_normed * unit, axis=-1, keepdims=True))


def halves(array):
    high = array.astype(jnp.bfloat16)
    return high, (array - high.astype(jnp.float32)).astype(jnp.bfloat16)


def three(left, right, left_dim, right_dim):
    def once(a, b):
        return lax.dot_general(
            a, b, (((left_dim,), (right_dim,)), ((), ())), preferred_element_type=jnp.float32
        )

    return once(left[0], right[0]) + (once(left[0], right[1]) + once(left[1], right[0]))


def attention_kernel(blocks, per_kv, *refs):
    query_ref, grad_ref, gain_ref, cos_ref, sin_ref, seg_ref, key_seg_ref = refs[:7]
    kv_refs = refs[7 : 7 + blocks]
    out_ref, d_query_ref = refs[7 + blocks : 9 + blocks]
    d_kv_refs = refs[9 + blocks : 9 + 2 * blocks]
    weight_ref, d_share_ref, share_high, share_low, score_high, score_low = refs[9 + 2 * blocks :]
    rows = query_ref.shape[0]
    head = gain_ref.shape[1]
    factor = head ** (-0.5)
    gain, cosine, sine = gain_ref[...], cos_ref[...], sin_ref[...]
    raw = [query_ref[:, h * head : (h + 1) * head] for h in range(per_kv)]
    q_rot = halves(
        jnp.concatenate([norm_rotate(u, gain, cosine, sine) for u in raw], axis=0)
    )
    grad = halves(
        jnp.concatenate([grad_ref[:, h * head : (h + 1) * head] for h in range(per_kv)], axis=0)
    )
    total = jnp.zeros((1, per_kv * rows), jnp.float32)
    mixed = jnp.zeros((1, per_kv * rows), jnp.float32)
    seg = jnp.concatenate([seg_ref[...]] * per_kv, axis=1)
    turned_keys, turned_values = [], []
    lane = lax.broadcasted_iota(jnp.int32, (rows, rows), 1)
    lane = jnp.concatenate([lane] * per_kv, axis=1)
    row = lax.broadcasted_iota(jnp.int32, (rows, per_kv * rows), 0)
    for j in range(blocks):
        place = slice(j * rows, (j + 1) * rows)
        key, value = kv_refs[j][:, :head], kv_refs[j][:, head:]
        turned_keys.append(key.T)
        turned_values.append(value.T)
        scores = three(halves(key), q_rot, 1, 1) * factor
        distance = (blocks - 1 - j) * rows + lane - row
        allowed = (distance >= 0) & (distance < WINDOW) & (key_seg_ref[place, :] == seg)
        weights = jnp.where(allowed, jnp.exp(scores), 0.0)
        d_shares = three(halves(value), grad, 1, 1)
        weight_ref[place, :] = weights
        d_share_ref[place, :] = d_shares
        total = total + jnp.sum(weights, axis=0, keepdims=True)
        mixed = mixed + jnp.sum(weights * d_shares, axis=0, keepdims=True)
    scale = 1.0 / total
    delta = mixed * scale
    for j in range(blocks):
        place = slice(j * rows, (j + 1) * rows)
        shares = weight_ref[place, :] * scale
        d_scores = shares * (d_share_ref[place, :] - delta) * factor
        share_pair = halves(shares)
        score_pair = halves(d_scores)
        share_high[place, :], share_low[place, :] = share_pair
        score_high[place, :], score_low[place, :] = score_pair
        d_kv_refs[j][:, :head] = three(score_pair, q_rot, 1, 0)
        d_kv_refs[j][:, head:] = three(share_pair, grad, 1, 0)
    turned_out = three(
        halves(jnp.concatenate(turned_values, axis=1)), (share_high[...], share_low[...]), 1, 0
    )
    turned_query = three(
        halves(jnp.concatenate(turned_keys, axis=1)), (score_high[...], score_low[...]), 1, 0
    )
    for h in range(per_kv):
        place = slice(h * rows, (h + 1) * rows)
        columns = slice(h * head, (h + 1) * head)
        out_ref[:, columns] = turned_out[:, place].T
        d_query_ref[:, columns] = norm_rotate_back(
            turned_query[:, place].T, raw[h], gain, cosine, sine
        )


def attention(queries, grads, gain, cosine, sine, query_seg, key_seg, window, per_kv):
    rows, width = queries.shape
    blocks = len(window)
    span = blocks * rows
    flat = jax.ShapeDtypeStruct((rows, width), jnp.float32)
    part = jax.ShapeDtypeStruct(window[0].shape, jnp.float32)
    wide = per_kv * rows
    results = pl.pallas_call(
        functools.partial(attention_kernel, blocks, per_kv),
        out_shape=[flat, flat] + [part] * blocks,
        scratch_shapes=[
            pltpu.VMEM((span, wide), jnp.float32),
            pltpu.VMEM((span, wide), jnp.float32),
            pltpu.VMEM((span, wide), jnp.bfloat16),
            pltpu.VMEM((span, wide), jnp.bfloat16),
            pltpu.VMEM((span, wide), jnp.bfloat16),
            pltpu.VMEM((span, wide), jnp.bfloat16),
        ],
        compiler_params=pltpu.CompilerParams(vmem_limit_bytes=40 * 1024 * 1024),
        cost_estimate=SOON,
    )(queries, grads, gain, cosine, sine, query_seg, key_seg, *window)
    return results[0], results[1], results[2:]


def project_kernel(normed, source_ref, *refs):
    if normed:
        key_ref, value_ref, gain_ref, cos_ref, sin_ref, raw_ref, packed_ref, total_ref = refs
        weight_refs = (key_ref, value_ref)
    else:
        weight_ref, raw_ref, total_ref = refs
        weight_refs = (weight_ref,)
    step = pl.program_id(0)
    source = halves(source_ref[...])
    start = 0
    for ref in weight_refs:
        columns = slice(start, start + ref.shape[1])
        start += ref.shape[1]
        product = three(source, halves(ref[...]), 1, 0)

        @pl.when(step == 0)
        def _():
            total_ref[:, columns] = product

        @pl.when(step > 0)
        def _():
            total_ref[:, columns] += product

    @pl.when(step == pl.num_programs(0) - 1)
    def _():
        if normed:
            head = gain_ref.shape[1]
            raw = total_ref[:, :head]
            raw_ref[...] = raw
            packed_ref[:, :head] = norm_rotate(raw, gain_ref[...], cos_ref[...], sin_ref[...])
            packed_ref[:, head:] = total_ref[:, head:]
        else:
            raw_ref[...] = total_ref[...]


def project(source, weights, group, columns, extra):
    rows, width = source.shape
    tile = width // 5
    normed = len(weights) > 1
    wide = columns * len(weights)
    whole = [pl.BlockSpec(e.shape, lambda k: (0, 0)) for e in extra]
    outs = [jax.ShapeDtypeStruct((rows, columns), jnp.float32)]
    if normed:
        outs.append(jax.ShapeDtypeStruct((rows, wide), jnp.float32))
    return pl.pallas_call(
        functools.partial(project_kernel, normed),
        grid=(5,),
        out_shape=outs,
        in_specs=[pl.BlockSpec((rows, tile), lambda k: (0, k))]
        + [pl.BlockSpec((tile, columns), lambda k: (k, group))] * len(weights)
        + whole,
        out_specs=[pl.BlockSpec(o.shape, lambda k: (0, 0)) for o in outs],
        scratch_shapes=[pltpu.VMEM((rows, wide), jnp.float32)],
        compiler_params=pltpu.CompilerParams(vmem_limit_bytes=56 * MIB),
        cost_estimate=SOON
        if normed
        else pl.CostEstimate(
            flops=24 * rows * width * wide, bytes_accessed=1024, transcendentals=0
        ),
    )(source, *weights, *extra)


def settle_kernel(mine_ref, one_ref, far_ref, keep_ref, raw_ref, gain_ref, cos_ref, sin_ref, out_ref):
    head = gain_ref.shape[1]
    total = mine_ref[...] + one_ref[...] * keep_ref[...] + far_ref[...]
    out_ref[:, :head] = norm_rotate_back(
        total[:, :head], raw_ref[...], gain_ref[...], cos_ref[...], sin_ref[...]
    )
    out_ref[:, head:] = total[:, head:]


def settle(mine, one, far, keep, raw, gain, cosine, sine):
    return pl.pallas_call(
        settle_kernel,
        out_shape=jax.ShapeDtypeStruct(mine.shape, jnp.float32),
        compiler_params=pltpu.CompilerParams(vmem_limit_bytes=16 * MIB),
        cost_estimate=SOON,
    )(mine, one, far, keep, raw, gain, cosine, sine)


def turn_kernel(place_ref, others_ref, own_ref, high_ref, low_ref):
    step = pl.program_id(0)

    @pl.when(step < CHAIN - 1)
    def _():
        high_ref[0], low_ref[0] = halves(others_ref[0])

    @pl.when(step == CHAIN - 1)
    def _():
        high_ref[0], low_ref[0] = halves(own_ref[...])


def turn(place, others, own):
    slab, rows = own.shape
    half = jax.ShapeDtypeStruct((CHAIN, slab, rows), jnp.bfloat16)
    out_spec = pl.BlockSpec((1, slab, rows), lambda i, p: ((p[0] + 1 + i) % CHAIN, 0, 0))
    return pl.pallas_call(
        turn_kernel,
        grid_spec=pltpu.PrefetchScalarGridSpec(
            num_scalar_prefetch=1,
            grid=(CHAIN,),
            in_specs=[
                pl.BlockSpec((1, slab, rows), lambda i, p: (jnp.minimum(i, CHAIN - 2), 0, 0)),
                pl.BlockSpec((slab, rows), lambda i, p: (0, 0)),
            ],
            out_specs=[out_spec, out_spec],
        ),
        out_shape=[half, half],
        compiler_params=pltpu.CompilerParams(vmem_limit_bytes=24 * MIB),
        cost_estimate=SOON,
    )(place, others, own)


def product_kernel(place_ref, high_ref, low_ref, *refs):
    blocks, out_ref = refs[:-1], refs[-1]
    total = None
    for hop in range(CHAIN):
        slot = lax.rem(place_ref[0] + (CHAIN - hop), CHAIN)
        term = three((high_ref[slot], low_ref[slot]), halves(blocks[hop][...]), 1, 0)
        total = term if total is None else total + term
    out_ref[...] = total


def product(place, step, turned, blocks, pair):
    high, low = turned
    part = high.shape[1] // pair
    rows = high.shape[2]
    columns = blocks[0].shape[1]
    spec = pl.BlockSpec((CHAIN, part, rows), lambda i, p: (0, (p[1] + step) % pair, 0))
    return pl.pallas_call(
        product_kernel,
        grid_spec=pltpu.PrefetchScalarGridSpec(
            num_scalar_prefetch=1,
            grid=(1,),
            in_specs=[spec, spec] + [pl.BlockSpec(b.shape, lambda i, p: (0, 0)) for b in blocks],
            out_specs=pl.BlockSpec((part, columns), lambda i, p: (0, 0)),
        ),
        out_shape=jax.ShapeDtypeStruct((part, columns), jnp.float32),
        compiler_params=pltpu.CompilerParams(vmem_limit_bytes=28 * MIB),
        cost_estimate=SOON,
    )(place, high, low, *blocks)


def strip_kernel(pieces, strips_ref, *refs):
    weight_refs, left_refs = refs[: len(pieces)], refs[len(pieces) : -1]
    total = None
    left_at = 0
    for ref, (count, start, wide) in zip(weight_refs, pieces):
        for group in range(count):
            left = left_refs[left_at + group][:, start : start + wide]
            right = ref[:, group * wide : (group + 1) * wide]
            term = three(halves(right), halves(left), 1, 1)
            total = term if total is None else total + term
        left_at = left_at if start == 0 and len(pieces) > 1 else left_at + count
    refs[-1][0] = total


def input_strips(strips, strip, weights, lefts, pieces):
    count = strips.shape[0]
    rows = lefts[0].shape[0]
    wide = sum(w.shape[1] for w in weights)
    whole = [pl.BlockSpec(d.shape, lambda i, p: (0, 0)) for d in lefts]
    return pl.pallas_call(
        functools.partial(strip_kernel, pieces),
        grid_spec=pltpu.PrefetchScalarGridSpec(
            num_scalar_prefetch=1,
            grid=(count,),
            in_specs=[pl.BlockSpec((strip, w.shape[1]), lambda i, p: (p[i], 0)) for w in weights]
            + whole,
            out_specs=pl.BlockSpec((1, strip, rows), lambda i, p: (i, 0, 0)),
        ),
        out_shape=jax.ShapeDtypeStruct((count, strip, rows), jnp.float32),
        compiler_params=pltpu.CompilerParams(vmem_limit_bytes=56 * MIB),
        cost_estimate=SOON,
    )(strips, *weights, *lefts)


def local(hidden_in, query_proj, key_proj, value_proj, query_gain, key_gain, segment_ids, grad_out):
    rows_dev, width = hidden_in.shape
    head = query_gain.shape[0]
    kv_local = key_proj.shape[1] // head
    per_kv = query_proj.shape[1] // key_proj.shape[1]
    pair = lax.axis_size("y")
    count = CHAIN * pair
    members = lax.axis_size("tensor")
    member = lax.axis_index("tensor")
    along = lax.axis_index("z")
    across = lax.axis_index("y")
    seq_index = along * pair + across
    reach = (WINDOW - 1) // rows_dev + 1
    span = (reach + 1) * rows_dev
    slab = width // CHAIN
    part = width // count
    piece = slab // members
    groups = range(kv_local)
    short = pair == 2 and reach == 4

    def z_shift(block, step):
        route = [(i, i + step) for i in range(CHAIN) if 0 <= i + step < CHAIN]
        return lax.ppermute(block, "z", route)

    def z_ring(block, step):
        return lax.ppermute(block, "z", [(i, (i + step) % CHAIN) for i in range(CHAIN)])

    def y_ring(block, step):
        return lax.ppermute(block, "y", [(i, (i + step) % pair) for i in range(pair)])

    def shifted(block, distance):
        route = [(i - distance, i) for i in range(count) if 0 <= i - distance < count]
        return lax.ppermute(block, ("z", "y"), route)

    first_row = seq_index * rows_dev
    positions = first_row + jnp.arange(rows_dev, dtype=jnp.int32)
    cosine, sine = rope_tables(positions, head)
    seg_pad = jnp.concatenate([jnp.full((reach * rows_dev,), -1, jnp.int32), segment_ids])
    key_seg = lax.dynamic_slice_in_dim(seg_pad, first_row, span, 0)[:, None]
    query_seg = lax.dynamic_slice_in_dim(segment_ids, first_row, rows_dev, 0)[None, :]

    def q_columns(array, group):
        return array[:, group * per_kv * head : (group + 1) * per_kv * head]

    key_raw, own, two, queries = [], [], [], []
    tables = (key_gain[None, :], cosine, sine)
    for group in groups:
        source = after(hidden_in, own[-1]) if own else hidden_in
        raw, packed = project(source, (key_proj, value_proj), group, head, tables)
        key_raw.append(raw)
        own.append(packed)
        if short:
            two.append(z_shift(own[group], 1))
    hidden_rows = after(hidden_in, *own).T

    def neighbour(group, *earlier):
        block = jnp.where(across == 0, own[group], two[group])
        return y_ring(after(block, *earlier) if earlier else block, 1)

    def farthest(group, four, *earlier):
        back = after(two[group], *earlier)
        return y_ring(jnp.where(across == 0, back, four), 1)

    for group in groups:
        source = after(hidden_in, hidden_rows, *queries)
        queries.append(project(source, (query_proj,), group, per_kv * head, ())[0])

    windows, fours = [], []
    if short:
        one = neighbour(0)
        for group in groups:
            fours.append(z_shift(after(two[group], own[-1], *([one] if group else [])), 1))
        three_back = farthest(0, fours[0], one, queries[0])
        windows.append([fours[0], three_back, two[0], one, own[0]])
    else:
        for group in groups:
            windows.append([shifted(own[group], d) for d in range(reach, 0, -1)] + [own[group]])
    ready = after(hidden_rows, *fours)
    pieces = []
    for step in range(CHAIN - 1, 0, -1):
        target = (along + step) % CHAIN
        start = target * slab + member * piece
        pieces.append(z_ring(lax.dynamic_slice_in_dim(ready, start, piece, 0), step))
    if short:
        for group in groups[1:]:
            one = neighbour(group, *windows[-1])
            three_back = farthest(group, fours[group], one)
            windows.append([fours[group], three_back, two[group], one, own[group]])

    chips = members // CORES
    chip, core = member // CORES, member % CORES

    def to_core(block):
        return lax.ppermute(block, "tensor", [(i, i ^ 1) for i in range(members)])

    def to_chip(block, step):
        route = [(i, (i + step * CORES) % members) for i in range(members)]
        return lax.ppermute(block, "tensor", route)

    def in_order(blocks, index, axis):
        size = blocks[0].shape[axis]
        both = jnp.concatenate(blocks + blocks[:-1], axis=axis)
        start = (len(blocks) - 1 - index) * size
        return lax.dynamic_slice_in_dim(both, start, len(blocks) * size, axis)

    mine = jnp.stack(pieces)
    chip_rows = in_order([to_core(mine), mine], core, 1)
    arrivals = [to_chip(chip_rows, step) for step in range(chips - 1, 0, -1)]
    others = in_order(arrivals + [chip_rows], chip, 1)
    own_slab = lax.dynamic_slice_in_dim(hidden_rows, along * slab, slab, 0)
    place = jnp.stack([along, across]).astype(jnp.int32)
    turned = turn(place, others, own_slab)

    attended, d_query, parts = [], [], []
    for group in groups:
        ready = attended + (pieces if attended else [])
        out, d_q, d_kv = attention(
            after(queries[group], *ready) if ready else queries[group],
            q_columns(grad_out, group),
            query_gain[None, :],
            cosine,
            sine,
            query_seg,
            key_seg,
            windows[group],
            per_kv,
        )
        attended.append(out)
        d_query.append(d_q)
        parts.append(d_kv)

    strip = width // members
    turns = [(chip + step) % chips for step in range(chips)]
    theirs_at = jnp.stack([c * CORES + 1 - core for c in turns]).astype(jnp.int32)
    mine_at = jnp.stack([c * CORES + core for c in turns]).astype(jnp.int32)

    def query_strips(which):
        pieces = ((kv_local, 0, per_kv * head),)
        return input_strips(which, strip, (query_proj,), d_query, pieces)

    def kv_strips(which):
        pieces = ((kv_local, 0, head), (kv_local, head, head))
        return input_strips(which, strip, (key_proj, value_proj), d_kv, pieces)

    def product_of(ring, step):
        return product(place, step, turned, ring, pair)

    def terms(ring):
        return [product_of(ring, step) for step in range(pair - 1, 0, -1)]

    def exchange(sent):
        return [y_ring(term, pair - 1 - i) for i, term in enumerate(sent)]

    sent = []

    def follow(block, send, extra):
        earlier = sent[-2:-1] + list(extra)
        sent.append(send(after(block, *earlier) if earlier else block))
        return sent[-1]

    keep = jnp.where(across == 0, 1.0, 0.0).reshape(1, 1).astype(jnp.float32)
    q_rings = [[d] for d in d_query]
    d_kv, k_rings, held = [], [], []

    def q_hop(group, *extra):
        q_rings[group].append(follow(q_rings[group][-1], lambda b: z_ring(b, 1), extra))

    def k_hop(group, *extra):
        k_rings[group].append(follow(k_rings[group][-1], lambda b: z_ring(b, 1), extra))

    def far_return(group, *extra):
        four, three_back, two_back, one, mine = parts[group]
        from_three = y_ring(three_back, 1)
        from_one = y_ring(one, 1)
        block = four + jnp.where(across == 0, 0.0, from_three)
        got = follow(block, lambda b: z_shift(b, -1), extra)
        held.append((two_back + jnp.where(across == 0, from_three, from_one) + got, from_one))

    def near_return(group, *extra):
        block, from_one = held[group]
        far = follow(block, lambda b: z_shift(b, -1), extra)
        mine = parts[group][-1]
        d_kv.append(settle(mine, from_one, far, keep, key_raw[group], *tables))
        k_rings.append([d_kv[group]])

    if short and kv_local == 2:
        q_hop(0)
        far_return(0, q_rings[0][1])
        q_hop(0)
        near_return(0)
        q_hop(1)
        far_return(1)
        theirs_q = query_strips(theirs_at)
        q_hop(0)
        near_return(1)
        mine_q = query_strips(mine_at)
        q_hop(1, theirs_q)
        k_hop(0, mine_q)
        q_terms = [terms(q_rings[0])]
        q_hop(1, *q_terms[0])
        k_hop(0)
        theirs = theirs_q + kv_strips(theirs_at)
        q_sent = [exchange(q_terms[0])]
        k_hop(1, theirs)
        q_terms.append(terms(q_rings[1]))
        k_hop(0, *q_terms[1])
        sums = mine_q + kv_strips(mine_at)
        k_hop(1, sums, *q_sent[0])
        k_terms = [terms(k_rings[0])]
        k_hop(1, *k_terms[0])
        q_sent.append(exchange(q_terms[1]))
        k_terms.append(terms(k_rings[1]))
    else:
        for group in groups:
            mine = parts[group][reach]
            total = jnp.zeros_like(mine)
            for distance in range(1, reach + 1):
                total = total + shifted(parts[group][reach - distance], -distance)
            d_kv.append(settle(mine, mine, total, 0.0 * keep, key_raw[group], *tables))
            k_rings.append([d_kv[group]])
            for _ in range(CHAIN - 1):
                q_hop(group)
            for _ in range(CHAIN - 1):
                k_hop(group)
        theirs = query_strips(theirs_at) + kv_strips(theirs_at)
        sums = query_strips(mine_at) + kv_strips(mine_at)
        q_sent = [exchange(terms(ring)) for ring in q_rings]
        k_terms = [terms(ring) for ring in k_rings]

    sums = sums + to_core(theirs)
    grad_input = sums[0]
    for step in range(1, chips):
        grad_input = grad_input + to_chip(sums[step], step)

    def finish(ring, arrived):
        total = product_of(ring, 0)
        for term in arrived:
            total = total + term
        return total

    grad_query = [finish(ring, arrived) for ring, arrived in zip(q_rings, q_sent)]
    grad_kv = [finish(ring, exchange(term)) for ring, term in zip(k_rings, k_terms)]

    return (
        jnp.concatenate(attended, axis=1),
        grad_input.T,
        jnp.concatenate(grad_query, axis=1),
        jnp.concatenate([g[:, :head] for g in grad_kv], axis=1),
        jnp.concatenate([g[:, head:] for g in grad_kv], axis=1),
    )


def solution(mesh):
    seq, members = mesh.devices.shape
    split = Mesh(mesh.devices.reshape(CHAIN, seq // CHAIN, members), ("z", "y", "tensor"))
    tokens = ("z", "y")
    return jax.shard_map(
        local,
        mesh=split,
        in_specs=(
            P(tokens, None),
            P(None, "tensor"),
            P(None, "tensor"),
            P(None, "tensor"),
            P(),
            P(),
            P(),
            P(tokens, "tensor"),
        ),
        out_specs=(
            P(tokens, "tensor"),
            P(tokens, "tensor"),
            P(tokens, "tensor"),
            P(tokens, "tensor"),
            P(tokens, "tensor"),
        ),
        check_vma=False,
    )
```

```python
import functools

import jax
import jax.numpy as jnp
from jax import lax
from jax.experimental import pallas as pl
from jax.experimental.pallas import tpu as pltpu
from jax.sharding import Mesh, PartitionSpec as P

WINDOW = 1024
CHAIN = 4
CORES = 2

MIB = 1024 * 1024
SOON = pl.CostEstimate(flops=1024, bytes_accessed=1024, transcendentals=0)
epsilon = 1e-06


def after(block, *earlier):
    return lax.optimization_barrier((block, earlier))[0]


def rope_tables(positions, head_width):
    middle = head_width // 2
    exponent = 2.0 * jnp.arange(middle).astype(jnp.float32) / head_width
    frequency = 10000.0 ** (-exponent)
    angles = positions.astype(jnp.float32)[:, None] * frequency[None, :]
    return jnp.cos(angles), jnp.sin(angles)


def inverse_rms(vector):
    return lax.rsqrt(jnp.mean(vector * vector, axis=-1, keepdims=True) + epsilon)


def norm_rotate(vector, scaling, cosine, sine):
    middle = vector.shape[-1] // 2
    normed = vector * inverse_rms(vector) * scaling
    low, high = normed[:, :middle], normed[:, middle:]
    return jnp.concatenate([low * cosine - high * sine, high * cosine + low * sine], axis=1)


def norm_rotate_back(grad, vector, scaling, cosine, sine):
    middle = vector.shape[-1] // 2
    low, high = grad[:, :middle], grad[:, middle:]
    d_normed = jnp.concatenate([low * cosine + high * sine, high * cosine - low * sine], axis=1)
    d_normed = d_normed * scaling
    inverse = inverse_rms(vector)
    unit = vector * inverse
    return inverse * (d_normed - unit * jnp.mean(d_normed * unit, axis=-1, keepdims=True))


def halves(array):
    high = array.astype(jnp.bfloat16)
    return high, (array - high.astype(jnp.float32)).astype(jnp.bfloat16)


def three(left, right, left_dim, right_dim):
    def once(a, b):
        return lax.dot_general(
            a, b, (((left_dim,), (right_dim,)), ((), ())), preferred_element_type=jnp.float32
        )

    return once(left[0], right[0]) + (once(left[0], right[1]) + once(left[1], right[0]))


def attention_kernel(blocks, per_kv, *refs):
    query_ref, grad_ref, gain_ref, cos_ref, sin_ref, seg_ref, key_seg_ref = refs[:7]
    kv_refs = refs[7 : 7 + blocks]
    out_ref, d_query_ref = refs[7 + blocks : 9 + blocks]
    d_kv_refs = refs[9 + blocks : 9 + 2 * blocks]
    weight_ref, d_share_ref, share_high, share_low, score_high, score_low = refs[9 + 2 * blocks :]
    rows = query_ref.shape[0]
    head = gain_ref.shape[1]
    factor = head ** (-0.5)
    gain, cosine, sine = gain_ref[...], cos_ref[...], sin_ref[...]
    raw = [query_ref[:, h * head : (h + 1) * head] for h in range(per_kv)]
    q_rot = halves(
        jnp.concatenate([norm_rotate(u, gain, cosine, sine) for u in raw], axis=0)
    )
    grad = halves(
        jnp.concatenate([grad_ref[:, h * head : (h + 1) * head] for h in range(per_kv)], axis=0)
    )
    total = jnp.zeros((1, per_kv * rows), jnp.float32)
    mixed = jnp.zeros((1, per_kv * rows), jnp.float32)
    seg = jnp.concatenate([seg_ref[...]] * per_kv, axis=1)
    turned_keys, turned_values = [], []
    lane = lax.broadcasted_iota(jnp.int32, (rows, rows), 1)
    lane = jnp.concatenate([lane] * per_kv, axis=1)
    row = lax.broadcasted_iota(jnp.int32, (rows, per_kv * rows), 0)
    for j in range(blocks):
        place = slice(j * rows, (j + 1) * rows)
        key, value = kv_refs[j][:, :head], kv_refs[j][:, head:]
        turned_keys.append(key.T)
        turned_values.append(value.T)
        scores = three(halves(key), q_rot, 1, 1) * factor
        distance = (blocks - 1 - j) * rows + lane - row
        allowed = (distance >= 0) & (distance < WINDOW) & (key_seg_ref[place, :] == seg)
        weights = jnp.where(allowed, jnp.exp(scores), 0.0)
        d_shares = three(halves(value), grad, 1, 1)
        weight_ref[place, :] = weights
        d_share_ref[place, :] = d_shares
        total = total + jnp.sum(weights, axis=0, keepdims=True)
        mixed = mixed + jnp.sum(weights * d_shares, axis=0, keepdims=True)
    scale = 1.0 / total
    delta = mixed * scale
    for j in range(blocks):
        place = slice(j * rows, (j + 1) * rows)
        shares = weight_ref[place, :] * scale
        d_scores = shares * (d_share_ref[place, :] - delta) * factor
        share_pair = halves(shares)
        score_pair = halves(d_scores)
        share_high[place, :], share_low[place, :] = share_pair
        score_high[place, :], score_low[place, :] = score_pair
        d_kv_refs[j][:, :head] = three(score_pair, q_rot, 1, 0)
        d_kv_refs[j][:, head:] = three(share_pair, grad, 1, 0)
    turned_out = three(
        halves(jnp.concatenate(turned_values, axis=1)), (share_high[...], share_low[...]), 1, 0
    )
    turned_query = three(
        halves(jnp.concatenate(turned_keys, axis=1)), (score_high[...], score_low[...]), 1, 0
    )
    for h in range(per_kv):
        place = slice(h * rows, (h + 1) * rows)
        columns = slice(h * head, (h + 1) * head)
        out_ref[:, columns] = turned_out[:, place].T
        d_query_ref[:, columns] = norm_rotate_back(
            turned_query[:, place].T, raw[h], gain, cosine, sine
        )


def attention(queries, grads, gain, cosine, sine, query_seg, key_seg, window, per_kv):
    rows, width = queries.shape
    blocks = len(window)
    span = blocks * rows
    flat = jax.ShapeDtypeStruct((rows, width), jnp.float32)
    part = jax.ShapeDtypeStruct(window[0].shape, jnp.float32)
    wide = per_kv * rows
    results = pl.pallas_call(
        functools.partial(attention_kernel, blocks, per_kv),
        out_shape=[flat, flat] + [part] * blocks,
        scratch_shapes=[
            pltpu.VMEM((span, wide), jnp.float32),
            pltpu.VMEM((span, wide), jnp.float32),
            pltpu.VMEM((span, wide), jnp.bfloat16),
            pltpu.VMEM((span, wide), jnp.bfloat16),
            pltpu.VMEM((span, wide), jnp.bfloat16),
            pltpu.VMEM((span, wide), jnp.bfloat16),
        ],
        compiler_params=pltpu.CompilerParams(vmem_limit_bytes=40 * 1024 * 1024),
        cost_estimate=SOON,
    )(queries, grads, gain, cosine, sine, query_seg, key_seg, *window)
    return results[0], results[1], results[2:]


def project_kernel(normed, lanes, source_ref, *refs):
    if normed:
        weight_refs, rest = refs[: 2 * lanes], refs[2 * lanes :]
        gain_ref, cos_ref, sin_ref, raw_ref, packed_ref, total_ref = rest
    else:
        weight_refs, (raw_ref, total_ref) = refs[:lanes], refs[lanes:]
    step = pl.program_id(0)
    stacked = [
        jnp.concatenate([ref[...] for ref in weight_refs[start : start + lanes]], axis=0)
        for start in range(0, len(weight_refs), lanes)
    ]
    weight = stacked[0] if len(stacked) == 1 else jnp.concatenate(stacked, axis=1)
    product = three(halves(source_ref[...]), halves(weight), 1, 0)

    @pl.when(step == 0)
    def _():
        total_ref[...] = product

    @pl.when(step > 0)
    def _():
        total_ref[...] += product

    @pl.when(step == pl.num_programs(0) - 1)
    def _():
        if normed:
            head = gain_ref.shape[1]
            raw = total_ref[:, :head]
            raw_ref[...] = raw
            packed_ref[:, :head] = norm_rotate(raw, gain_ref[...], cos_ref[...], sin_ref[...])
            packed_ref[:, head:] = total_ref[:, head:]
        else:
            raw_ref[...] = total_ref[...]


def project(source, weights, group, columns, extra):
    rows, width = source.shape
    steps, lanes = 5, 3
    tile = width // steps
    thin = tile // lanes
    normed = len(weights) > 1
    wide = columns * len(weights)
    whole = [pl.BlockSpec(e.shape, lambda k: (0, 0)) for e in extra]
    outs = [jax.ShapeDtypeStruct((rows, columns), jnp.float32)]
    if normed:
        outs.append(jax.ShapeDtypeStruct((rows, wide), jnp.float32))
    return pl.pallas_call(
        functools.partial(project_kernel, normed, lanes),
        grid=(steps,),
        out_shape=outs,
        in_specs=[pl.BlockSpec((rows, tile), lambda k: (0, k))]
        + [
            pl.BlockSpec((thin, columns), lambda k, lane=lane: (k * lanes + lane, group))
            for lane in range(lanes)
        ]
        * len(weights)
        + whole,
        out_specs=[pl.BlockSpec(o.shape, lambda k: (0, 0)) for o in outs],
        scratch_shapes=[pltpu.VMEM((rows, wide), jnp.float32)],
        compiler_params=pltpu.CompilerParams(vmem_limit_bytes=56 * MIB),
        cost_estimate=SOON
        if normed
        else pl.CostEstimate(
            flops=24 * rows * width * wide, bytes_accessed=1024, transcendentals=0
        ),
    )(source, *[w for w in weights for _ in range(lanes)], *extra)


def settle_kernel(mine_ref, one_ref, far_ref, keep_ref, raw_ref, gain_ref, cos_ref, sin_ref, out_ref):
    head = gain_ref.shape[1]
    total = mine_ref[...] + one_ref[...] * keep_ref[...] + far_ref[...]
    out_ref[:, :head] = norm_rotate_back(
        total[:, :head], raw_ref[...], gain_ref[...], cos_ref[...], sin_ref[...]
    )
    out_ref[:, head:] = total[:, head:]


def settle(mine, one, far, keep, raw, gain, cosine, sine):
    return pl.pallas_call(
        settle_kernel,
        out_shape=jax.ShapeDtypeStruct(mine.shape, jnp.float32),
        compiler_params=pltpu.CompilerParams(vmem_limit_bytes=16 * MIB),
        cost_estimate=SOON,
    )(mine, one, far, keep, raw, gain, cosine, sine)


def flip_kernel(source_ref, out_ref):
    out_ref[...] = source_ref[...].T


def flip(source):
    rows, width = source.shape
    tile = width // 5
    return pl.pallas_call(
        flip_kernel,
        grid=(5,),
        out_shape=jax.ShapeDtypeStruct((width, rows), jnp.float32),
        in_specs=[pl.BlockSpec((rows, tile), lambda k: (0, k))],
        out_specs=pl.BlockSpec((tile, rows), lambda k: (k, 0)),
        compiler_params=pltpu.CompilerParams(vmem_limit_bytes=16 * MIB),
        cost_estimate=SOON,
    )(source)


def turn_kernel(place_ref, others_ref, own_ref, high_ref, low_ref):
    step = pl.program_id(0)

    @pl.when(step < CHAIN - 1)
    def _():
        high_ref[0], low_ref[0] = halves(others_ref[0])

    @pl.when(step == CHAIN - 1)
    def _():
        high_ref[0], low_ref[0] = halves(own_ref[...])


def turn(place, others, own):
    slab, rows = own.shape
    half = jax.ShapeDtypeStruct((CHAIN, slab, rows), jnp.bfloat16)
    out_spec = pl.BlockSpec((1, slab, rows), lambda i, p: ((p[0] + 1 + i) % CHAIN, 0, 0))
    return pl.pallas_call(
        turn_kernel,
        grid_spec=pltpu.PrefetchScalarGridSpec(
            num_scalar_prefetch=1,
            grid=(CHAIN,),
            in_specs=[
                pl.BlockSpec((1, slab, rows), lambda i, p: (jnp.minimum(i, CHAIN - 2), 0, 0)),
                pl.BlockSpec((slab, rows), lambda i, p: (0, 0)),
            ],
            out_specs=[out_spec, out_spec],
        ),
        out_shape=[half, half],
        compiler_params=pltpu.CompilerParams(vmem_limit_bytes=24 * MIB),
        cost_estimate=SOON,
    )(place, others, own)


def product_kernel(place_ref, high_ref, low_ref, *refs):
    blocks, out_ref = refs[:-1], refs[-1]
    total = None
    for hop in range(CHAIN):
        slot = lax.rem(place_ref[0] + (CHAIN - hop), CHAIN)
        term = three((high_ref[slot], low_ref[slot]), halves(blocks[hop][...]), 1, 0)
        total = term if total is None else total + term
    out_ref[...] = total


def product(place, step, turned, blocks, pair):
    high, low = turned
    part = high.shape[1] // pair
    rows = high.shape[2]
    columns = blocks[0].shape[1]
    spec = pl.BlockSpec((CHAIN, part, rows), lambda i, p: (0, (p[1] + step) % pair, 0))
    return pl.pallas_call(
        product_kernel,
        grid_spec=pltpu.PrefetchScalarGridSpec(
            num_scalar_prefetch=1,
            grid=(1,),
            in_specs=[spec, spec] + [pl.BlockSpec(b.shape, lambda i, p: (0, 0)) for b in blocks],
            out_specs=pl.BlockSpec((part, columns), lambda i, p: (0, 0)),
        ),
        out_shape=jax.ShapeDtypeStruct((part, columns), jnp.float32),
        compiler_params=pltpu.CompilerParams(vmem_limit_bytes=28 * MIB),
        cost_estimate=SOON,
    )(place, high, low, *blocks)


def strip_kernel(pieces, strips_ref, *refs):
    weight_refs, left_refs = refs[: len(pieces)], refs[len(pieces) : -1]
    total = None
    left_at = 0
    for ref, (count, start, wide) in zip(weight_refs, pieces):
        for group in range(count):
            left = left_refs[left_at + group][:, start : start + wide]
            right = ref[:, group * wide : (group + 1) * wide]
            term = three(halves(right), halves(left), 1, 1)
            total = term if total is None else total + term
        left_at = left_at if start == 0 and len(pieces) > 1 else left_at + count
    refs[-1][0] = total


def input_strips(strips, strip, weights, lefts, pieces):
    count = strips.shape[0]
    rows = lefts[0].shape[0]
    wide = sum(w.shape[1] for w in weights)
    whole = [pl.BlockSpec(d.shape, lambda i, p: (0, 0)) for d in lefts]
    return pl.pallas_call(
        functools.partial(strip_kernel, pieces),
        grid_spec=pltpu.PrefetchScalarGridSpec(
            num_scalar_prefetch=1,
            grid=(count,),
            in_specs=[pl.BlockSpec((strip, w.shape[1]), lambda i, p: (p[i], 0)) for w in weights]
            + whole,
            out_specs=pl.BlockSpec((1, strip, rows), lambda i, p: (i, 0, 0)),
        ),
        out_shape=jax.ShapeDtypeStruct((count, strip, rows), jnp.float32),
        compiler_params=pltpu.CompilerParams(vmem_limit_bytes=56 * MIB),
        cost_estimate=SOON,
    )(strips, *weights, *lefts)


def local(hidden_in, query_proj, key_proj, value_proj, query_gain, key_gain, segment_ids, grad_out):
    rows_dev, width = hidden_in.shape
    head = query_gain.shape[0]
    kv_local = key_proj.shape[1] // head
    per_kv = query_proj.shape[1] // key_proj.shape[1]
    pair = lax.axis_size("y")
    count = CHAIN * pair
    members = lax.axis_size("tensor")
    member = lax.axis_index("tensor")
    along = lax.axis_index("z")
    across = lax.axis_index("y")
    seq_index = along * pair + across
    reach = (WINDOW - 1) // rows_dev + 1
    span = (reach + 1) * rows_dev
    slab = width // CHAIN
    part = width // count
    piece = slab // members
    groups = range(kv_local)
    short = pair == 2 and reach == 4

    def z_shift(block, step):
        route = [(i, i + step) for i in range(CHAIN) if 0 <= i + step < CHAIN]
        return lax.ppermute(block, "z", route)

    def z_ring(block, step):
        return lax.ppermute(block, "z", [(i, (i + step) % CHAIN) for i in range(CHAIN)])

    def y_ring(block, step):
        return lax.ppermute(block, "y", [(i, (i + step) % pair) for i in range(pair)])

    def shifted(block, distance):
        route = [(i - distance, i) for i in range(count) if 0 <= i - distance < count]
        return lax.ppermute(block, ("z", "y"), route)

    first_row = seq_index * rows_dev
    positions = first_row + jnp.arange(rows_dev, dtype=jnp.int32)
    cosine, sine = rope_tables(positions, head)
    seg_pad = jnp.concatenate([jnp.full((reach * rows_dev,), -1, jnp.int32), segment_ids])
    key_seg = lax.dynamic_slice_in_dim(seg_pad, first_row, span, 0)[:, None]
    query_seg = lax.dynamic_slice_in_dim(segment_ids, first_row, rows_dev, 0)[None, :]

    def q_columns(array, group):
        return array[:, group * per_kv * head : (group + 1) * per_kv * head]

    key_raw, own, two, queries = [], [], [], []
    tables = (key_gain[None, :], cosine, sine)
    for group in groups:
        source = after(hidden_in, own[-1]) if own else hidden_in
        raw, packed = project(source, (key_proj, value_proj), group, head, tables)
        key_raw.append(raw)
        own.append(packed)
        if short:
            two.append(z_shift(own[group], 1))

    def neighbour(group, *earlier):
        block = jnp.where(across == 0, own[group], two[group])
        return y_ring(after(block, *earlier) if earlier else block, 1)

    def farthest(group, four, *earlier):
        back = after(two[group], *earlier)
        return y_ring(jnp.where(across == 0, back, four), 1)

    for group in groups:
        source = after(hidden_in, *own, *queries)
        queries.append(project(source, (query_proj,), group, per_kv * head, ())[0])

    hidden_rows = flip(after(hidden_in, *queries))
    windows, fours, ones = [], [], []
    if short:
        for group in groups:
            ones.append(neighbour(group))
        for group in groups:
            fours.append(z_shift(after(two[group], own[-1], *ones[:group]), 1))
        for group in groups:
            earlier = [w[1] for w in windows]
            three_back = farthest(group, fours[group], *ones, hidden_rows, *earlier)
            windows.append([fours[group], three_back, two[group], ones[group], own[group]])
    else:
        for group in groups:
            windows.append([shifted(own[group], d) for d in range(reach, 0, -1)] + [own[group]])
    pieces = []
    for step in range(CHAIN - 1, 0, -1):
        target = (along + step) % CHAIN
        start = target * slab + member * piece
        pieces.append(z_ring(lax.dynamic_slice_in_dim(hidden_rows, start, piece, 0), step))
    chips = members // CORES
    chip, core = member // CORES, member % CORES

    def to_core(block):
        return lax.ppermute(block, "tensor", [(i, i ^ 1) for i in range(members)])

    def to_chip(block, step):
        route = [(i, (i + step * CORES) % members) for i in range(members)]
        return lax.ppermute(block, "tensor", route)

    def in_order(blocks, index, axis):
        size = blocks[0].shape[axis]
        both = jnp.concatenate(blocks + blocks[:-1], axis=axis)
        start = (len(blocks) - 1 - index) * size
        return lax.dynamic_slice_in_dim(both, start, len(blocks) * size, axis)

    mine = jnp.stack(pieces)
    chip_rows = in_order([to_core(mine), mine], core, 1)
    arrivals = [to_chip(chip_rows, step) for step in range(chips - 1, 0, -1)]
    others = in_order(arrivals + [chip_rows], chip, 1)
    own_slab = lax.dynamic_slice_in_dim(hidden_rows, along * slab, slab, 0)
    place = jnp.stack([along, across]).astype(jnp.int32)
    turned = turn(place, others, own_slab)

    attended, d_query, parts = [], [], []
    for group in groups:
        ready = attended or (pieces + [w[1] for w in windows])
        out, d_q, d_kv = attention(
            after(queries[group], *ready),
            q_columns(grad_out, group),
            query_gain[None, :],
            cosine,
            sine,
            query_seg,
            key_seg,
            windows[group],
            per_kv,
        )
        attended.append(out)
        d_query.append(d_q)
        parts.append(d_kv)

    strip = width // members
    turns = [(chip + step) % chips for step in range(chips)]
    theirs_at = jnp.stack([c * CORES + 1 - core for c in turns]).astype(jnp.int32)
    mine_at = jnp.stack([c * CORES + core for c in turns]).astype(jnp.int32)

    def query_strips(which):
        pieces = ((kv_local, 0, per_kv * head),)
        return input_strips(which, strip, (query_proj,), d_query, pieces)

    def kv_strips(which):
        pieces = ((kv_local, 0, head), (kv_local, head, head))
        return input_strips(which, strip, (key_proj, value_proj), d_kv, pieces)

    def product_of(ring, step):
        return product(place, step, turned, ring, pair)

    def terms(ring):
        return [product_of(ring, step) for step in range(pair - 1, 0, -1)]

    def exchange(sent):
        return [y_ring(term, pair - 1 - i) for i, term in enumerate(sent)]

    sent = []

    def follow(block, send, extra):
        earlier = sent[-2:-1] + list(extra)
        sent.append(send(after(block, *earlier) if earlier else block))
        return sent[-1]

    keep = jnp.where(across == 0, 1.0, 0.0).reshape(1, 1).astype(jnp.float32)
    q_rings = [[d] for d in d_query]
    d_kv, k_rings, held = [], [], []

    def q_hop(group, *extra):
        q_rings[group].append(follow(q_rings[group][-1], lambda b: z_ring(b, 1), extra))

    def k_hop(group, *extra):
        k_rings[group].append(follow(k_rings[group][-1], lambda b: z_ring(b, 1), extra))

    def far_return(group, *extra):
        four, three_back, two_back, one, mine = parts[group]
        from_three = y_ring(three_back, 1)
        from_one = y_ring(one, 1)
        block = four + jnp.where(across == 0, 0.0, from_three)
        got = follow(block, lambda b: z_shift(b, -1), extra)
        held.append((two_back + jnp.where(across == 0, from_three, from_one) + got, from_one))

    def near_return(group, *extra):
        block, from_one = held[group]
        far = follow(block, lambda b: z_shift(b, -1), extra)
        mine = parts[group][-1]
        d_kv.append(settle(mine, from_one, far, keep, key_raw[group], *tables))
        k_rings.append([d_kv[group]])

    if short and kv_local == 2:
        q_hop(0)
        far_return(0, q_rings[0][1])
        q_hop(0)
        near_return(0)
        q_hop(1)
        far_return(1)
        theirs_q = query_strips(theirs_at)
        q_hop(0)
        near_return(1)
        mine_q = query_strips(mine_at)
        q_hop(1, theirs_q)
        k_hop(0, mine_q)
        q_terms = [terms(q_rings[0])]
        q_hop(1, *q_terms[0])
        k_hop(0)
        theirs = theirs_q + kv_strips(theirs_at)
        q_sent = [exchange(q_terms[0])]
        k_hop(1, theirs)
        q_terms.append(terms(q_rings[1]))
        k_hop(0, *q_terms[1])
        sums = mine_q + kv_strips(mine_at)
        k_hop(1, sums, *q_sent[0])
        k_terms = [terms(k_rings[0])]
        q_sent.append(exchange(q_terms[1]))
        k_hop(1, *k_terms[0], *q_sent[1])
        k_terms.append(terms(k_rings[1]))
    else:
        for group in groups:
            mine = parts[group][reach]
            total = jnp.zeros_like(mine)
            for distance in range(1, reach + 1):
                total = total + shifted(parts[group][reach - distance], -distance)
            d_kv.append(settle(mine, mine, total, 0.0 * keep, key_raw[group], *tables))
            k_rings.append([d_kv[group]])
            for _ in range(CHAIN - 1):
                q_hop(group)
            for _ in range(CHAIN - 1):
                k_hop(group)
        theirs = query_strips(theirs_at) + kv_strips(theirs_at)
        sums = query_strips(mine_at) + kv_strips(mine_at)
        q_sent = [exchange(terms(ring)) for ring in q_rings]
        k_terms = [terms(ring) for ring in k_rings]

    sums = sums + to_core(theirs)
    grad_input = sums[0]
    for step in range(1, chips):
        grad_input = grad_input + to_chip(sums[step], step)

    def finish(ring, arrived):
        total = product_of(ring, 0)
        for term in arrived:
            total = total + term
        return total

    grad_query = [finish(ring, arrived) for ring, arrived in zip(q_rings, q_sent)]
    grad_kv = [finish(ring, exchange(term)) for ring, term in zip(k_rings, k_terms)]

    return (
        jnp.concatenate(attended, axis=1),
        grad_input.T,
        jnp.concatenate(grad_query, axis=1),
        jnp.concatenate([g[:, :head] for g in grad_kv], axis=1),
        jnp.concatenate([g[:, head:] for g in grad_kv], axis=1),
    )


def solution(mesh):
    seq, members = mesh.devices.shape
    split = Mesh(mesh.devices.reshape(CHAIN, seq // CHAIN, members), ("z", "y", "tensor"))
    tokens = ("z", "y")
    return jax.shard_map(
        local,
        mesh=split,
        in_specs=(
            P(tokens, None),
            P(None, "tensor"),
            P(None, "tensor"),
            P(None, "tensor"),
            P(),
            P(),
            P(),
            P(tokens, "tensor"),
        ),
        out_specs=(
            P(tokens, "tensor"),
            P(tokens, "tensor"),
            P(tokens, "tensor"),
            P(tokens, "tensor"),
            P(tokens, "tensor"),
        ),
        check_vma=False,
    )
```

```python
import functools

import jax
import jax.numpy as jnp
from jax import lax
from jax.experimental import pallas as pl
from jax.experimental.pallas import tpu as pltpu
from jax.sharding import Mesh, PartitionSpec as P

WINDOW = 1024
CHAIN = 4
CORES = 2

MIB = 1024 * 1024
SOON = pl.CostEstimate(flops=1024, bytes_accessed=1024, transcendentals=0)
epsilon = 1e-06


def after(block, *earlier):
    return lax.optimization_barrier((block, earlier))[0]


def rope_tables(positions, head_width):
    middle = head_width // 2
    exponent = 2.0 * jnp.arange(middle).astype(jnp.float32) / head_width
    frequency = 10000.0 ** (-exponent)
    angles = positions.astype(jnp.float32)[:, None] * frequency[None, :]
    return jnp.cos(angles), jnp.sin(angles)


def inverse_rms(vector):
    return lax.rsqrt(jnp.mean(vector * vector, axis=-1, keepdims=True) + epsilon)


def norm_rotate(vector, scaling, cosine, sine):
    middle = vector.shape[-1] // 2
    normed = vector * inverse_rms(vector) * scaling
    low, high = normed[:, :middle], normed[:, middle:]
    return jnp.concatenate([low * cosine - high * sine, high * cosine + low * sine], axis=1)


def norm_rotate_back(grad, vector, scaling, cosine, sine):
    middle = vector.shape[-1] // 2
    low, high = grad[:, :middle], grad[:, middle:]
    d_normed = jnp.concatenate([low * cosine + high * sine, high * cosine - low * sine], axis=1)
    d_normed = d_normed * scaling
    inverse = inverse_rms(vector)
    unit = vector * inverse
    return inverse * (d_normed - unit * jnp.mean(d_normed * unit, axis=-1, keepdims=True))


def halves(array):
    high = array.astype(jnp.bfloat16)
    return high, (array - high.astype(jnp.float32)).astype(jnp.bfloat16)


def three(left, right, left_dim, right_dim):
    def once(a, b):
        return lax.dot_general(
            a, b, (((left_dim,), (right_dim,)), ((), ())), preferred_element_type=jnp.float32
        )

    return once(left[0], right[0]) + (once(left[0], right[1]) + once(left[1], right[0]))


def attention_kernel(blocks, per_kv, *refs):
    query_ref, grad_ref, gain_ref, cos_ref, sin_ref, seg_ref, key_seg_ref = refs[:7]
    kv_refs = refs[7 : 7 + blocks]
    out_ref, d_query_ref = refs[7 + blocks : 9 + blocks]
    d_kv_refs = refs[9 + blocks : 9 + 2 * blocks]
    weight_ref, d_share_ref, share_high, share_low, score_high, score_low = refs[9 + 2 * blocks :]
    rows = query_ref.shape[0]
    head = gain_ref.shape[1]
    factor = head ** (-0.5)
    gain, cosine, sine = gain_ref[...], cos_ref[...], sin_ref[...]
    raw = [query_ref[:, h * head : (h + 1) * head] for h in range(per_kv)]
    q_rot = halves(
        jnp.concatenate([norm_rotate(u, gain, cosine, sine) for u in raw], axis=0)
    )
    grad = halves(
        jnp.concatenate([grad_ref[:, h * head : (h + 1) * head] for h in range(per_kv)], axis=0)
    )
    total = jnp.zeros((1, per_kv * rows), jnp.float32)
    mixed = jnp.zeros((1, per_kv * rows), jnp.float32)
    seg = jnp.concatenate([seg_ref[...]] * per_kv, axis=1)
    turned_keys, turned_values = [], []
    lane = lax.broadcasted_iota(jnp.int32, (rows, rows), 1)
    lane = jnp.concatenate([lane] * per_kv, axis=1)
    row = lax.broadcasted_iota(jnp.int32, (rows, per_kv * rows), 0)
    for j in range(blocks):
        place = slice(j * rows, (j + 1) * rows)
        key, value = kv_refs[j][:, :head], kv_refs[j][:, head:]
        turned_keys.append(key.T)
        turned_values.append(value.T)
        scores = three(halves(key), q_rot, 1, 1) * factor
        distance = (blocks - 1 - j) * rows + lane - row
        allowed = (distance >= 0) & (distance < WINDOW) & (key_seg_ref[place, :] == seg)
        weights = jnp.where(allowed, jnp.exp(scores), 0.0)
        d_shares = three(halves(value), grad, 1, 1)
        weight_ref[place, :] = weights
        d_share_ref[place, :] = d_shares
        total = total + jnp.sum(weights, axis=0, keepdims=True)
        mixed = mixed + jnp.sum(weights * d_shares, axis=0, keepdims=True)
    scale = 1.0 / total
    delta = mixed * scale
    for j in range(blocks):
        place = slice(j * rows, (j + 1) * rows)
        shares = weight_ref[place, :] * scale
        d_scores = shares * (d_share_ref[place, :] - delta) * factor
        share_pair = halves(shares)
        score_pair = halves(d_scores)
        share_high[place, :], share_low[place, :] = share_pair
        score_high[place, :], score_low[place, :] = score_pair
        d_kv_refs[j][:, :head] = three(score_pair, q_rot, 1, 0)
        d_kv_refs[j][:, head:] = three(share_pair, grad, 1, 0)
    turned_out = three(
        halves(jnp.concatenate(turned_values, axis=1)), (share_high[...], share_low[...]), 1, 0
    )
    turned_query = three(
        halves(jnp.concatenate(turned_keys, axis=1)), (score_high[...], score_low[...]), 1, 0
    )
    for h in range(per_kv):
        place = slice(h * rows, (h + 1) * rows)
        columns = slice(h * head, (h + 1) * head)
        out_ref[:, columns] = turned_out[:, place].T
        d_query_ref[:, columns] = norm_rotate_back(
            turned_query[:, place].T, raw[h], gain, cosine, sine
        )


def attention(queries, grads, gain, cosine, sine, query_seg, key_seg, window, per_kv):
    rows, width = queries.shape
    blocks = len(window)
    span = blocks * rows
    flat = jax.ShapeDtypeStruct((rows, width), jnp.float32)
    part = jax.ShapeDtypeStruct(window[0].shape, jnp.float32)
    wide = per_kv * rows
    results = pl.pallas_call(
        functools.partial(attention_kernel, blocks, per_kv),
        out_shape=[flat, flat] + [part] * blocks,
        scratch_shapes=[
            pltpu.VMEM((span, wide), jnp.float32),
            pltpu.VMEM((span, wide), jnp.float32),
            pltpu.VMEM((span, wide), jnp.bfloat16),
            pltpu.VMEM((span, wide), jnp.bfloat16),
            pltpu.VMEM((span, wide), jnp.bfloat16),
            pltpu.VMEM((span, wide), jnp.bfloat16),
        ],
        compiler_params=pltpu.CompilerParams(vmem_limit_bytes=40 * 1024 * 1024),
        cost_estimate=SOON,
    )(queries, grads, gain, cosine, sine, query_seg, key_seg, *window)
    return results[0], results[1], results[2:]


def project_kernel(normed, lanes, source_ref, *refs):
    if normed:
        weight_refs, rest = refs[: 2 * lanes], refs[2 * lanes :]
        gain_ref, cos_ref, sin_ref, raw_ref, packed_ref, total_ref = rest
    else:
        weight_refs, (raw_ref, total_ref) = refs[:lanes], refs[lanes:]
    step = pl.program_id(0)
    stacked = [
        jnp.concatenate([ref[...] for ref in weight_refs[start : start + lanes]], axis=0)
        for start in range(0, len(weight_refs), lanes)
    ]
    weight = stacked[0] if len(stacked) == 1 else jnp.concatenate(stacked, axis=1)
    product = three(halves(source_ref[...]), halves(weight), 1, 0)

    @pl.when(step == 0)
    def _():
        total_ref[...] = product

    @pl.when(step > 0)
    def _():
        total_ref[...] += product

    @pl.when(step == pl.num_programs(0) - 1)
    def _():
        if normed:
            head = gain_ref.shape[1]
            raw = total_ref[:, :head]
            raw_ref[...] = raw
            packed_ref[:, :head] = norm_rotate(raw, gain_ref[...], cos_ref[...], sin_ref[...])
            packed_ref[:, head:] = total_ref[:, head:]
        else:
            raw_ref[...] = total_ref[...]


def project(source, weights, group, columns, extra):
    rows, width = source.shape
    steps, lanes = 5, 3
    tile = width // steps
    thin = tile // lanes
    normed = len(weights) > 1
    wide = columns * len(weights)
    whole = [pl.BlockSpec(e.shape, lambda k: (0, 0)) for e in extra]
    outs = [jax.ShapeDtypeStruct((rows, columns), jnp.float32)]
    if normed:
        outs.append(jax.ShapeDtypeStruct((rows, wide), jnp.float32))
    return pl.pallas_call(
        functools.partial(project_kernel, normed, lanes),
        grid=(steps,),
        out_shape=outs,
        in_specs=[pl.BlockSpec((rows, tile), lambda k: (0, k))]
        + [
            pl.BlockSpec((thin, columns), lambda k, lane=lane: (k * lanes + lane, group))
            for lane in range(lanes)
        ]
        * len(weights)
        + whole,
        out_specs=[pl.BlockSpec(o.shape, lambda k: (0, 0)) for o in outs],
        scratch_shapes=[pltpu.VMEM((rows, wide), jnp.float32)],
        compiler_params=pltpu.CompilerParams(vmem_limit_bytes=56 * MIB),
        cost_estimate=SOON
        if normed
        else pl.CostEstimate(
            flops=24 * rows * width * wide, bytes_accessed=1024, transcendentals=0
        ),
    )(source, *[w for w in weights for _ in range(lanes)], *extra)


def settle_kernel(mine_ref, one_ref, far_ref, keep_ref, raw_ref, gain_ref, cos_ref, sin_ref, out_ref):
    head = gain_ref.shape[1]
    total = mine_ref[...] + one_ref[...] * keep_ref[...] + far_ref[...]
    out_ref[:, :head] = norm_rotate_back(
        total[:, :head], raw_ref[...], gain_ref[...], cos_ref[...], sin_ref[...]
    )
    out_ref[:, head:] = total[:, head:]


def settle(mine, one, far, keep, raw, gain, cosine, sine):
    return pl.pallas_call(
        settle_kernel,
        out_shape=jax.ShapeDtypeStruct(mine.shape, jnp.float32),
        compiler_params=pltpu.CompilerParams(vmem_limit_bytes=16 * MIB),
        cost_estimate=SOON,
    )(mine, one, far, keep, raw, gain, cosine, sine)


def flip_kernel(source_ref, out_ref):
    out_ref[...] = source_ref[...].T


def flip(source):
    rows, width = source.shape
    tile = width // 5
    return pl.pallas_call(
        flip_kernel,
        grid=(5,),
        out_shape=jax.ShapeDtypeStruct((width, rows), jnp.float32),
        in_specs=[pl.BlockSpec((rows, tile), lambda k: (0, k))],
        out_specs=pl.BlockSpec((tile, rows), lambda k: (k, 0)),
        compiler_params=pltpu.CompilerParams(vmem_limit_bytes=16 * MIB),
        cost_estimate=SOON,
    )(source)


def turn_kernel(place_ref, others_ref, own_ref, high_ref, low_ref):
    step = pl.program_id(0)

    @pl.when(step < CHAIN - 1)
    def _():
        high_ref[0], low_ref[0] = halves(others_ref[0])

    @pl.when(step == CHAIN - 1)
    def _():
        high_ref[0], low_ref[0] = halves(own_ref[...])


def turn(place, others, own):
    slab, rows = own.shape
    half = jax.ShapeDtypeStruct((CHAIN, slab, rows), jnp.bfloat16)
    out_spec = pl.BlockSpec((1, slab, rows), lambda i, p: ((p[0] + 1 + i) % CHAIN, 0, 0))
    return pl.pallas_call(
        turn_kernel,
        grid_spec=pltpu.PrefetchScalarGridSpec(
            num_scalar_prefetch=1,
            grid=(CHAIN,),
            in_specs=[
                pl.BlockSpec((1, slab, rows), lambda i, p: (jnp.minimum(i, CHAIN - 2), 0, 0)),
                pl.BlockSpec((slab, rows), lambda i, p: (0, 0)),
            ],
            out_specs=[out_spec, out_spec],
        ),
        out_shape=[half, half],
        compiler_params=pltpu.CompilerParams(vmem_limit_bytes=24 * MIB),
        cost_estimate=SOON,
    )(place, others, own)


def product_kernel(start, place_ref, high_ref, low_ref, *refs):
    blocks, out_ref = refs[:-1], refs[-1]
    total = None
    for hop in range(CHAIN):
        slot = lax.rem(place_ref[0] + (CHAIN - hop), CHAIN)
        block = blocks[hop]
        if block.shape[1] == out_ref.shape[1]:
            block = block[...]
        else:
            block = block[:, start : start + out_ref.shape[1]]
        term = three((high_ref[slot], low_ref[slot]), halves(block), 1, 0)
        total = term if total is None else total + term
    out_ref[...] = total


def product(place, step, turned, blocks, pair, span):
    high, low = turned
    part = high.shape[1] // pair
    rows = high.shape[2]
    columns = span[1] or blocks[0].shape[1]
    spec = pl.BlockSpec((CHAIN, part, rows), lambda i, p: (0, (p[1] + step) % pair, 0))
    return pl.pallas_call(
        functools.partial(product_kernel, span[0]),
        grid_spec=pltpu.PrefetchScalarGridSpec(
            num_scalar_prefetch=1,
            grid=(1,),
            in_specs=[spec, spec] + [pl.BlockSpec(b.shape, lambda i, p: (0, 0)) for b in blocks],
            out_specs=pl.BlockSpec((part, columns), lambda i, p: (0, 0)),
        ),
        out_shape=jax.ShapeDtypeStruct((part, columns), jnp.float32),
        compiler_params=pltpu.CompilerParams(vmem_limit_bytes=28 * MIB),
        cost_estimate=SOON,
    )(place, high, low, *blocks)


def strip_kernel(pieces, strips_ref, *refs):
    weight_refs, left_refs = refs[: len(pieces)], refs[len(pieces) : -1]
    total = None
    left_at = 0
    for ref, (count, start, wide) in zip(weight_refs, pieces):
        for group in range(count):
            left = left_refs[left_at + group][:, start : start + wide]
            right = ref[:, group * wide : (group + 1) * wide]
            term = three(halves(right), halves(left), 1, 1)
            total = term if total is None else total + term
        left_at = left_at if start == 0 and len(pieces) > 1 else left_at + count
    refs[-1][0] = total


def input_strips(strips, strip, weights, lefts, pieces):
    count = strips.shape[0]
    rows = lefts[0].shape[0]
    wide = sum(w.shape[1] for w in weights)
    whole = [pl.BlockSpec(d.shape, lambda i, p: (0, 0)) for d in lefts]
    return pl.pallas_call(
        functools.partial(strip_kernel, pieces),
        grid_spec=pltpu.PrefetchScalarGridSpec(
            num_scalar_prefetch=1,
            grid=(count,),
            in_specs=[pl.BlockSpec((strip, w.shape[1]), lambda i, p: (p[i], 0)) for w in weights]
            + whole,
            out_specs=pl.BlockSpec((1, strip, rows), lambda i, p: (i, 0, 0)),
        ),
        out_shape=jax.ShapeDtypeStruct((count, strip, rows), jnp.float32),
        compiler_params=pltpu.CompilerParams(vmem_limit_bytes=56 * MIB),
        cost_estimate=SOON,
    )(strips, *weights, *lefts)


def local(hidden_in, query_proj, key_proj, value_proj, query_gain, key_gain, segment_ids, grad_out):
    rows_dev, width = hidden_in.shape
    head = query_gain.shape[0]
    kv_local = key_proj.shape[1] // head
    per_kv = query_proj.shape[1] // key_proj.shape[1]
    pair = lax.axis_size("y")
    count = CHAIN * pair
    members = lax.axis_size("tensor")
    member = lax.axis_index("tensor")
    along = lax.axis_index("z")
    across = lax.axis_index("y")
    seq_index = along * pair + across
    reach = (WINDOW - 1) // rows_dev + 1
    span = (reach + 1) * rows_dev
    slab = width // CHAIN
    part = width // count
    piece = slab // members
    groups = range(kv_local)
    short = pair == 2 and reach == 4

    def z_shift(block, step):
        route = [(i, i + step) for i in range(CHAIN) if 0 <= i + step < CHAIN]
        return lax.ppermute(block, "z", route)

    def z_ring(block, step):
        return lax.ppermute(block, "z", [(i, (i + step) % CHAIN) for i in range(CHAIN)])

    def y_ring(block, step):
        return lax.ppermute(block, "y", [(i, (i + step) % pair) for i in range(pair)])

    def shifted(block, distance):
        route = [(i - distance, i) for i in range(count) if 0 <= i - distance < count]
        return lax.ppermute(block, ("z", "y"), route)

    first_row = seq_index * rows_dev
    positions = first_row + jnp.arange(rows_dev, dtype=jnp.int32)
    cosine, sine = rope_tables(positions, head)
    seg_pad = jnp.concatenate([jnp.full((reach * rows_dev,), -1, jnp.int32), segment_ids])
    key_seg = lax.dynamic_slice_in_dim(seg_pad, first_row, span, 0)[:, None]
    query_seg = lax.dynamic_slice_in_dim(segment_ids, first_row, rows_dev, 0)[None, :]

    def q_columns(array, group):
        return array[:, group * per_kv * head : (group + 1) * per_kv * head]

    key_raw, own, two, queries = [], [], [], []
    tables = (key_gain[None, :], cosine, sine)
    for group in groups:
        source = after(hidden_in, own[-1]) if own else hidden_in
        raw, packed = project(source, (key_proj, value_proj), group, head, tables)
        key_raw.append(raw)
        own.append(packed)
        if short:
            two.append(z_shift(own[group], 1))

    def neighbour(group, *earlier):
        block = jnp.where(across == 0, own[group], two[group])
        return y_ring(after(block, *earlier) if earlier else block, 1)

    def farthest(group, four, *earlier):
        back = after(two[group], *earlier)
        return y_ring(jnp.where(across == 0, back, four), 1)

    for group in groups:
        source = after(hidden_in, *own, *queries)
        queries.append(project(source, (query_proj,), group, per_kv * head, ())[0])

    hidden_rows = flip(after(hidden_in, *queries))
    windows, fours, ones = [], [], []
    if short:
        for group in groups:
            ones.append(neighbour(group))
        for group in groups:
            fours.append(z_shift(after(two[group], own[-1]), 1))
        for group in groups:
            three_back = farthest(group, fours[group], *ones, *fours, hidden_rows)
            windows.append([fours[group], three_back, two[group], ones[group], own[group]])
    else:
        for group in groups:
            windows.append([shifted(own[group], d) for d in range(reach, 0, -1)] + [own[group]])
    pieces = []
    for step in range(CHAIN - 1, 0, -1):
        target = (along + step) % CHAIN
        start = target * slab + member * piece
        pieces.append(z_ring(lax.dynamic_slice_in_dim(hidden_rows, start, piece, 0), step))
    chips = members // CORES
    chip, core = member // CORES, member % CORES

    def to_core(block):
        return lax.ppermute(block, "tensor", [(i, i ^ 1) for i in range(members)])

    def to_chip(block, step):
        route = [(i, (i + step * CORES) % members) for i in range(members)]
        return lax.ppermute(block, "tensor", route)

    def in_order(blocks, index, axis):
        size = blocks[0].shape[axis]
        both = jnp.concatenate(blocks + blocks[:-1], axis=axis)
        start = (len(blocks) - 1 - index) * size
        return lax.dynamic_slice_in_dim(both, start, len(blocks) * size, axis)

    mine = jnp.stack(pieces)
    chip_rows = in_order([to_core(mine), mine], core, 1)
    arrivals = [to_chip(chip_rows, step) for step in range(chips - 1, 0, -1)]
    others = in_order(arrivals + [chip_rows], chip, 1)
    own_slab = lax.dynamic_slice_in_dim(hidden_rows, along * slab, slab, 0)
    place = jnp.stack([along, across]).astype(jnp.int32)
    turned = turn(place, others, own_slab)

    attended, d_query, parts = [], [], []
    for group in groups:
        ready = attended or pieces
        out, d_q, d_kv = attention(
            after(queries[group], *ready),
            q_columns(grad_out, group),
            query_gain[None, :],
            cosine,
            sine,
            query_seg,
            key_seg,
            windows[group],
            per_kv,
        )
        attended.append(out)
        d_query.append(d_q)
        parts.append(d_kv)

    strip = width // members
    turns = [(chip + step) % chips for step in range(chips)]
    theirs_at = jnp.stack([c * CORES + 1 - core for c in turns]).astype(jnp.int32)
    mine_at = jnp.stack([c * CORES + core for c in turns]).astype(jnp.int32)

    def query_strips(which):
        pieces = ((kv_local, 0, per_kv * head),)
        return input_strips(which, strip, (query_proj,), d_query, pieces)

    def kv_strips(which):
        pieces = ((kv_local, 0, head), (kv_local, head, head))
        return input_strips(which, strip, (key_proj, value_proj), d_kv, pieces)

    def product_of(ring, step, span=(0, 0)):
        return product(place, step, turned, ring, pair, span)

    def terms(ring, span=(0, 0)):
        return [product_of(ring, step, span) for step in range(pair - 1, 0, -1)]

    def exchange(sent):
        return [y_ring(term, pair - 1 - i) for i, term in enumerate(sent)]

    sent = []

    def follow(block, send, extra):
        earlier = sent[-2:-1] + list(extra)
        sent.append(send(after(block, *earlier) if earlier else block))
        return sent[-1]

    keep = jnp.where(across == 0, 1.0, 0.0).reshape(1, 1).astype(jnp.float32)
    q_rings = [[d] for d in d_query]
    d_kv, k_rings, held = [], [], []

    def q_hop(group, *extra):
        q_rings[group].append(follow(q_rings[group][-1], lambda b: z_ring(b, 1), extra))

    def k_hop(group, *extra):
        k_rings[group].append(follow(k_rings[group][-1], lambda b: z_ring(b, 1), extra))

    def far_return(group, *extra):
        four, three_back, two_back, one, mine = parts[group]
        from_three = y_ring(three_back, 1)
        from_one = y_ring(one, 1)
        block = four + jnp.where(across == 0, 0.0, from_three)
        got = follow(block, lambda b: z_shift(b, -1), extra)
        held.append((two_back + jnp.where(across == 0, from_three, from_one) + got, from_one))

    def near_return(group, *extra):
        block, from_one = held[group]
        far = follow(block, lambda b: z_shift(b, -1), extra)
        mine = parts[group][-1]
        d_kv.append(settle(mine, from_one, far, keep, key_raw[group], *tables))
        k_rings.append([d_kv[group]])

    if short and kv_local == 2:
        q_hop(0)
        far_return(0, q_rings[0][1], *attended)
        q_hop(0)
        near_return(0, q_rings[0][2])
        q_hop(1)
        theirs_q = query_strips(theirs_at)
        far_return(1, theirs_q, q_rings[1][1])
        q_hop(0)
        mine_q = query_strips(mine_at)
        q_hop(1)
        near_return(1, mine_q, q_rings[0][3])
        k_hop(0)
        q_terms = [terms(q_rings[0])]
        q_hop(1, *q_terms[0])
        k_hop(0)
        theirs = theirs_q + kv_strips(theirs_at)
        q_sent = [exchange(q_terms[0])]
        k_hop(1, theirs)
        q_terms.append(terms(q_rings[1]))
        k_hop(0, *q_terms[1])
        sums = mine_q + kv_strips(mine_at)
        k_hop(1, sums, *q_sent[0])
        k_terms = [terms(k_rings[0])]
        q_sent.append(exchange(q_terms[1]))
        last = after(k_rings[1][-1], sent[-2], *k_terms[0], *q_sent[1])
        tails = [z_ring(last[:, head:], 1), z_ring(last[:, :head], 1)]
        tail_rings = [k_rings[1] + [tail] for tail in tails]
        tail_spans = [(head, head), (0, head)]
    else:
        for group in groups:
            mine = parts[group][reach]
            total = jnp.zeros_like(mine)
            for distance in range(1, reach + 1):
                total = total + shifted(parts[group][reach - distance], -distance)
            d_kv.append(settle(mine, mine, total, 0.0 * keep, key_raw[group], *tables))
            k_rings.append([d_kv[group]])
            for _ in range(CHAIN - 1):
                q_hop(group)
            for _ in range(CHAIN - 1):
                k_hop(group)
        theirs = query_strips(theirs_at) + kv_strips(theirs_at)
        sums = query_strips(mine_at) + kv_strips(mine_at)
        q_sent = [exchange(terms(ring)) for ring in q_rings]
        k_terms = [terms(ring) for ring in k_rings[:-1]]
        tail_rings, tail_spans = [k_rings[-1]], [(0, 2 * head)]

    sums = sums + to_core(theirs)
    grad_input = sums[0]
    for step in range(1, chips):
        grad_input = grad_input + to_chip(sums[step], step)

    def finish(ring, arrived, span=(0, 0)):
        total = product_of(ring, 0, span)
        for term in arrived:
            total = total + term
        return total

    grad_query = [finish(ring, arrived) for ring, arrived in zip(q_rings, q_sent)]
    tail_sent = [exchange(terms(ring, span)) for ring, span in zip(tail_rings, tail_spans)]
    grad_kv = [finish(ring, exchange(term)) for ring, term in zip(k_rings, k_terms)]
    ends = [finish(*each) for each in zip(tail_rings, tail_sent, tail_spans)]
    grad_kv.append(jnp.concatenate(ends[::-1], axis=1))

    return (
        jnp.concatenate(attended, axis=1),
        grad_input.T,
        jnp.concatenate(grad_query, axis=1),
        jnp.concatenate([g[:, :head] for g in grad_kv], axis=1),
        jnp.concatenate([g[:, head:] for g in grad_kv], axis=1),
    )


def solution(mesh):
    seq, members = mesh.devices.shape
    split = Mesh(mesh.devices.reshape(CHAIN, seq // CHAIN, members), ("z", "y", "tensor"))
    tokens = ("z", "y")
    return jax.shard_map(
        local,
        mesh=split,
        in_specs=(
            P(tokens, None),
            P(None, "tensor"),
            P(None, "tensor"),
            P(None, "tensor"),
            P(),
            P(),
            P(),
            P(tokens, "tensor"),
        ),
        out_specs=(
            P(tokens, "tensor"),
            P(tokens, "tensor"),
            P(tokens, "tensor"),
            P(tokens, "tensor"),
            P(tokens, "tensor"),
        ),
        check_vma=False,
    )
```

```python
import functools

import jax
import jax.numpy as jnp
from jax import lax
from jax.experimental import pallas as pl
from jax.experimental.pallas import tpu as pltpu
from jax.sharding import Mesh, PartitionSpec as P

WINDOW = 1024
CHAIN = 4
CORES = 2

MIB = 1024 * 1024
SOON = pl.CostEstimate(flops=1024, bytes_accessed=1024, transcendentals=0)
epsilon = 1e-06


def after(block, *earlier):
    return lax.optimization_barrier((block, earlier))[0]


def rope_tables(positions, head_width):
    middle = head_width // 2
    exponent = 2.0 * jnp.arange(middle).astype(jnp.float32) / head_width
    frequency = 10000.0 ** (-exponent)
    angles = positions.astype(jnp.float32)[:, None] * frequency[None, :]
    return jnp.cos(angles), jnp.sin(angles)


def inverse_rms(vector):
    return lax.rsqrt(jnp.mean(vector * vector, axis=-1, keepdims=True) + epsilon)


def norm_rotate(vector, scaling, cosine, sine):
    middle = vector.shape[-1] // 2
    normed = vector * inverse_rms(vector) * scaling
    low, high = normed[:, :middle], normed[:, middle:]
    return jnp.concatenate([low * cosine - high * sine, high * cosine + low * sine], axis=1)


def norm_rotate_back(grad, vector, scaling, cosine, sine):
    middle = vector.shape[-1] // 2
    low, high = grad[:, :middle], grad[:, middle:]
    d_normed = jnp.concatenate([low * cosine + high * sine, high * cosine - low * sine], axis=1)
    d_normed = d_normed * scaling
    inverse = inverse_rms(vector)
    unit = vector * inverse
    return inverse * (d_normed - unit * jnp.mean(d_normed * unit, axis=-1, keepdims=True))


def halves(array):
    high = array.astype(jnp.bfloat16)
    return high, (array - high.astype(jnp.float32)).astype(jnp.bfloat16)


def three(left, right, left_dim, right_dim):
    def once(a, b):
        return lax.dot_general(
            a, b, (((left_dim,), (right_dim,)), ((), ())), preferred_element_type=jnp.float32
        )

    return once(left[0], right[0]) + (once(left[0], right[1]) + once(left[1], right[0]))


def attention_kernel(blocks, per_kv, *refs):
    query_ref, grad_ref, gain_ref, cos_ref, sin_ref, seg_ref, key_seg_ref = refs[:7]
    kv_refs = refs[7 : 7 + blocks]
    out_ref, d_query_ref = refs[7 + blocks : 9 + blocks]
    d_kv_refs = refs[9 + blocks : 9 + 2 * blocks]
    weight_ref, d_share_ref, share_high, share_low, score_high, score_low = refs[9 + 2 * blocks :]
    rows = query_ref.shape[0]
    head = gain_ref.shape[1]
    factor = head ** (-0.5)
    gain, cosine, sine = gain_ref[...], cos_ref[...], sin_ref[...]
    raw = [query_ref[:, h * head : (h + 1) * head] for h in range(per_kv)]
    q_rot = halves(
        jnp.concatenate([norm_rotate(u, gain, cosine, sine) for u in raw], axis=0)
    )
    grad = halves(
        jnp.concatenate([grad_ref[:, h * head : (h + 1) * head] for h in range(per_kv)], axis=0)
    )
    total = jnp.zeros((1, per_kv * rows), jnp.float32)
    mixed = jnp.zeros((1, per_kv * rows), jnp.float32)
    seg = jnp.concatenate([seg_ref[...]] * per_kv, axis=1)
    turned_keys, turned_values = [], []
    lane = lax.broadcasted_iota(jnp.int32, (rows, rows), 1)
    lane = jnp.concatenate([lane] * per_kv, axis=1)
    row = lax.broadcasted_iota(jnp.int32, (rows, per_kv * rows), 0)
    for j in range(blocks):
        place = slice(j * rows, (j + 1) * rows)
        key, value = kv_refs[j][:, :head], kv_refs[j][:, head:]
        turned_keys.append(key.T)
        turned_values.append(value.T)
        scores = three(halves(key), q_rot, 1, 1) * factor
        distance = (blocks - 1 - j) * rows + lane - row
        allowed = (distance >= 0) & (distance < WINDOW) & (key_seg_ref[place, :] == seg)
        weights = jnp.where(allowed, jnp.exp(scores), 0.0)
        d_shares = three(halves(value), grad, 1, 1)
        weight_ref[place, :] = weights
        d_share_ref[place, :] = d_shares
        total = total + jnp.sum(weights, axis=0, keepdims=True)
        mixed = mixed + jnp.sum(weights * d_shares, axis=0, keepdims=True)
    scale = 1.0 / total
    delta = mixed * scale
    for j in range(blocks):
        place = slice(j * rows, (j + 1) * rows)
        shares = weight_ref[place, :] * scale
        d_scores = shares * (d_share_ref[place, :] - delta) * factor
        share_pair = halves(shares)
        score_pair = halves(d_scores)
        share_high[place, :], share_low[place, :] = share_pair
        score_high[place, :], score_low[place, :] = score_pair
        d_kv_refs[j][:, :head] = three(score_pair, q_rot, 1, 0)
        d_kv_refs[j][:, head:] = three(share_pair, grad, 1, 0)
    turned_out = three(
        halves(jnp.concatenate(turned_values, axis=1)), (share_high[...], share_low[...]), 1, 0
    )
    turned_query = three(
        halves(jnp.concatenate(turned_keys, axis=1)), (score_high[...], score_low[...]), 1, 0
    )
    for h in range(per_kv):
        place = slice(h * rows, (h + 1) * rows)
        columns = slice(h * head, (h + 1) * head)
        out_ref[:, columns] = turned_out[:, place].T
        d_query_ref[:, columns] = norm_rotate_back(
            turned_query[:, place].T, raw[h], gain, cosine, sine
        )


def attention(queries, grads, gain, cosine, sine, query_seg, key_seg, window, per_kv):
    rows, width = queries.shape
    blocks = len(window)
    span = blocks * rows
    flat = jax.ShapeDtypeStruct((rows, width), jnp.float32)
    part = jax.ShapeDtypeStruct(window[0].shape, jnp.float32)
    wide = per_kv * rows
    results = pl.pallas_call(
        functools.partial(attention_kernel, blocks, per_kv),
        out_shape=[flat, flat] + [part] * blocks,
        scratch_shapes=[
            pltpu.VMEM((span, wide), jnp.float32),
            pltpu.VMEM((span, wide), jnp.float32),
            pltpu.VMEM((span, wide), jnp.bfloat16),
            pltpu.VMEM((span, wide), jnp.bfloat16),
            pltpu.VMEM((span, wide), jnp.bfloat16),
            pltpu.VMEM((span, wide), jnp.bfloat16),
        ],
        compiler_params=pltpu.CompilerParams(vmem_limit_bytes=40 * 1024 * 1024),
        cost_estimate=SOON,
    )(queries, grads, gain, cosine, sine, query_seg, key_seg, *window)
    return results[0], results[1], results[2:]


def project_kernel(normed, lanes, source_ref, *refs):
    if normed:
        weight_refs, rest = refs[: 2 * lanes], refs[2 * lanes :]
        gain_ref, cos_ref, sin_ref, raw_ref, packed_ref, total_ref = rest
    else:
        weight_refs, (raw_ref, total_ref) = refs[:lanes], refs[lanes:]
    step = pl.program_id(0)
    stacked = [
        jnp.concatenate([ref[...] for ref in weight_refs[start : start + lanes]], axis=0)
        for start in range(0, len(weight_refs), lanes)
    ]
    weight = stacked[0] if len(stacked) == 1 else jnp.concatenate(stacked, axis=1)
    product = three(halves(source_ref[...]), halves(weight), 1, 0)

    @pl.when(step == 0)
    def _():
        total_ref[...] = product

    @pl.when(step > 0)
    def _():
        total_ref[...] += product

    @pl.when(step == pl.num_programs(0) - 1)
    def _():
        if normed:
            head = gain_ref.shape[1]
            raw = total_ref[:, :head]
            raw_ref[...] = raw
            packed_ref[:, :head] = norm_rotate(raw, gain_ref[...], cos_ref[...], sin_ref[...])
            packed_ref[:, head:] = total_ref[:, head:]
        else:
            raw_ref[...] = total_ref[...]


def project(source, weights, group, columns, extra):
    rows, width = source.shape
    steps, lanes = 5, 3
    tile = width // steps
    thin = tile // lanes
    normed = len(weights) > 1
    wide = columns * len(weights)
    whole = [pl.BlockSpec(e.shape, lambda k: (0, 0)) for e in extra]
    outs = [jax.ShapeDtypeStruct((rows, columns), jnp.float32)]
    if normed:
        outs.append(jax.ShapeDtypeStruct((rows, wide), jnp.float32))
    return pl.pallas_call(
        functools.partial(project_kernel, normed, lanes),
        grid=(steps,),
        out_shape=outs,
        in_specs=[pl.BlockSpec((rows, tile), lambda k: (0, k))]
        + [
            pl.BlockSpec((thin, columns), lambda k, lane=lane: (k * lanes + lane, group))
            for lane in range(lanes)
        ]
        * len(weights)
        + whole,
        out_specs=[pl.BlockSpec(o.shape, lambda k: (0, 0)) for o in outs],
        scratch_shapes=[pltpu.VMEM((rows, wide), jnp.float32)],
        compiler_params=pltpu.CompilerParams(vmem_limit_bytes=56 * MIB),
        cost_estimate=SOON
        if normed
        else pl.CostEstimate(
            flops=24 * rows * width * wide, bytes_accessed=1024, transcendentals=0
        ),
    )(source, *[w for w in weights for _ in range(lanes)], *extra)


def settle_kernel(mine_ref, one_ref, far_ref, keep_ref, raw_ref, gain_ref, cos_ref, sin_ref, out_ref):
    head = gain_ref.shape[1]
    total = mine_ref[...] + one_ref[...] * keep_ref[...] + far_ref[...]
    out_ref[:, :head] = norm_rotate_back(
        total[:, :head], raw_ref[...], gain_ref[...], cos_ref[...], sin_ref[...]
    )
    out_ref[:, head:] = total[:, head:]


def settle(mine, one, far, keep, raw, gain, cosine, sine):
    return pl.pallas_call(
        settle_kernel,
        out_shape=jax.ShapeDtypeStruct(mine.shape, jnp.float32),
        compiler_params=pltpu.CompilerParams(vmem_limit_bytes=16 * MIB),
        cost_estimate=SOON,
    )(mine, one, far, keep, raw, gain, cosine, sine)


def flip_kernel(source_ref, out_ref):
    out_ref[...] = source_ref[...].T


def flip(source):
    rows, width = source.shape
    tile = width // 5
    return pl.pallas_call(
        flip_kernel,
        grid=(5,),
        out_shape=jax.ShapeDtypeStruct((width, rows), jnp.float32),
        in_specs=[pl.BlockSpec((rows, tile), lambda k: (0, k))],
        out_specs=pl.BlockSpec((tile, rows), lambda k: (k, 0)),
        compiler_params=pltpu.CompilerParams(vmem_limit_bytes=16 * MIB),
        cost_estimate=SOON,
    )(source)


def turn_kernel(place_ref, others_ref, own_ref, high_ref, low_ref):
    step = pl.program_id(0)

    @pl.when(step < CHAIN - 1)
    def _():
        high_ref[0], low_ref[0] = halves(others_ref[0])

    @pl.when(step == CHAIN - 1)
    def _():
        high_ref[0], low_ref[0] = halves(own_ref[...])


def turn(place, others, own):
    slab, rows = own.shape
    half = jax.ShapeDtypeStruct((CHAIN, slab, rows), jnp.bfloat16)
    out_spec = pl.BlockSpec((1, slab, rows), lambda i, p: ((p[0] + 1 + i) % CHAIN, 0, 0))
    return pl.pallas_call(
        turn_kernel,
        grid_spec=pltpu.PrefetchScalarGridSpec(
            num_scalar_prefetch=1,
            grid=(CHAIN,),
            in_specs=[
                pl.BlockSpec((1, slab, rows), lambda i, p: (jnp.minimum(i, CHAIN - 2), 0, 0)),
                pl.BlockSpec((slab, rows), lambda i, p: (0, 0)),
            ],
            out_specs=[out_spec, out_spec],
        ),
        out_shape=[half, half],
        compiler_params=pltpu.CompilerParams(vmem_limit_bytes=24 * MIB),
        cost_estimate=SOON,
    )(place, others, own)


def product_kernel(start, place_ref, high_ref, low_ref, *refs):
    blocks, out_ref = refs[:-1], refs[-1]
    total = None
    for hop in range(CHAIN):
        slot = lax.rem(place_ref[0] + (CHAIN - hop), CHAIN)
        block = blocks[hop]
        if block.shape[1] == out_ref.shape[1]:
            block = block[...]
        else:
            block = block[:, start : start + out_ref.shape[1]]
        term = three((high_ref[slot], low_ref[slot]), halves(block), 1, 0)
        total = term if total is None else total + term
    out_ref[...] = total


def product(place, step, turned, blocks, pair, span):
    high, low = turned
    part = high.shape[1] // pair
    rows = high.shape[2]
    columns = span[1] or blocks[0].shape[1]
    spec = pl.BlockSpec((CHAIN, part, rows), lambda i, p: (0, (p[1] + step) % pair, 0))
    return pl.pallas_call(
        functools.partial(product_kernel, span[0]),
        grid_spec=pltpu.PrefetchScalarGridSpec(
            num_scalar_prefetch=1,
            grid=(1,),
            in_specs=[spec, spec] + [pl.BlockSpec(b.shape, lambda i, p: (0, 0)) for b in blocks],
            out_specs=pl.BlockSpec((part, columns), lambda i, p: (0, 0)),
        ),
        out_shape=jax.ShapeDtypeStruct((part, columns), jnp.float32),
        compiler_params=pltpu.CompilerParams(vmem_limit_bytes=28 * MIB),
        cost_estimate=SOON,
    )(place, high, low, *blocks)


def strip_kernel(pieces, added, strips_ref, *refs):
    weight_refs, left_refs = refs[: len(pieces)], refs[len(pieces) : -1]
    total = left_refs[-1][0] if added else None
    left_at = 0
    for ref, (count, start, wide) in zip(weight_refs, pieces):
        for group in range(count):
            left = left_refs[left_at + group][:, start : start + wide]
            right = ref[:, group * wide : (group + 1) * wide]
            term = three(halves(right), halves(left), 1, 1)
            total = term if total is None else total + term
        left_at = left_at if start == 0 and len(pieces) > 1 else left_at + count
    refs[-1][0] = total


def input_strips(strips, strip, weights, lefts, pieces, partial):
    count = strips.shape[0]
    rows = lefts[0].shape[0]
    wide = sum(w.shape[1] for w in weights)
    whole = [pl.BlockSpec(d.shape, lambda i, p: (0, 0)) for d in lefts]
    out_spec = pl.BlockSpec((1, strip, rows), lambda i, p: (i, 0, 0))
    return pl.pallas_call(
        functools.partial(strip_kernel, pieces, partial is not None),
        grid_spec=pltpu.PrefetchScalarGridSpec(
            num_scalar_prefetch=1,
            grid=(count,),
            in_specs=[pl.BlockSpec((strip, w.shape[1]), lambda i, p: (p[i], 0)) for w in weights]
            + whole
            + ([] if partial is None else [out_spec]),
            out_specs=out_spec,
        ),
        out_shape=jax.ShapeDtypeStruct((count, strip, rows), jnp.float32),
        compiler_params=pltpu.CompilerParams(vmem_limit_bytes=56 * MIB),
        cost_estimate=SOON,
    )(strips, *weights, *lefts, *([] if partial is None else [partial]))


def local(hidden_in, query_proj, key_proj, value_proj, query_gain, key_gain, segment_ids, grad_out):
    rows_dev, width = hidden_in.shape
    head = query_gain.shape[0]
    kv_local = key_proj.shape[1] // head
    per_kv = query_proj.shape[1] // key_proj.shape[1]
    pair = lax.axis_size("y")
    count = CHAIN * pair
    members = lax.axis_size("tensor")
    member = lax.axis_index("tensor")
    along = lax.axis_index("z")
    across = lax.axis_index("y")
    seq_index = along * pair + across
    reach = (WINDOW - 1) // rows_dev + 1
    span = (reach + 1) * rows_dev
    slab = width // CHAIN
    part = width // count
    piece = slab // members
    groups = range(kv_local)
    short = pair == 2 and reach == 4

    def z_shift(block, step):
        route = [(i, i + step) for i in range(CHAIN) if 0 <= i + step < CHAIN]
        return lax.ppermute(block, "z", route)

    def z_ring(block, step):
        return lax.ppermute(block, "z", [(i, (i + step) % CHAIN) for i in range(CHAIN)])

    def y_ring(block, step):
        return lax.ppermute(block, "y", [(i, (i + step) % pair) for i in range(pair)])

    def shifted(block, distance):
        route = [(i - distance, i) for i in range(count) if 0 <= i - distance < count]
        return lax.ppermute(block, ("z", "y"), route)

    first_row = seq_index * rows_dev
    positions = first_row + jnp.arange(rows_dev, dtype=jnp.int32)
    cosine, sine = rope_tables(positions, head)
    seg_pad = jnp.concatenate([jnp.full((reach * rows_dev,), -1, jnp.int32), segment_ids])
    key_seg = lax.dynamic_slice_in_dim(seg_pad, first_row, span, 0)[:, None]
    query_seg = lax.dynamic_slice_in_dim(segment_ids, first_row, rows_dev, 0)[None, :]

    def q_columns(array, group):
        return array[:, group * per_kv * head : (group + 1) * per_kv * head]

    key_raw, own, two, queries = [], [], [], []
    tables = (key_gain[None, :], cosine, sine)
    for group in groups:
        source = after(hidden_in, own[-1]) if own else hidden_in
        raw, packed = project(source, (key_proj, value_proj), group, head, tables)
        key_raw.append(raw)
        own.append(packed)
        if short:
            two.append(z_shift(own[group], 1))

    def neighbour(group, *earlier):
        block = jnp.where(across == 0, own[group], two[group])
        return y_ring(after(block, *earlier) if earlier else block, 1)

    def farthest(group, four, *earlier):
        back = after(two[group], *earlier)
        return y_ring(jnp.where(across == 0, back, four), 1)

    for group in groups:
        source = after(hidden_in, *own, *queries)
        queries.append(project(source, (query_proj,), group, per_kv * head, ())[0])

    hidden_rows = flip(after(hidden_in, *queries))
    windows, fours, ones = [], [], []
    if short:
        for group in groups:
            ones.append(neighbour(group))
        for group in groups:
            fours.append(z_shift(after(two[group], own[-1]), 1))
        for group in groups:
            three_back = farthest(group, fours[group], *ones, *fours[:group], hidden_rows)
            windows.append([fours[group], three_back, two[group], ones[group], own[group]])
    else:
        for group in groups:
            windows.append([shifted(own[group], d) for d in range(reach, 0, -1)] + [own[group]])
    shared = after(hidden_rows, *fours) if fours else hidden_rows
    pieces = []
    for step in range(CHAIN - 1, 0, -1):
        target = (along + step) % CHAIN
        start = target * slab + member * piece
        pieces.append(z_ring(lax.dynamic_slice_in_dim(shared, start, piece, 0), step))
    chips = members // CORES
    chip, core = member // CORES, member % CORES

    def to_core(block):
        return lax.ppermute(block, "tensor", [(i, i ^ 1) for i in range(members)])

    def to_chip(block, step):
        route = [(i, (i + step * CORES) % members) for i in range(members)]
        return lax.ppermute(block, "tensor", route)

    def in_order(blocks, index, axis):
        size = blocks[0].shape[axis]
        both = jnp.concatenate(blocks + blocks[:-1], axis=axis)
        start = (len(blocks) - 1 - index) * size
        return lax.dynamic_slice_in_dim(both, start, len(blocks) * size, axis)

    mine = jnp.stack(pieces)
    chip_rows = in_order([to_core(mine), mine], core, 1)
    arrivals = [to_chip(chip_rows, step) for step in range(chips - 1, 0, -1)]
    others = in_order(arrivals + [chip_rows], chip, 1)
    own_slab = lax.dynamic_slice_in_dim(hidden_rows, along * slab, slab, 0)
    place = jnp.stack([along, across]).astype(jnp.int32)
    turned = turn(place, others, own_slab)

    attended, d_query, parts = [], [], []
    for group in groups:
        ready = attended or pieces
        out, d_q, d_kv = attention(
            after(queries[group], *ready),
            q_columns(grad_out, group),
            query_gain[None, :],
            cosine,
            sine,
            query_seg,
            key_seg,
            windows[group],
            per_kv,
        )
        attended.append(out)
        d_query.append(d_q)
        parts.append(d_kv)

    strip = width // members
    turns = [(chip + step) % chips for step in range(chips)]
    theirs_at = jnp.stack([c * CORES + 1 - core for c in turns]).astype(jnp.int32)
    mine_at = jnp.stack([c * CORES + core for c in turns]).astype(jnp.int32)

    def query_strips(which):
        pieces = ((kv_local, 0, per_kv * head),)
        return input_strips(which, strip, (query_proj,), d_query, pieces, None)

    def kv_strips(which, partial):
        pieces = ((kv_local, 0, head), (kv_local, head, head))
        return input_strips(which, strip, (key_proj, value_proj), d_kv, pieces, partial)

    def product_of(ring, step, span=(0, 0)):
        return product(place, step, turned, ring, pair, span)

    def terms(ring, span=(0, 0)):
        return [product_of(ring, step, span) for step in range(pair - 1, 0, -1)]

    def exchange(sent):
        return [y_ring(term, pair - 1 - i) for i, term in enumerate(sent)]

    sent = []

    def follow(block, send, extra):
        earlier = sent[-2:-1] + list(extra)
        sent.append(send(after(block, *earlier) if earlier else block))
        return sent[-1]

    keep = jnp.where(across == 0, 1.0, 0.0).reshape(1, 1).astype(jnp.float32)
    q_rings = [[d] for d in d_query]
    d_kv, k_rings, held = [], [], []

    def q_hop(group, *extra):
        q_rings[group].append(follow(q_rings[group][-1], lambda b: z_ring(b, 1), extra))

    def k_hop(group, *extra):
        k_rings[group].append(follow(k_rings[group][-1], lambda b: z_ring(b, 1), extra))

    def far_return(group, *extra):
        four, three_back, two_back, one, mine = parts[group]
        from_three = y_ring(three_back, 1)
        from_one = y_ring(one, 1)
        block = four + jnp.where(across == 0, 0.0, from_three)
        got = follow(block, lambda b: z_shift(b, -1), extra)
        held.append((two_back + jnp.where(across == 0, from_three, from_one) + got, from_one))

    def near_return(group, extra, before):
        block, from_one = held[group]
        far = follow(block, lambda b: z_shift(b, -1), extra)
        far = after(far, *before) if before else far
        mine = parts[group][-1]
        d_kv.append(settle(mine, from_one, far, keep, key_raw[group], *tables))
        k_rings.append([d_kv[group]])

    if short and kv_local == 2:
        q_hop(0)
        far_return(0, q_rings[0][1], *attended)
        q_hop(0)
        near_return(0, [q_rings[0][2]], [])
        q_hop(1)
        theirs_q = query_strips(theirs_at)
        far_return(1, theirs_q, q_rings[1][1])
        q_hop(0)
        mine_q = query_strips(mine_at)
        q_hop(1)
        k_hop(0)
        near_return(1, [mine_q, q_rings[0][3], q_rings[1][2]], [k_rings[0][1]])
        q_terms = [terms(q_rings[0])]
        q_hop(1, *q_terms[0])
        k_hop(0)
        theirs = kv_strips(theirs_at, theirs_q)
        q_sent = [exchange(q_terms[0])]
        k_hop(1)
        q_terms.append(terms(q_rings[1]))
        k_hop(0, *q_terms[1])
        sums = kv_strips(mine_at, mine_q)
        k_hop(1, theirs, *q_sent[0])
        k_terms = [terms(k_rings[0])]
        q_sent.append(exchange(q_terms[1]))
        last = after(k_rings[1][-1], sent[-2], sums, *k_terms[0], *q_sent[1])
        tails = [z_ring(last[:, head:], 1)]
        tails.append(z_ring(after(last[:, :head], tails[0]), 1))
        tail_rings = [k_rings[1] + [tail] for tail in tails]
        tail_spans = [(head, head), (0, head)]
    else:
        for group in groups:
            mine = parts[group][reach]
            total = jnp.zeros_like(mine)
            for distance in range(1, reach + 1):
                total = total + shifted(parts[group][reach - distance], -distance)
            d_kv.append(settle(mine, mine, total, 0.0 * keep, key_raw[group], *tables))
            k_rings.append([d_kv[group]])
            for _ in range(CHAIN - 1):
                q_hop(group)
            for _ in range(CHAIN - 1):
                k_hop(group)
        theirs = kv_strips(theirs_at, query_strips(theirs_at))
        sums = kv_strips(mine_at, query_strips(mine_at))
        q_sent = [exchange(terms(ring)) for ring in q_rings]
        k_terms = [terms(ring) for ring in k_rings[:-1]]
        tail_rings, tail_spans = [k_rings[-1]], [(0, 2 * head)]

    sums = sums + to_core(theirs)
    grad_input = sums[0]
    for step in range(1, chips):
        grad_input = grad_input + to_chip(sums[step], step)

    def finish(ring, arrived, span=(0, 0)):
        total = product_of(ring, 0, span)
        for term in arrived:
            total = total + term
        return total

    grad_query = [finish(ring, arrived) for ring, arrived in zip(q_rings, q_sent)]
    tail_sent = [exchange(terms(ring, span)) for ring, span in zip(tail_rings, tail_spans)]
    grad_kv = [finish(ring, exchange(term)) for ring, term in zip(k_rings, k_terms)]
    ends = [finish(*each) for each in zip(tail_rings, tail_sent, tail_spans)]
    grad_kv.append(jnp.concatenate(ends[::-1], axis=1))

    return (
        jnp.concatenate(attended, axis=1),
        grad_input.T,
        jnp.concatenate(grad_query, axis=1),
        jnp.concatenate([g[:, :head] for g in grad_kv], axis=1),
        jnp.concatenate([g[:, head:] for g in grad_kv], axis=1),
    )


def solution(mesh):
    seq, members = mesh.devices.shape
    split = Mesh(mesh.devices.reshape(CHAIN, seq // CHAIN, members), ("z", "y", "tensor"))
    tokens = ("z", "y")
    return jax.shard_map(
        local,
        mesh=split,
        in_specs=(
            P(tokens, None),
            P(None, "tensor"),
            P(None, "tensor"),
            P(None, "tensor"),
            P(),
            P(),
            P(),
            P(tokens, "tensor"),
        ),
        out_specs=(
            P(tokens, "tensor"),
            P(tokens, "tensor"),
            P(tokens, "tensor"),
            P(tokens, "tensor"),
            P(tokens, "tensor"),
        ),
        check_vma=False,
    )
```

```python
import functools

import jax
import jax.numpy as jnp
from jax import lax
from jax.experimental import pallas as pl
from jax.experimental.pallas import tpu as pltpu
from jax.sharding import Mesh, PartitionSpec as P

WINDOW = 1024
CHAIN = 4
CORES = 2

MIB = 1024 * 1024
SOON = pl.CostEstimate(flops=1024, bytes_accessed=1024, transcendentals=0)
epsilon = 1e-06


def after(block, *earlier):
    return lax.optimization_barrier((block, earlier))[0]


def rope_tables(positions, head_width):
    middle = head_width // 2
    exponent = 2.0 * jnp.arange(middle).astype(jnp.float32) / head_width
    frequency = 10000.0 ** (-exponent)
    angles = positions.astype(jnp.float32)[:, None] * frequency[None, :]
    return jnp.cos(angles), jnp.sin(angles)


def inverse_rms(vector):
    return lax.rsqrt(jnp.mean(vector * vector, axis=-1, keepdims=True) + epsilon)


def norm_rotate(vector, scaling, cosine, sine):
    middle = vector.shape[-1] // 2
    normed = vector * inverse_rms(vector) * scaling
    low, high = normed[:, :middle], normed[:, middle:]
    return jnp.concatenate([low * cosine - high * sine, high * cosine + low * sine], axis=1)


def norm_rotate_back(grad, vector, scaling, cosine, sine):
    middle = vector.shape[-1] // 2
    low, high = grad[:, :middle], grad[:, middle:]
    d_normed = jnp.concatenate([low * cosine + high * sine, high * cosine - low * sine], axis=1)
    d_normed = d_normed * scaling
    inverse = inverse_rms(vector)
    unit = vector * inverse
    return inverse * (d_normed - unit * jnp.mean(d_normed * unit, axis=-1, keepdims=True))


def halves(array):
    high = array.astype(jnp.bfloat16)
    return high, (array - high.astype(jnp.float32)).astype(jnp.bfloat16)


def three(left, right, left_dim, right_dim):
    def once(a, b):
        return lax.dot_general(
            a, b, (((left_dim,), (right_dim,)), ((), ())), preferred_element_type=jnp.float32
        )

    return once(left[0], right[0]) + (once(left[0], right[1]) + once(left[1], right[0]))


def attention_kernel(blocks, per_kv, *refs):
    query_ref, grad_ref, gain_ref, cos_ref, sin_ref, seg_ref, key_seg_ref = refs[:7]
    kv_refs = refs[7 : 7 + blocks]
    out_ref, d_query_ref = refs[7 + blocks : 9 + blocks]
    d_kv_refs = refs[9 + blocks : 9 + 2 * blocks]
    weight_ref, d_share_ref, share_high, share_low, score_high, score_low = refs[9 + 2 * blocks :]
    rows = query_ref.shape[0]
    head = gain_ref.shape[1]
    factor = head ** (-0.5)
    gain, cosine, sine = gain_ref[...], cos_ref[...], sin_ref[...]
    raw = [query_ref[:, h * head : (h + 1) * head] for h in range(per_kv)]
    q_rot = halves(
        jnp.concatenate([norm_rotate(u, gain, cosine, sine) for u in raw], axis=0)
    )
    grad = halves(
        jnp.concatenate([grad_ref[:, h * head : (h + 1) * head] for h in range(per_kv)], axis=0)
    )
    total = jnp.zeros((1, per_kv * rows), jnp.float32)
    mixed = jnp.zeros((1, per_kv * rows), jnp.float32)
    seg = jnp.concatenate([seg_ref[...]] * per_kv, axis=1)
    turned_keys, turned_values = [], []
    lane = lax.broadcasted_iota(jnp.int32, (rows, rows), 1)
    lane = jnp.concatenate([lane] * per_kv, axis=1)
    row = lax.broadcasted_iota(jnp.int32, (rows, per_kv * rows), 0)
    for j in range(blocks):
        place = slice(j * rows, (j + 1) * rows)
        key, value = kv_refs[j][:, :head], kv_refs[j][:, head:]
        turned_keys.append(key.T)
        turned_values.append(value.T)
        scores = three(halves(key), q_rot, 1, 1) * factor
        distance = (blocks - 1 - j) * rows + lane - row
        allowed = (distance >= 0) & (distance < WINDOW) & (key_seg_ref[place, :] == seg)
        weights = jnp.where(allowed, jnp.exp(scores), 0.0)
        d_shares = three(halves(value), grad, 1, 1)
        weight_ref[place, :] = weights
        d_share_ref[place, :] = d_shares
        total = total + jnp.sum(weights, axis=0, keepdims=True)
        mixed = mixed + jnp.sum(weights * d_shares, axis=0, keepdims=True)
    scale = 1.0 / total
    delta = mixed * scale
    for j in range(blocks):
        place = slice(j * rows, (j + 1) * rows)
        shares = weight_ref[place, :] * scale
        d_scores = shares * (d_share_ref[place, :] - delta) * factor
        share_pair = halves(shares)
        score_pair = halves(d_scores)
        share_high[place, :], share_low[place, :] = share_pair
        score_high[place, :], score_low[place, :] = score_pair
        d_kv_refs[j][:, :head] = three(score_pair, q_rot, 1, 0)
        d_kv_refs[j][:, head:] = three(share_pair, grad, 1, 0)
    turned_out = three(
        halves(jnp.concatenate(turned_values, axis=1)), (share_high[...], share_low[...]), 1, 0
    )
    turned_query = three(
        halves(jnp.concatenate(turned_keys, axis=1)), (score_high[...], score_low[...]), 1, 0
    )
    for h in range(per_kv):
        place = slice(h * rows, (h + 1) * rows)
        columns = slice(h * head, (h + 1) * head)
        out_ref[:, columns] = turned_out[:, place].T
        d_query_ref[:, columns] = norm_rotate_back(
            turned_query[:, place].T, raw[h], gain, cosine, sine
        )


def attention(queries, grads, gain, cosine, sine, query_seg, key_seg, window, per_kv):
    rows, width = queries.shape
    blocks = len(window)
    span = blocks * rows
    flat = jax.ShapeDtypeStruct((rows, width), jnp.float32)
    part = jax.ShapeDtypeStruct(window[0].shape, jnp.float32)
    wide = per_kv * rows
    results = pl.pallas_call(
        functools.partial(attention_kernel, blocks, per_kv),
        out_shape=[flat, flat] + [part] * blocks,
        scratch_shapes=[
            pltpu.VMEM((span, wide), jnp.float32),
            pltpu.VMEM((span, wide), jnp.float32),
            pltpu.VMEM((span, wide), jnp.bfloat16),
            pltpu.VMEM((span, wide), jnp.bfloat16),
            pltpu.VMEM((span, wide), jnp.bfloat16),
            pltpu.VMEM((span, wide), jnp.bfloat16),
        ],
        compiler_params=pltpu.CompilerParams(vmem_limit_bytes=40 * 1024 * 1024),
        cost_estimate=SOON,
    )(queries, grads, gain, cosine, sine, query_seg, key_seg, *window)
    return results[0], results[1], results[2:]


def project_kernel(normed, lanes, source_ref, *refs):
    if normed:
        weight_refs, rest = refs[: 2 * lanes], refs[2 * lanes :]
        gain_ref, cos_ref, sin_ref, raw_ref, packed_ref, total_ref = rest
    else:
        weight_refs, (raw_ref, total_ref) = refs[:lanes], refs[lanes:]
    step = pl.program_id(0)
    stacked = [
        jnp.concatenate([ref[...] for ref in weight_refs[start : start + lanes]], axis=0)
        for start in range(0, len(weight_refs), lanes)
    ]
    weight = stacked[0] if len(stacked) == 1 else jnp.concatenate(stacked, axis=1)
    product = three(halves(source_ref[...]), halves(weight), 1, 0)

    @pl.when(step == 0)
    def _():
        total_ref[...] = product

    @pl.when(step > 0)
    def _():
        total_ref[...] += product

    @pl.when(step == pl.num_programs(0) - 1)
    def _():
        if normed:
            head = gain_ref.shape[1]
            raw = total_ref[:, :head]
            raw_ref[...] = raw
            packed_ref[:, :head] = norm_rotate(raw, gain_ref[...], cos_ref[...], sin_ref[...])
            packed_ref[:, head:] = total_ref[:, head:]
        else:
            raw_ref[...] = total_ref[...]


def project(source, weights, group, columns, extra):
    rows, width = source.shape
    steps, lanes = 5, 3
    tile = width // steps
    thin = tile // lanes
    normed = len(weights) > 1
    wide = columns * len(weights)
    whole = [pl.BlockSpec(e.shape, lambda k: (0, 0)) for e in extra]
    outs = [jax.ShapeDtypeStruct((rows, columns), jnp.float32)]
    if normed:
        outs.append(jax.ShapeDtypeStruct((rows, wide), jnp.float32))
    return pl.pallas_call(
        functools.partial(project_kernel, normed, lanes),
        grid=(steps,),
        out_shape=outs,
        in_specs=[pl.BlockSpec((rows, tile), lambda k: (0, k))]
        + [
            pl.BlockSpec((thin, columns), lambda k, lane=lane: (k * lanes + lane, group))
            for lane in range(lanes)
        ]
        * len(weights)
        + whole,
        out_specs=[pl.BlockSpec(o.shape, lambda k: (0, 0)) for o in outs],
        scratch_shapes=[pltpu.VMEM((rows, wide), jnp.float32)],
        compiler_params=pltpu.CompilerParams(vmem_limit_bytes=56 * MIB),
        cost_estimate=SOON
        if normed
        else pl.CostEstimate(
            flops=24 * rows * width * wide, bytes_accessed=1024, transcendentals=0
        ),
    )(source, *[w for w in weights for _ in range(lanes)], *extra)


def settle_kernel(mine_ref, one_ref, far_ref, keep_ref, raw_ref, gain_ref, cos_ref, sin_ref, out_ref):
    head = gain_ref.shape[1]
    total = mine_ref[...] + one_ref[...] * keep_ref[...] + far_ref[...]
    out_ref[:, :head] = norm_rotate_back(
        total[:, :head], raw_ref[...], gain_ref[...], cos_ref[...], sin_ref[...]
    )
    out_ref[:, head:] = total[:, head:]


def settle(mine, one, far, keep, raw, gain, cosine, sine):
    return pl.pallas_call(
        settle_kernel,
        out_shape=jax.ShapeDtypeStruct(mine.shape, jnp.float32),
        compiler_params=pltpu.CompilerParams(vmem_limit_bytes=16 * MIB),
        cost_estimate=SOON,
    )(mine, one, far, keep, raw, gain, cosine, sine)


def flip_kernel(source_ref, out_ref):
    out_ref[...] = source_ref[...].T


def flip(source):
    rows, width = source.shape
    tile = width // 5
    return pl.pallas_call(
        flip_kernel,
        grid=(5,),
        out_shape=jax.ShapeDtypeStruct((width, rows), jnp.float32),
        in_specs=[pl.BlockSpec((rows, tile), lambda k: (0, k))],
        out_specs=pl.BlockSpec((tile, rows), lambda k: (k, 0)),
        compiler_params=pltpu.CompilerParams(vmem_limit_bytes=16 * MIB),
        cost_estimate=SOON,
    )(source)


def turn_kernel(place_ref, others_ref, own_ref, high_ref, low_ref):
    step = pl.program_id(0)

    @pl.when(step < CHAIN - 1)
    def _():
        high_ref[0], low_ref[0] = halves(others_ref[0])

    @pl.when(step == CHAIN - 1)
    def _():
        high_ref[0], low_ref[0] = halves(own_ref[...])


def turn(place, others, own):
    slab, rows = own.shape
    half = jax.ShapeDtypeStruct((CHAIN, slab, rows), jnp.bfloat16)
    out_spec = pl.BlockSpec((1, slab, rows), lambda i, p: ((p[0] + 1 + i) % CHAIN, 0, 0))
    return pl.pallas_call(
        turn_kernel,
        grid_spec=pltpu.PrefetchScalarGridSpec(
            num_scalar_prefetch=1,
            grid=(CHAIN,),
            in_specs=[
                pl.BlockSpec((1, slab, rows), lambda i, p: (jnp.minimum(i, CHAIN - 2), 0, 0)),
                pl.BlockSpec((slab, rows), lambda i, p: (0, 0)),
            ],
            out_specs=[out_spec, out_spec],
        ),
        out_shape=[half, half],
        compiler_params=pltpu.CompilerParams(vmem_limit_bytes=24 * MIB),
        cost_estimate=SOON,
    )(place, others, own)


def product_kernel(start, place_ref, high_ref, low_ref, *refs):
    blocks, out_ref = refs[:-1], refs[-1]
    total = None
    for hop in range(CHAIN):
        slot = lax.rem(place_ref[0] + (CHAIN - hop), CHAIN)
        block = blocks[hop]
        if block.shape[1] == out_ref.shape[1]:
            block = block[...]
        else:
            block = block[:, start : start + out_ref.shape[1]]
        term = three((high_ref[slot], low_ref[slot]), halves(block), 1, 0)
        total = term if total is None else total + term
    out_ref[...] = total


def product(place, step, turned, blocks, pair, span):
    high, low = turned
    part = high.shape[1] // pair
    rows = high.shape[2]
    columns = span[1] or blocks[0].shape[1]
    spec = pl.BlockSpec((CHAIN, part, rows), lambda i, p: (0, (p[1] + step) % pair, 0))
    return pl.pallas_call(
        functools.partial(product_kernel, span[0]),
        grid_spec=pltpu.PrefetchScalarGridSpec(
            num_scalar_prefetch=1,
            grid=(1,),
            in_specs=[spec, spec] + [pl.BlockSpec(b.shape, lambda i, p: (0, 0)) for b in blocks],
            out_specs=pl.BlockSpec((part, columns), lambda i, p: (0, 0)),
        ),
        out_shape=jax.ShapeDtypeStruct((part, columns), jnp.float32),
        compiler_params=pltpu.CompilerParams(vmem_limit_bytes=28 * MIB),
        cost_estimate=SOON,
    )(place, high, low, *blocks)


def strip_kernel(pieces, added, strips_ref, *refs):
    weight_refs, left_refs = refs[: len(pieces)], refs[len(pieces) : -1]
    total = left_refs[-1][0] if added else None
    left_at = 0
    for ref, (count, start, wide) in zip(weight_refs, pieces):
        for group in range(count):
            left = left_refs[left_at + group][:, start : start + wide]
            right = ref[:, group * wide : (group + 1) * wide]
            term = three(halves(right), halves(left), 1, 1)
            total = term if total is None else total + term
        left_at = left_at if start == 0 and len(pieces) > 1 else left_at + count
    refs[-1][0] = total


def input_strips(strips, strip, weights, lefts, pieces, partial):
    count = strips.shape[0]
    rows = lefts[0].shape[0]
    wide = sum(w.shape[1] for w in weights)
    whole = [pl.BlockSpec(d.shape, lambda i, p: (0, 0)) for d in lefts]
    out_spec = pl.BlockSpec((1, strip, rows), lambda i, p: (i, 0, 0))
    return pl.pallas_call(
        functools.partial(strip_kernel, pieces, partial is not None),
        grid_spec=pltpu.PrefetchScalarGridSpec(
            num_scalar_prefetch=1,
            grid=(count,),
            in_specs=[pl.BlockSpec((strip, w.shape[1]), lambda i, p: (p[i], 0)) for w in weights]
            + whole
            + ([] if partial is None else [out_spec]),
            out_specs=out_spec,
        ),
        out_shape=jax.ShapeDtypeStruct((count, strip, rows), jnp.float32),
        compiler_params=pltpu.CompilerParams(vmem_limit_bytes=56 * MIB),
        cost_estimate=SOON,
    )(strips, *weights, *lefts, *([] if partial is None else [partial]))


def local(hidden_in, query_proj, key_proj, value_proj, query_gain, key_gain, segment_ids, grad_out):
    rows_dev, width = hidden_in.shape
    head = query_gain.shape[0]
    kv_local = key_proj.shape[1] // head
    per_kv = query_proj.shape[1] // key_proj.shape[1]
    pair = lax.axis_size("y")
    count = CHAIN * pair
    members = lax.axis_size("tensor")
    member = lax.axis_index("tensor")
    along = lax.axis_index("z")
    across = lax.axis_index("y")
    seq_index = along * pair + across
    reach = (WINDOW - 1) // rows_dev + 1
    span = (reach + 1) * rows_dev
    slab = width // CHAIN
    part = width // count
    piece = slab // members
    groups = range(kv_local)
    short = pair == 2 and reach == 4

    def z_shift(block, step):
        route = [(i, i + step) for i in range(CHAIN) if 0 <= i + step < CHAIN]
        return lax.ppermute(block, "z", route)

    def z_ring(block, step):
        return lax.ppermute(block, "z", [(i, (i + step) % CHAIN) for i in range(CHAIN)])

    def y_ring(block, step):
        return lax.ppermute(block, "y", [(i, (i + step) % pair) for i in range(pair)])

    def shifted(block, distance):
        route = [(i - distance, i) for i in range(count) if 0 <= i - distance < count]
        return lax.ppermute(block, ("z", "y"), route)

    first_row = seq_index * rows_dev
    positions = first_row + jnp.arange(rows_dev, dtype=jnp.int32)
    cosine, sine = rope_tables(positions, head)
    seg_pad = jnp.concatenate([jnp.full((reach * rows_dev,), -1, jnp.int32), segment_ids])
    key_seg = lax.dynamic_slice_in_dim(seg_pad, first_row, span, 0)[:, None]
    query_seg = lax.dynamic_slice_in_dim(segment_ids, first_row, rows_dev, 0)[None, :]

    def q_columns(array, group):
        return array[:, group * per_kv * head : (group + 1) * per_kv * head]

    key_raw, own, two, queries = [], [], [], []
    tables = (key_gain[None, :], cosine, sine)
    for group in groups:
        source = after(hidden_in, own[-1]) if own else hidden_in
        raw, packed = project(source, (key_proj, value_proj), group, head, tables)
        key_raw.append(raw)
        own.append(packed)
        if short:
            two.append(z_shift(own[group], 1))

    def neighbour(group, *earlier):
        block = jnp.where(across == 0, own[group], two[group])
        return y_ring(after(block, *earlier) if earlier else block, 1)

    def farthest(group, four, *earlier):
        back = after(two[group], *earlier)
        return y_ring(jnp.where(across == 0, back, four), 1)

    for group in groups:
        source = after(hidden_in, *own, *queries)
        queries.append(project(source, (query_proj,), group, per_kv * head, ())[0])

    hidden_rows = flip(after(hidden_in, *queries))
    windows, fours, ones = [], [], []
    if short:
        for group in groups:
            ones.append(neighbour(group))
        for group in groups:
            fours.append(z_shift(after(two[group], own[-1]), 1))
        for group in groups:
            three_back = farthest(group, fours[group], *ones, *fours[: group + 1], hidden_rows)
            windows.append([fours[group], three_back, two[group], ones[group], own[group]])
    else:
        for group in groups:
            windows.append([shifted(own[group], d) for d in range(reach, 0, -1)] + [own[group]])
    def sent_along(source, step):
        start = (along + step) % CHAIN * slab + member * piece
        return z_shift(lax.dynamic_slice_in_dim(source, start, piece, 0), step)

    from_above = [sent_along(hidden_rows, -step) for step in range(1, CHAIN)]

    chips = members // CORES
    chip, core = member // CORES, member % CORES

    def to_core(block):
        return lax.ppermute(block, "tensor", [(i, i ^ 1) for i in range(members)])

    def to_chip(block, step):
        route = [(i, (i + step * CORES) % members) for i in range(members)]
        return lax.ppermute(block, "tensor", route)

    def in_order(blocks, index, axis):
        size = blocks[0].shape[axis]
        both = jnp.concatenate(blocks + blocks[:-1], axis=axis)
        start = (len(blocks) - 1 - index) * size
        return lax.dynamic_slice_in_dim(both, start, len(blocks) * size, axis)

    attended, d_query, parts = [], [], []
    for group in groups:
        ready = attended or from_above
        out, d_q, d_kv = attention(
            after(queries[group], *ready),
            q_columns(grad_out, group),
            query_gain[None, :],
            cosine,
            sine,
            query_seg,
            key_seg,
            windows[group],
            per_kv,
        )
        attended.append(out)
        d_query.append(d_q)
        parts.append(d_kv)

    upward = after(hidden_rows, *attended[:1])
    from_below = [sent_along(upward, step) for step in range(1, CHAIN)]
    pieces = [
        jnp.where(along >= step, from_below[step - 1], from_above[CHAIN - 1 - step])
        for step in range(CHAIN - 1, 0, -1)
    ]
    mine = jnp.stack(pieces)
    chip_rows = in_order([to_core(mine), mine], core, 1)
    arrivals = [to_chip(chip_rows, step) for step in range(chips - 1, 0, -1)]
    others = in_order(arrivals + [chip_rows], chip, 1)
    own_slab = lax.dynamic_slice_in_dim(hidden_rows, along * slab, slab, 0)
    place = jnp.stack([along, across]).astype(jnp.int32)
    turned = turn(place, others, own_slab)

    strip = width // members
    turns = [(chip + step) % chips for step in range(chips)]
    theirs_at = jnp.stack([c * CORES + 1 - core for c in turns]).astype(jnp.int32)
    mine_at = jnp.stack([c * CORES + core for c in turns]).astype(jnp.int32)

    def query_strips(which):
        pieces = ((kv_local, 0, per_kv * head),)
        return input_strips(which, strip, (query_proj,), d_query, pieces, None)

    def kv_strips(which, partial):
        pieces = ((kv_local, 0, head), (kv_local, head, head))
        return input_strips(which, strip, (key_proj, value_proj), d_kv, pieces, partial)

    def product_of(ring, step, span=(0, 0)):
        return product(place, step, turned, ring, pair, span)

    def terms(ring, span=(0, 0)):
        return [product_of(ring, step, span) for step in range(pair - 1, 0, -1)]

    def exchange(sent):
        return [y_ring(term, pair - 1 - i) for i, term in enumerate(sent)]

    sent = []

    def follow(block, send, extra):
        earlier = sent[-2:-1] + list(extra)
        sent.append(send(after(block, *earlier) if earlier else block))
        return sent[-1]

    keep = jnp.where(across == 0, 1.0, 0.0).reshape(1, 1).astype(jnp.float32)
    q_rings = [[d] for d in d_query]
    d_kv, k_rings, held = [], [], []

    def q_hop(group, *extra):
        q_rings[group].append(follow(q_rings[group][-1], lambda b: z_ring(b, 1), extra))

    def k_hop(group, *extra):
        k_rings[group].append(follow(k_rings[group][-1], lambda b: z_ring(b, 1), extra))

    def far_return(group, *extra):
        four, three_back, two_back, one, mine = parts[group]
        from_three = y_ring(three_back, 1)
        from_one = y_ring(one, 1)
        block = four + jnp.where(across == 0, 0.0, from_three)
        got = follow(block, lambda b: z_shift(b, -1), extra)
        held.append((two_back + jnp.where(across == 0, from_three, from_one) + got, from_one))

    def near_return(group, extra, before):
        block, from_one = held[group]
        far = follow(block, lambda b: z_shift(b, -1), extra)
        far = after(far, *before) if before else far
        mine = parts[group][-1]
        d_kv.append(settle(mine, from_one, far, keep, key_raw[group], *tables))
        k_rings.append([d_kv[group]])

    if short and kv_local == 2:
        q_hop(0)
        far_return(0, q_rings[0][1], *attended)
        q_hop(0)
        near_return(0, [q_rings[0][2]], from_below)
        q_hop(1)
        theirs_q = query_strips(theirs_at)
        far_return(1, theirs_q, q_rings[1][1])
        q_hop(0)
        mine_q = query_strips(mine_at)
        q_hop(1)
        near_return(1, [mine_q, q_rings[0][3]], [q_rings[1][2]])
        k_hop(0)
        q_terms = [terms(q_rings[0])]
        q_hop(1, *q_terms[0])
        k_hop(0)
        theirs = kv_strips(theirs_at, theirs_q)
        q_sent = [exchange(q_terms[0])]
        k_hop(1, theirs)
        q_terms.append(terms(q_rings[1]))
        sums = kv_strips(mine_at, mine_q) + to_core(theirs)
        from_chips = [to_chip(sums[step], step) for step in range(1, chips)]
        k_hop(0, sums, *q_terms[1])
        k_hop(1, *q_sent[0])
        k_terms = [terms(k_rings[0])]
        q_sent.append(exchange(q_terms[1]))
        last = after(k_rings[1][-1], sent[-2], *from_chips, *k_terms[0], *q_sent[1])
        tails = [z_ring(last[:, head:], 1), z_ring(last[:, :head], 1)]
        tail_rings = [k_rings[1] + [tail] for tail in tails]
        tail_spans = [(head, head), (0, head)]
    else:
        for group in groups:
            mine = parts[group][reach]
            total = jnp.zeros_like(mine)
            for distance in range(1, reach + 1):
                total = total + shifted(parts[group][reach - distance], -distance)
            d_kv.append(settle(mine, mine, total, 0.0 * keep, key_raw[group], *tables))
            k_rings.append([d_kv[group]])
            for _ in range(CHAIN - 1):
                q_hop(group)
            for _ in range(CHAIN - 1):
                k_hop(group)
        theirs = kv_strips(theirs_at, query_strips(theirs_at))
        sums = kv_strips(mine_at, query_strips(mine_at))
        q_sent = [exchange(terms(ring)) for ring in q_rings]
        sums = sums + to_core(theirs)
        from_chips = [to_chip(sums[step], step) for step in range(1, chips)]
        k_terms = [terms(ring) for ring in k_rings[:-1]]
        tail_rings, tail_spans = [k_rings[-1]], [(0, 2 * head)]

    grad_input = sums[0]
    for arrival in from_chips:
        grad_input = grad_input + arrival

    def finish(ring, arrived, span=(0, 0)):
        total = product_of(ring, 0, span)
        for term in arrived:
            total = total + term
        return total

    grad_query = [finish(ring, arrived) for ring, arrived in zip(q_rings, q_sent)]
    tail_terms = [terms(ring, span) for ring, span in zip(tail_rings, tail_spans)]
    tail_sent = [exchange(term) for term in tail_terms]
    grad_kv = [finish(ring, exchange(term)) for ring, term in zip(k_rings, k_terms)]
    ends = [finish(*each) for each in zip(tail_rings, tail_sent, tail_spans)]
    grad_kv.append(jnp.concatenate(ends[::-1], axis=1))

    return (
        jnp.concatenate(attended, axis=1),
        grad_input.T,
        jnp.concatenate(grad_query, axis=1),
        jnp.concatenate([g[:, :head] for g in grad_kv], axis=1),
        jnp.concatenate([g[:, head:] for g in grad_kv], axis=1),
    )


def solution(mesh):
    seq, members = mesh.devices.shape
    split = Mesh(mesh.devices.reshape(CHAIN, seq // CHAIN, members), ("z", "y", "tensor"))
    tokens = ("z", "y")
    return jax.shard_map(
        local,
        mesh=split,
        in_specs=(
            P(tokens, None),
            P(None, "tensor"),
            P(None, "tensor"),
            P(None, "tensor"),
            P(),
            P(),
            P(),
            P(tokens, "tensor"),
        ),
        out_specs=(
            P(tokens, "tensor"),
            P(tokens, "tensor"),
            P(tokens, "tensor"),
            P(tokens, "tensor"),
            P(tokens, "tensor"),
        ),
        check_vma=False,
    )
```

```python
import functools

import jax
import jax.numpy as jnp
from jax import lax
from jax.experimental import pallas as pl
from jax.experimental.pallas import tpu as pltpu
from jax.sharding import Mesh, PartitionSpec as P

WINDOW = 1024
CHAIN = 4
CORES = 2

MIB = 1024 * 1024
SOON = pl.CostEstimate(flops=1024, bytes_accessed=1024, transcendentals=0)
epsilon = 1e-06


def after(block, *earlier):
    return lax.optimization_barrier((block, earlier))[0]


def rope_tables(positions, head_width):
    middle = head_width // 2
    exponent = 2.0 * jnp.arange(middle).astype(jnp.float32) / head_width
    frequency = 10000.0 ** (-exponent)
    angles = positions.astype(jnp.float32)[:, None] * frequency[None, :]
    return jnp.cos(angles), jnp.sin(angles)


def inverse_rms(vector):
    return lax.rsqrt(jnp.mean(vector * vector, axis=-1, keepdims=True) + epsilon)


def norm_rotate(vector, scaling, cosine, sine):
    middle = vector.shape[-1] // 2
    normed = vector * inverse_rms(vector) * scaling
    low, high = normed[:, :middle], normed[:, middle:]
    return jnp.concatenate([low * cosine - high * sine, high * cosine + low * sine], axis=1)


def norm_rotate_back(grad, vector, scaling, cosine, sine):
    middle = vector.shape[-1] // 2
    low, high = grad[:, :middle], grad[:, middle:]
    d_normed = jnp.concatenate([low * cosine + high * sine, high * cosine - low * sine], axis=1)
    d_normed = d_normed * scaling
    inverse = inverse_rms(vector)
    unit = vector * inverse
    return inverse * (d_normed - unit * jnp.mean(d_normed * unit, axis=-1, keepdims=True))


def halves(array):
    high = array.astype(jnp.bfloat16)
    return high, (array - high.astype(jnp.float32)).astype(jnp.bfloat16)


def three(left, right, left_dim, right_dim):
    def once(a, b):
        return lax.dot_general(
            a, b, (((left_dim,), (right_dim,)), ((), ())), preferred_element_type=jnp.float32
        )

    return once(left[0], right[0]) + (once(left[0], right[1]) + once(left[1], right[0]))


def attention_kernel(blocks, per_kv, *refs):
    query_ref, grad_ref, gain_ref, cos_ref, sin_ref, seg_ref, key_seg_ref = refs[:7]
    kv_refs = refs[7 : 7 + blocks]
    out_ref, d_query_ref = refs[7 + blocks : 9 + blocks]
    d_kv_refs = refs[9 + blocks : 9 + 2 * blocks]
    weight_ref, d_share_ref, share_high, share_low, score_high, score_low = refs[9 + 2 * blocks :]
    rows = query_ref.shape[0]
    head = gain_ref.shape[1]
    factor = head ** (-0.5)
    gain, cosine, sine = gain_ref[...], cos_ref[...], sin_ref[...]
    raw = [query_ref[:, h * head : (h + 1) * head] for h in range(per_kv)]
    q_rot = halves(
        jnp.concatenate([norm_rotate(u, gain, cosine, sine) for u in raw], axis=0)
    )
    grad = halves(
        jnp.concatenate([grad_ref[:, h * head : (h + 1) * head] for h in range(per_kv)], axis=0)
    )
    total = jnp.zeros((1, per_kv * rows), jnp.float32)
    mixed = jnp.zeros((1, per_kv * rows), jnp.float32)
    seg = jnp.concatenate([seg_ref[...]] * per_kv, axis=1)
    turned_keys, turned_values = [], []
    lane = lax.broadcasted_iota(jnp.int32, (rows, rows), 1)
    lane = jnp.concatenate([lane] * per_kv, axis=1)
    row = lax.broadcasted_iota(jnp.int32, (rows, per_kv * rows), 0)
    for j in range(blocks):
        place = slice(j * rows, (j + 1) * rows)
        key, value = kv_refs[j][:, :head], kv_refs[j][:, head:]
        turned_keys.append(key.T)
        turned_values.append(value.T)
        scores = three(halves(key), q_rot, 1, 1) * factor
        distance = (blocks - 1 - j) * rows + lane - row
        allowed = (distance >= 0) & (distance < WINDOW) & (key_seg_ref[place, :] == seg)
        weights = jnp.where(allowed, jnp.exp(scores), 0.0)
        d_shares = three(halves(value), grad, 1, 1)
        weight_ref[place, :] = weights
        d_share_ref[place, :] = d_shares
        total = total + jnp.sum(weights, axis=0, keepdims=True)
        mixed = mixed + jnp.sum(weights * d_shares, axis=0, keepdims=True)
    scale = 1.0 / total
    delta = mixed * scale
    for j in range(blocks):
        place = slice(j * rows, (j + 1) * rows)
        shares = weight_ref[place, :] * scale
        d_scores = shares * (d_share_ref[place, :] - delta) * factor
        share_pair = halves(shares)
        score_pair = halves(d_scores)
        share_high[place, :], share_low[place, :] = share_pair
        score_high[place, :], score_low[place, :] = score_pair
        d_kv_refs[j][:, :head] = three(score_pair, q_rot, 1, 0)
        d_kv_refs[j][:, head:] = three(share_pair, grad, 1, 0)
    turned_out = three(
        halves(jnp.concatenate(turned_values, axis=1)), (share_high[...], share_low[...]), 1, 0
    )
    turned_query = three(
        halves(jnp.concatenate(turned_keys, axis=1)), (score_high[...], score_low[...]), 1, 0
    )
    for h in range(per_kv):
        place = slice(h * rows, (h + 1) * rows)
        columns = slice(h * head, (h + 1) * head)
        out_ref[:, columns] = turned_out[:, place].T
        d_query_ref[:, columns] = norm_rotate_back(
            turned_query[:, place].T, raw[h], gain, cosine, sine
        )


def attention(queries, grads, gain, cosine, sine, query_seg, key_seg, window, per_kv):
    rows, width = queries.shape
    blocks = len(window)
    span = blocks * rows
    flat = jax.ShapeDtypeStruct((rows, width), jnp.float32)
    part = jax.ShapeDtypeStruct(window[0].shape, jnp.float32)
    wide = per_kv * rows
    results = pl.pallas_call(
        functools.partial(attention_kernel, blocks, per_kv),
        out_shape=[flat, flat] + [part] * blocks,
        scratch_shapes=[
            pltpu.VMEM((span, wide), jnp.float32),
            pltpu.VMEM((span, wide), jnp.float32),
            pltpu.VMEM((span, wide), jnp.bfloat16),
            pltpu.VMEM((span, wide), jnp.bfloat16),
            pltpu.VMEM((span, wide), jnp.bfloat16),
            pltpu.VMEM((span, wide), jnp.bfloat16),
        ],
        compiler_params=pltpu.CompilerParams(vmem_limit_bytes=40 * 1024 * 1024),
        cost_estimate=SOON,
    )(queries, grads, gain, cosine, sine, query_seg, key_seg, *window)
    return results[0], results[1], results[2:]


def project_kernel(normed, lanes, source_ref, *refs):
    if normed:
        weight_refs, rest = refs[: 2 * lanes], refs[2 * lanes :]
        gain_ref, cos_ref, sin_ref, raw_ref, packed_ref, total_ref = rest
    else:
        weight_refs, (raw_ref, total_ref) = refs[:lanes], refs[lanes:]
    step = pl.program_id(0)
    stacked = [
        jnp.concatenate([ref[...] for ref in weight_refs[start : start + lanes]], axis=0)
        for start in range(0, len(weight_refs), lanes)
    ]
    weight = stacked[0] if len(stacked) == 1 else jnp.concatenate(stacked, axis=1)
    product = three(halves(source_ref[...]), halves(weight), 1, 0)

    @pl.when(step == 0)
    def _():
        total_ref[...] = product

    @pl.when(step > 0)
    def _():
        total_ref[...] += product

    @pl.when(step == pl.num_programs(0) - 1)
    def _():
        if normed:
            head = gain_ref.shape[1]
            raw = total_ref[:, :head]
            raw_ref[...] = raw
            packed_ref[:, :head] = norm_rotate(raw, gain_ref[...], cos_ref[...], sin_ref[...])
            packed_ref[:, head:] = total_ref[:, head:]
        else:
            raw_ref[...] = total_ref[...]


def project(source, weights, group, columns, extra):
    rows, width = source.shape
    steps, lanes = 5, 3
    tile = width // steps
    thin = tile // lanes
    normed = len(weights) > 1
    wide = columns * len(weights)
    whole = [pl.BlockSpec(e.shape, lambda k: (0, 0)) for e in extra]
    outs = [jax.ShapeDtypeStruct((rows, columns), jnp.float32)]
    if normed:
        outs.append(jax.ShapeDtypeStruct((rows, wide), jnp.float32))
    return pl.pallas_call(
        functools.partial(project_kernel, normed, lanes),
        grid=(steps,),
        out_shape=outs,
        in_specs=[pl.BlockSpec((rows, tile), lambda k: (0, k))]
        + [
            pl.BlockSpec((thin, columns), lambda k, lane=lane: (k * lanes + lane, group))
            for lane in range(lanes)
        ]
        * len(weights)
        + whole,
        out_specs=[pl.BlockSpec(o.shape, lambda k: (0, 0)) for o in outs],
        scratch_shapes=[pltpu.VMEM((rows, wide), jnp.float32)],
        compiler_params=pltpu.CompilerParams(vmem_limit_bytes=56 * MIB),
        cost_estimate=SOON,
    )(source, *[w for w in weights for _ in range(lanes)], *extra)


def settle_kernel(mine_ref, one_ref, far_ref, keep_ref, raw_ref, gain_ref, cos_ref, sin_ref, out_ref):
    head = gain_ref.shape[1]
    total = mine_ref[...] + one_ref[...] * keep_ref[...] + far_ref[...]
    out_ref[:, :head] = norm_rotate_back(
        total[:, :head], raw_ref[...], gain_ref[...], cos_ref[...], sin_ref[...]
    )
    out_ref[:, head:] = total[:, head:]


def settle(mine, one, far, keep, raw, gain, cosine, sine):
    return pl.pallas_call(
        settle_kernel,
        out_shape=jax.ShapeDtypeStruct(mine.shape, jnp.float32),
        compiler_params=pltpu.CompilerParams(vmem_limit_bytes=16 * MIB),
        cost_estimate=SOON,
    )(mine, one, far, keep, raw, gain, cosine, sine)


def flip_kernel(source_ref, out_ref):
    out_ref[...] = source_ref[...].T


def flip(source):
    rows, width = source.shape
    tile = width // 5
    return pl.pallas_call(
        flip_kernel,
        grid=(5,),
        out_shape=jax.ShapeDtypeStruct((width, rows), jnp.float32),
        in_specs=[pl.BlockSpec((rows, tile), lambda k: (0, k))],
        out_specs=pl.BlockSpec((tile, rows), lambda k: (k, 0)),
        compiler_params=pltpu.CompilerParams(vmem_limit_bytes=16 * MIB),
        cost_estimate=SOON,
    )(source)


def turn_kernel(place_ref, others_ref, own_ref, high_ref, low_ref):
    step = pl.program_id(0)

    @pl.when(step < CHAIN - 1)
    def _():
        high_ref[0], low_ref[0] = halves(others_ref[0])

    @pl.when(step == CHAIN - 1)
    def _():
        high_ref[0], low_ref[0] = halves(own_ref[...])


def turn(place, others, own):
    slab, rows = own.shape
    half = jax.ShapeDtypeStruct((CHAIN, slab, rows), jnp.bfloat16)
    out_spec = pl.BlockSpec((1, slab, rows), lambda i, p: ((p[0] + 1 + i) % CHAIN, 0, 0))
    return pl.pallas_call(
        turn_kernel,
        grid_spec=pltpu.PrefetchScalarGridSpec(
            num_scalar_prefetch=1,
            grid=(CHAIN,),
            in_specs=[
                pl.BlockSpec((1, slab, rows), lambda i, p: (jnp.minimum(i, CHAIN - 2), 0, 0)),
                pl.BlockSpec((slab, rows), lambda i, p: (0, 0)),
            ],
            out_specs=[out_spec, out_spec],
        ),
        out_shape=[half, half],
        compiler_params=pltpu.CompilerParams(vmem_limit_bytes=24 * MIB),
        cost_estimate=SOON,
    )(place, others, own)


def product_kernel(start, place_ref, high_ref, low_ref, *refs):
    blocks, out_ref = refs[:-1], refs[-1]
    total = None
    for hop in range(CHAIN):
        slot = lax.rem(place_ref[0] + (CHAIN - hop), CHAIN)
        block = blocks[hop]
        if block.shape[1] == out_ref.shape[1]:
            block = block[...]
        else:
            block = block[:, start : start + out_ref.shape[1]]
        term = three((high_ref[slot], low_ref[slot]), halves(block), 1, 0)
        total = term if total is None else total + term
    out_ref[...] = total


def product(place, step, turned, blocks, pair, span):
    high, low = turned
    part = high.shape[1] // pair
    rows = high.shape[2]
    columns = span[1] or blocks[0].shape[1]
    spec = pl.BlockSpec((CHAIN, part, rows), lambda i, p: (0, (p[1] + step) % pair, 0))
    return pl.pallas_call(
        functools.partial(product_kernel, span[0]),
        grid_spec=pltpu.PrefetchScalarGridSpec(
            num_scalar_prefetch=1,
            grid=(1,),
            in_specs=[spec, spec] + [pl.BlockSpec(b.shape, lambda i, p: (0, 0)) for b in blocks],
            out_specs=pl.BlockSpec((part, columns), lambda i, p: (0, 0)),
        ),
        out_shape=jax.ShapeDtypeStruct((part, columns), jnp.float32),
        compiler_params=pltpu.CompilerParams(vmem_limit_bytes=28 * MIB),
        cost_estimate=SOON,
    )(place, high, low, *blocks)


def strip_kernel(pieces, added, strips_ref, *refs):
    weight_refs, left_refs = refs[: len(pieces)], refs[len(pieces) : -1]
    total = left_refs[-1][0] if added else None
    left_at = 0
    for ref, (count, start, wide) in zip(weight_refs, pieces):
        for group in range(count):
            left = left_refs[left_at + group][:, start : start + wide]
            right = ref[:, group * wide : (group + 1) * wide]
            term = three(halves(right), halves(left), 1, 1)
            total = term if total is None else total + term
        left_at = left_at if start == 0 and len(pieces) > 1 else left_at + count
    refs[-1][0] = total


def input_strips(strips, strip, weights, lefts, pieces, partial):
    count = strips.shape[0]
    rows = lefts[0].shape[0]
    wide = sum(w.shape[1] for w in weights)
    whole = [pl.BlockSpec(d.shape, lambda i, p: (0, 0)) for d in lefts]
    out_spec = pl.BlockSpec((1, strip, rows), lambda i, p: (i, 0, 0))
    return pl.pallas_call(
        functools.partial(strip_kernel, pieces, partial is not None),
        grid_spec=pltpu.PrefetchScalarGridSpec(
            num_scalar_prefetch=1,
            grid=(count,),
            in_specs=[pl.BlockSpec((strip, w.shape[1]), lambda i, p: (p[i], 0)) for w in weights]
            + whole
            + ([] if partial is None else [out_spec]),
            out_specs=out_spec,
        ),
        out_shape=jax.ShapeDtypeStruct((count, strip, rows), jnp.float32),
        compiler_params=pltpu.CompilerParams(vmem_limit_bytes=56 * MIB),
        cost_estimate=pl.CostEstimate(
            flops=6 * count * rows * strip * wide,
            bytes_accessed=4 * count * strip * (wide + rows),
            transcendentals=0,
        ),
    )(strips, *weights, *lefts, *([] if partial is None else [partial]))


def local(hidden_in, query_proj, key_proj, value_proj, query_gain, key_gain, segment_ids, grad_out):
    rows_dev, width = hidden_in.shape
    head = query_gain.shape[0]
    kv_local = key_proj.shape[1] // head
    per_kv = query_proj.shape[1] // key_proj.shape[1]
    pair = lax.axis_size("y")
    count = CHAIN * pair
    members = lax.axis_size("tensor")
    member = lax.axis_index("tensor")
    along = lax.axis_index("z")
    across = lax.axis_index("y")
    seq_index = along * pair + across
    reach = (WINDOW - 1) // rows_dev + 1
    span = (reach + 1) * rows_dev
    slab = width // CHAIN
    part = width // count
    piece = slab // members
    groups = range(kv_local)
    short = pair == 2 and reach == 4

    def z_shift(block, step):
        route = [(i, i + step) for i in range(CHAIN) if 0 <= i + step < CHAIN]
        return lax.ppermute(block, "z", route)

    def z_ring(block, step):
        return lax.ppermute(block, "z", [(i, (i + step) % CHAIN) for i in range(CHAIN)])

    def y_ring(block, step):
        return lax.ppermute(block, "y", [(i, (i + step) % pair) for i in range(pair)])

    def shifted(block, distance):
        route = [(i - distance, i) for i in range(count) if 0 <= i - distance < count]
        return lax.ppermute(block, ("z", "y"), route)

    first_row = seq_index * rows_dev
    positions = first_row + jnp.arange(rows_dev, dtype=jnp.int32)
    cosine, sine = rope_tables(positions, head)
    seg_pad = jnp.concatenate([jnp.full((reach * rows_dev,), -1, jnp.int32), segment_ids])
    key_seg = lax.dynamic_slice_in_dim(seg_pad, first_row, span, 0)[:, None]
    query_seg = lax.dynamic_slice_in_dim(segment_ids, first_row, rows_dev, 0)[None, :]

    def q_columns(array, group):
        return array[:, group * per_kv * head : (group + 1) * per_kv * head]

    key_raw, own, two, queries = [], [], [], []
    tables = (key_gain[None, :], cosine, sine)
    for group in groups:
        source = after(hidden_in, own[-1]) if own else hidden_in
        raw, packed = project(source, (key_proj, value_proj), group, head, tables)
        key_raw.append(raw)
        own.append(packed)
        if short:
            two.append(z_shift(own[group], 1))

    def neighbour(group, *earlier):
        block = jnp.where(across == 0, own[group], two[group])
        return y_ring(after(block, *earlier) if earlier else block, 1)

    def farthest(group, four, *earlier):
        back = after(two[group], *earlier)
        return y_ring(jnp.where(across == 0, back, four), 1)

    for group in groups:
        source = after(hidden_in, *own, *two[:1], *queries)
        queries.append(project(source, (query_proj,), group, per_kv * head, ())[0])

    hidden_rows = flip(after(hidden_in, *queries))
    windows, fours, ones = [], [], []
    if short:
        for group in groups:
            ones.append(neighbour(group))
        for group in groups:
            fours.append(z_shift(after(two[group], own[-1]), 1))
        for group in groups:
            three_back = farthest(group, fours[group], *ones, *fours[: group + 1], hidden_rows)
            windows.append([fours[group], three_back, two[group], ones[group], own[group]])
    else:
        for group in groups:
            windows.append([shifted(own[group], d) for d in range(reach, 0, -1)] + [own[group]])
    def sent_along(source, step):
        start = (along + step) % CHAIN * slab + member * piece
        return z_shift(lax.dynamic_slice_in_dim(source, start, piece, 0), step)

    from_above = [sent_along(hidden_rows, -step) for step in range(1, CHAIN)]

    chips = members // CORES
    chip, core = member // CORES, member % CORES

    def to_core(block):
        return lax.ppermute(block, "tensor", [(i, i ^ 1) for i in range(members)])

    def to_chip(block, step):
        route = [(i, (i + step * CORES) % members) for i in range(members)]
        return lax.ppermute(block, "tensor", route)

    def in_order(blocks, index, axis):
        size = blocks[0].shape[axis]
        both = jnp.concatenate(blocks + blocks[:-1], axis=axis)
        start = (len(blocks) - 1 - index) * size
        return lax.dynamic_slice_in_dim(both, start, len(blocks) * size, axis)

    attended, d_query, parts = [], [], []
    for group in groups:
        ready = attended + (from_above if attended else [])
        out, d_q, d_kv = attention(
            after(queries[group], *ready) if ready else queries[group],
            q_columns(grad_out, group),
            query_gain[None, :],
            cosine,
            sine,
            query_seg,
            key_seg,
            windows[group],
            per_kv,
        )
        attended.append(out)
        d_query.append(d_q)
        parts.append(d_kv)

    upward = after(hidden_rows, *attended[:1])
    from_below = [sent_along(upward, step) for step in range(1, CHAIN)]
    pieces = [
        jnp.where(along >= step, from_below[step - 1], from_above[CHAIN - 1 - step])
        for step in range(CHAIN - 1, 0, -1)
    ]
    mine = jnp.stack(pieces)
    chip_rows = in_order([to_core(mine), mine], core, 1)
    arrivals = [to_chip(chip_rows, step) for step in range(chips - 1, 0, -1)]
    others = in_order(arrivals + [chip_rows], chip, 1)
    own_slab = lax.dynamic_slice_in_dim(hidden_rows, along * slab, slab, 0)
    place = jnp.stack([along, across]).astype(jnp.int32)
    turned = turn(place, others, own_slab)

    strip = width // members
    turns = [(chip + step) % chips for step in range(chips)]
    theirs_at = jnp.stack([c * CORES + 1 - core for c in turns]).astype(jnp.int32)
    mine_at = jnp.stack([c * CORES + core for c in turns]).astype(jnp.int32)

    def query_strips(which):
        pieces = ((kv_local, 0, per_kv * head),)
        return input_strips(which, strip, (query_proj,), d_query, pieces, None)

    def kv_strips(which, partial):
        pieces = ((kv_local, 0, head), (kv_local, head, head))
        return input_strips(which, strip, (key_proj, value_proj), d_kv, pieces, partial)

    def product_of(ring, step, span=(0, 0)):
        return product(place, step, turned, ring, pair, span)

    def terms(ring, span=(0, 0)):
        return [product_of(ring, step, span) for step in range(pair - 1, 0, -1)]

    def exchange(sent):
        return [y_ring(term, pair - 1 - i) for i, term in enumerate(sent)]

    sent = []

    def follow(block, send, extra):
        earlier = sent[-2:-1] + list(extra)
        sent.append(send(after(block, *earlier) if earlier else block))
        return sent[-1]

    keep = jnp.where(across == 0, 1.0, 0.0).reshape(1, 1).astype(jnp.float32)
    q_rings = [[d] for d in d_query]
    d_kv, k_rings, held = [], [], []

    def q_hop(group, *extra):
        q_rings[group].append(follow(q_rings[group][-1], lambda b: z_ring(b, 1), extra))

    def k_hop(group, *extra):
        k_rings[group].append(follow(k_rings[group][-1], lambda b: z_ring(b, 1), extra))

    def far_return(group, *extra):
        four, three_back, two_back, one, mine = parts[group]
        from_three = y_ring(three_back, 1)
        from_one = y_ring(one, 1)
        block = four + jnp.where(across == 0, 0.0, from_three)
        got = follow(block, lambda b: z_shift(b, -1), extra)
        held.append((two_back + jnp.where(across == 0, from_three, from_one) + got, from_one))

    def near_return(group, extra, before):
        block, from_one = held[group]
        far = follow(block, lambda b: z_shift(b, -1), extra)
        far = after(far, *before) if before else far
        mine = parts[group][-1]
        d_kv.append(settle(mine, from_one, far, keep, key_raw[group], *tables))
        k_rings.append([d_kv[group]])

    if short and kv_local == 2:
        q_hop(0)
        far_return(0, q_rings[0][1], *attended)
        q_hop(0)
        near_return(0, [q_rings[0][2]], from_below)
        q_hop(1)
        theirs_q = query_strips(theirs_at)
        far_return(1, theirs_q, q_rings[1][1])
        q_hop(0)
        mine_q = query_strips(mine_at)
        q_hop(1)
        k_hop(0)
        near_return(1, [mine_q, q_rings[0][3]], [q_rings[1][2], k_rings[0][1], *turned])
        q_hop(1)
        q_terms = [terms(q_rings[0])]
        k_hop(0, *q_terms[0])
        q_sent = [exchange(q_terms[0])]
        k_hop(1)
        theirs = kv_strips(theirs_at, theirs_q)
        q_terms.append(terms(q_rings[1]))
        k_hop(0, *q_terms[1])
        sums = kv_strips(mine_at, mine_q) + to_core(theirs)
        from_chips = [to_chip(sums[step], step) for step in range(1, chips)]
        k_hop(1, *q_sent[0])
        k_terms = [terms(k_rings[0])]
        q_sent.append(exchange(q_terms[1]))
        last = after(k_rings[1][-1], sent[-2], sums, *k_terms[0], *q_sent[1])
        tails = [z_ring(last[:, head:], 1), z_ring(last[:, :head], 1)]
        tail_rings = [k_rings[1] + [tail] for tail in tails]
        tail_spans = [(head, head), (0, head)]
    else:
        for group in groups:
            mine = parts[group][reach]
            total = jnp.zeros_like(mine)
            for distance in range(1, reach + 1):
                total = total + shifted(parts[group][reach - distance], -distance)
            d_kv.append(settle(mine, mine, total, 0.0 * keep, key_raw[group], *tables))
            k_rings.append([d_kv[group]])
            for _ in range(CHAIN - 1):
                q_hop(group)
            for _ in range(CHAIN - 1):
                k_hop(group)
        theirs = kv_strips(theirs_at, query_strips(theirs_at))
        sums = kv_strips(mine_at, query_strips(mine_at))
        q_sent = [exchange(terms(ring)) for ring in q_rings]
        sums = sums + to_core(theirs)
        from_chips = [to_chip(sums[step], step) for step in range(1, chips)]
        k_terms = [terms(ring) for ring in k_rings[:-1]]
        tail_rings, tail_spans = [k_rings[-1]], [(0, 2 * head)]

    grad_input = sums[0]
    for arrival in from_chips:
        grad_input = grad_input + arrival

    def finish(ring, arrived, span=(0, 0)):
        total = product_of(ring, 0, span)
        for term in arrived:
            total = total + term
        return total

    grad_query = [finish(ring, arrived) for ring, arrived in zip(q_rings, q_sent)]
    tail_terms = [terms(ring, span) for ring, span in zip(tail_rings, tail_spans)]
    tail_sent = [exchange(term) for term in tail_terms]
    grad_kv = [finish(ring, exchange(term)) for ring, term in zip(k_rings, k_terms)]
    ends = [finish(*each) for each in zip(tail_rings, tail_sent, tail_spans)]
    grad_kv.append(jnp.concatenate(ends[::-1], axis=1))

    return (
        jnp.concatenate(attended, axis=1),
        grad_input.T,
        jnp.concatenate(grad_query, axis=1),
        jnp.concatenate([g[:, :head] for g in grad_kv], axis=1),
        jnp.concatenate([g[:, head:] for g in grad_kv], axis=1),
    )


def solution(mesh):
    seq, members = mesh.devices.shape
    split = Mesh(mesh.devices.reshape(CHAIN, seq // CHAIN, members), ("z", "y", "tensor"))
    tokens = ("z", "y")
    return jax.shard_map(
        local,
        mesh=split,
        in_specs=(
            P(tokens, None),
            P(None, "tensor"),
            P(None, "tensor"),
            P(None, "tensor"),
            P(),
            P(),
            P(),
            P(tokens, "tensor"),
        ),
        out_specs=(
            P(tokens, "tensor"),
            P(tokens, "tensor"),
            P(tokens, "tensor"),
            P(tokens, "tensor"),
            P(tokens, "tensor"),
        ),
        check_vma=False,
    )
```

```python
import functools

import jax
import jax.numpy as jnp
from jax import lax
from jax.experimental import pallas as pl
from jax.experimental.pallas import tpu as pltpu
from jax.sharding import Mesh, PartitionSpec as P

WINDOW = 1024
CHAIN = 4
CORES = 2

MIB = 1024 * 1024
SOON = pl.CostEstimate(flops=1024, bytes_accessed=1024, transcendentals=0)
epsilon = 1e-06


def after(block, *earlier):
    return lax.optimization_barrier((block, earlier))[0]


def rope_tables(positions, head_width):
    middle = head_width // 2
    exponent = 2.0 * jnp.arange(middle).astype(jnp.float32) / head_width
    frequency = 10000.0 ** (-exponent)
    angles = positions.astype(jnp.float32)[:, None] * frequency[None, :]
    return jnp.cos(angles), jnp.sin(angles)


def inverse_rms(vector):
    return lax.rsqrt(jnp.mean(vector * vector, axis=-1, keepdims=True) + epsilon)


def norm_rotate(vector, scaling, cosine, sine):
    middle = vector.shape[-1] // 2
    normed = vector * inverse_rms(vector) * scaling
    low, high = normed[:, :middle], normed[:, middle:]
    return jnp.concatenate([low * cosine - high * sine, high * cosine + low * sine], axis=1)


def norm_rotate_back(grad, vector, scaling, cosine, sine):
    middle = vector.shape[-1] // 2
    low, high = grad[:, :middle], grad[:, middle:]
    d_normed = jnp.concatenate([low * cosine + high * sine, high * cosine - low * sine], axis=1)
    d_normed = d_normed * scaling
    inverse = inverse_rms(vector)
    unit = vector * inverse
    return inverse * (d_normed - unit * jnp.mean(d_normed * unit, axis=-1, keepdims=True))


def halves(array):
    high = array.astype(jnp.bfloat16)
    return high, (array - high.astype(jnp.float32)).astype(jnp.bfloat16)


def three(left, right, left_dim, right_dim):
    def once(a, b):
        return lax.dot_general(
            a, b, (((left_dim,), (right_dim,)), ((), ())), preferred_element_type=jnp.float32
        )

    return once(left[0], right[0]) + (once(left[0], right[1]) + once(left[1], right[0]))


def attention_kernel(blocks, per_kv, *refs):
    query_ref, grad_ref, gain_ref, cos_ref, sin_ref, seg_ref, key_seg_ref = refs[:7]
    kv_refs = refs[7 : 7 + blocks]
    out_ref, d_query_ref = refs[7 + blocks : 9 + blocks]
    d_kv_refs = refs[9 + blocks : 9 + 2 * blocks]
    weight_ref, d_share_ref, share_high, share_low, score_high, score_low = refs[9 + 2 * blocks :]
    rows = query_ref.shape[0]
    head = gain_ref.shape[1]
    factor = head ** (-0.5)
    gain, cosine, sine = gain_ref[...], cos_ref[...], sin_ref[...]
    raw = [query_ref[:, h * head : (h + 1) * head] for h in range(per_kv)]
    q_rot = halves(
        jnp.concatenate([norm_rotate(u, gain, cosine, sine) for u in raw], axis=0)
    )
    grad = halves(
        jnp.concatenate([grad_ref[:, h * head : (h + 1) * head] for h in range(per_kv)], axis=0)
    )
    total = jnp.zeros((1, per_kv * rows), jnp.float32)
    mixed = jnp.zeros((1, per_kv * rows), jnp.float32)
    seg = jnp.concatenate([seg_ref[...]] * per_kv, axis=1)
    turned_keys, turned_values = [], []
    lane = lax.broadcasted_iota(jnp.int32, (rows, rows), 1)
    lane = jnp.concatenate([lane] * per_kv, axis=1)
    row = lax.broadcasted_iota(jnp.int32, (rows, per_kv * rows), 0)
    for j in range(blocks):
        place = slice(j * rows, (j + 1) * rows)
        key, value = kv_refs[j][:, :head], kv_refs[j][:, head:]
        turned_keys.append(key.T)
        turned_values.append(value.T)
        scores = three(halves(key), q_rot, 1, 1) * factor
        distance = (blocks - 1 - j) * rows + lane - row
        allowed = (distance >= 0) & (distance < WINDOW) & (key_seg_ref[place, :] == seg)
        weights = jnp.where(allowed, jnp.exp(scores), 0.0)
        d_shares = three(halves(value), grad, 1, 1)
        weight_ref[place, :] = weights
        d_share_ref[place, :] = d_shares
        total = total + jnp.sum(weights, axis=0, keepdims=True)
        mixed = mixed + jnp.sum(weights * d_shares, axis=0, keepdims=True)
    scale = 1.0 / total
    delta = mixed * scale
    for j in range(blocks):
        place = slice(j * rows, (j + 1) * rows)
        shares = weight_ref[place, :] * scale
        d_scores = shares * (d_share_ref[place, :] - delta) * factor
        share_pair = halves(shares)
        score_pair = halves(d_scores)
        share_high[place, :], share_low[place, :] = share_pair
        score_high[place, :], score_low[place, :] = score_pair
        d_kv_refs[j][:, :head] = three(score_pair, q_rot, 1, 0)
        d_kv_refs[j][:, head:] = three(share_pair, grad, 1, 0)
    turned_out = three(
        halves(jnp.concatenate(turned_values, axis=1)), (share_high[...], share_low[...]), 1, 0
    )
    turned_query = three(
        halves(jnp.concatenate(turned_keys, axis=1)), (score_high[...], score_low[...]), 1, 0
    )
    for h in range(per_kv):
        place = slice(h * rows, (h + 1) * rows)
        columns = slice(h * head, (h + 1) * head)
        out_ref[:, columns] = turned_out[:, place].T
        d_query_ref[:, columns] = norm_rotate_back(
            turned_query[:, place].T, raw[h], gain, cosine, sine
        )


def attention(queries, grads, gain, cosine, sine, query_seg, key_seg, window, per_kv):
    rows, width = queries.shape
    blocks = len(window)
    span = blocks * rows
    flat = jax.ShapeDtypeStruct((rows, width), jnp.float32)
    part = jax.ShapeDtypeStruct(window[0].shape, jnp.float32)
    wide = per_kv * rows
    results = pl.pallas_call(
        functools.partial(attention_kernel, blocks, per_kv),
        out_shape=[flat, flat] + [part] * blocks,
        scratch_shapes=[
            pltpu.VMEM((span, wide), jnp.float32),
            pltpu.VMEM((span, wide), jnp.float32),
            pltpu.VMEM((span, wide), jnp.bfloat16),
            pltpu.VMEM((span, wide), jnp.bfloat16),
            pltpu.VMEM((span, wide), jnp.bfloat16),
            pltpu.VMEM((span, wide), jnp.bfloat16),
        ],
        compiler_params=pltpu.CompilerParams(vmem_limit_bytes=40 * 1024 * 1024),
        cost_estimate=SOON,
    )(queries, grads, gain, cosine, sine, query_seg, key_seg, *window)
    return results[0], results[1], results[2:]


def project_kernel(normed, lanes, source_ref, *refs):
    if normed:
        weight_refs, rest = refs[: 2 * lanes], refs[2 * lanes :]
        gain_ref, cos_ref, sin_ref, raw_ref, packed_ref, total_ref = rest
    else:
        weight_refs, (raw_ref, total_ref) = refs[:lanes], refs[lanes:]
    step = pl.program_id(0)
    stacked = [
        jnp.concatenate([ref[...] for ref in weight_refs[start : start + lanes]], axis=0)
        for start in range(0, len(weight_refs), lanes)
    ]
    weight = stacked[0] if len(stacked) == 1 else jnp.concatenate(stacked, axis=1)
    product = three(halves(source_ref[...]), halves(weight), 1, 0)

    @pl.when(step == 0)
    def _():
        total_ref[...] = product

    @pl.when(step > 0)
    def _():
        total_ref[...] += product

    @pl.when(step == pl.num_programs(0) - 1)
    def _():
        if normed:
            head = gain_ref.shape[1]
            raw = total_ref[:, :head]
            raw_ref[...] = raw
            packed_ref[:, :head] = norm_rotate(raw, gain_ref[...], cos_ref[...], sin_ref[...])
            packed_ref[:, head:] = total_ref[:, head:]
        else:
            raw_ref[...] = total_ref[...]


def project(source, weights, group, columns, extra):
    rows, width = source.shape
    steps, lanes = 5, 3
    tile = width // steps
    thin = tile // lanes
    normed = len(weights) > 1
    wide = columns * len(weights)
    whole = [pl.BlockSpec(e.shape, lambda k: (0, 0)) for e in extra]
    outs = [jax.ShapeDtypeStruct((rows, columns), jnp.float32)]
    if normed:
        outs.append(jax.ShapeDtypeStruct((rows, wide), jnp.float32))
    return pl.pallas_call(
        functools.partial(project_kernel, normed, lanes),
        grid=(steps,),
        out_shape=outs,
        in_specs=[pl.BlockSpec((rows, tile), lambda k: (0, k))]
        + [
            pl.BlockSpec((thin, columns), lambda k, lane=lane: (k * lanes + lane, group))
            for lane in range(lanes)
        ]
        * len(weights)
        + whole,
        out_specs=[pl.BlockSpec(o.shape, lambda k: (0, 0)) for o in outs],
        scratch_shapes=[pltpu.VMEM((rows, wide), jnp.float32)],
        compiler_params=pltpu.CompilerParams(vmem_limit_bytes=56 * MIB),
        cost_estimate=SOON
        if normed
        else pl.CostEstimate(
            flops=24 * rows * width * wide, bytes_accessed=1024, transcendentals=0
        ),
    )(source, *[w for w in weights for _ in range(lanes)], *extra)


def settle_kernel(mine_ref, one_ref, far_ref, keep_ref, raw_ref, gain_ref, cos_ref, sin_ref, out_ref):
    head = gain_ref.shape[1]
    total = mine_ref[...] + one_ref[...] * keep_ref[...] + far_ref[...]
    out_ref[:, :head] = norm_rotate_back(
        total[:, :head], raw_ref[...], gain_ref[...], cos_ref[...], sin_ref[...]
    )
    out_ref[:, head:] = total[:, head:]


def settle(mine, one, far, keep, raw, gain, cosine, sine):
    return pl.pallas_call(
        settle_kernel,
        out_shape=jax.ShapeDtypeStruct(mine.shape, jnp.float32),
        compiler_params=pltpu.CompilerParams(vmem_limit_bytes=16 * MIB),
        cost_estimate=SOON,
    )(mine, one, far, keep, raw, gain, cosine, sine)


def flip_kernel(source_ref, out_ref):
    out_ref[...] = source_ref[...].T


def flip(source):
    rows, width = source.shape
    tile = width // 5
    return pl.pallas_call(
        flip_kernel,
        grid=(5,),
        out_shape=jax.ShapeDtypeStruct((width, rows), jnp.float32),
        in_specs=[pl.BlockSpec((rows, tile), lambda k: (0, k))],
        out_specs=pl.BlockSpec((tile, rows), lambda k: (k, 0)),
        compiler_params=pltpu.CompilerParams(vmem_limit_bytes=16 * MIB),
        cost_estimate=SOON,
    )(source)


def turn_kernel(place_ref, others_ref, own_ref, high_ref, low_ref):
    step = pl.program_id(0)

    @pl.when(step < CHAIN - 1)
    def _():
        high_ref[0], low_ref[0] = halves(others_ref[0])

    @pl.when(step == CHAIN - 1)
    def _():
        high_ref[0], low_ref[0] = halves(own_ref[...])


def turn(place, others, own):
    slab, rows = own.shape
    half = jax.ShapeDtypeStruct((CHAIN, slab, rows), jnp.bfloat16)
    out_spec = pl.BlockSpec((1, slab, rows), lambda i, p: ((p[0] + 1 + i) % CHAIN, 0, 0))
    return pl.pallas_call(
        turn_kernel,
        grid_spec=pltpu.PrefetchScalarGridSpec(
            num_scalar_prefetch=1,
            grid=(CHAIN,),
            in_specs=[
                pl.BlockSpec((1, slab, rows), lambda i, p: (jnp.minimum(i, CHAIN - 2), 0, 0)),
                pl.BlockSpec((slab, rows), lambda i, p: (0, 0)),
            ],
            out_specs=[out_spec, out_spec],
        ),
        out_shape=[half, half],
        compiler_params=pltpu.CompilerParams(vmem_limit_bytes=24 * MIB),
        cost_estimate=SOON,
    )(place, others, own)


def product_kernel(start, place_ref, high_ref, low_ref, *refs):
    blocks, out_ref = refs[:-1], refs[-1]
    total = None
    for hop in range(CHAIN):
        slot = lax.rem(place_ref[0] + (CHAIN - hop), CHAIN)
        block = blocks[hop]
        if block.shape[1] == out_ref.shape[1]:
            block = block[...]
        else:
            block = block[:, start : start + out_ref.shape[1]]
        term = three((high_ref[slot], low_ref[slot]), halves(block), 1, 0)
        total = term if total is None else total + term
    out_ref[...] = total


def product(place, step, turned, blocks, pair, span):
    high, low = turned
    part = high.shape[1] // pair
    rows = high.shape[2]
    columns = span[1] or blocks[0].shape[1]
    spec = pl.BlockSpec((CHAIN, part, rows), lambda i, p: (0, (p[1] + step) % pair, 0))
    return pl.pallas_call(
        functools.partial(product_kernel, span[0]),
        grid_spec=pltpu.PrefetchScalarGridSpec(
            num_scalar_prefetch=1,
            grid=(1,),
            in_specs=[spec, spec] + [pl.BlockSpec(b.shape, lambda i, p: (0, 0)) for b in blocks],
            out_specs=pl.BlockSpec((part, columns), lambda i, p: (0, 0)),
        ),
        out_shape=jax.ShapeDtypeStruct((part, columns), jnp.float32),
        compiler_params=pltpu.CompilerParams(vmem_limit_bytes=28 * MIB),
        cost_estimate=SOON,
    )(place, high, low, *blocks)


def strip_kernel(pieces, added, strips_ref, *refs):
    weight_refs, left_refs = refs[: len(pieces)], refs[len(pieces) : -1]
    total = left_refs[-1][0] if added else None
    left_at = 0
    for ref, (count, start, wide) in zip(weight_refs, pieces):
        for group in range(count):
            left = left_refs[left_at + group][:, start : start + wide]
            right = ref[:, group * wide : (group + 1) * wide]
            term = three(halves(right), halves(left), 1, 1)
            total = term if total is None else total + term
        left_at = left_at if start == 0 and len(pieces) > 1 else left_at + count
    refs[-1][0] = total


def input_strips(strips, strip, weights, lefts, pieces, partial):
    count = strips.shape[0]
    rows = lefts[0].shape[0]
    wide = sum(w.shape[1] for w in weights)
    whole = [pl.BlockSpec(d.shape, lambda i, p: (0, 0)) for d in lefts]
    out_spec = pl.BlockSpec((1, strip, rows), lambda i, p: (i, 0, 0))
    return pl.pallas_call(
        functools.partial(strip_kernel, pieces, partial is not None),
        grid_spec=pltpu.PrefetchScalarGridSpec(
            num_scalar_prefetch=1,
            grid=(count,),
            in_specs=[pl.BlockSpec((strip, w.shape[1]), lambda i, p: (p[i], 0)) for w in weights]
            + whole
            + ([] if partial is None else [out_spec]),
            out_specs=out_spec,
        ),
        out_shape=jax.ShapeDtypeStruct((count, strip, rows), jnp.float32),
        compiler_params=pltpu.CompilerParams(vmem_limit_bytes=56 * MIB),
        cost_estimate=SOON,
    )(strips, *weights, *lefts, *([] if partial is None else [partial]))


def local(hidden_in, query_proj, key_proj, value_proj, query_gain, key_gain, segment_ids, grad_out):
    rows_dev, width = hidden_in.shape
    head = query_gain.shape[0]
    kv_local = key_proj.shape[1] // head
    per_kv = query_proj.shape[1] // key_proj.shape[1]
    pair = lax.axis_size("y")
    count = CHAIN * pair
    members = lax.axis_size("tensor")
    member = lax.axis_index("tensor")
    along = lax.axis_index("z")
    across = lax.axis_index("y")
    seq_index = along * pair + across
    reach = (WINDOW - 1) // rows_dev + 1
    span = (reach + 1) * rows_dev
    slab = width // CHAIN
    part = width // count
    piece = slab // members
    groups = range(kv_local)
    short = pair == 2 and reach == 4

    def z_shift(block, step):
        route = [(i, i + step) for i in range(CHAIN) if 0 <= i + step < CHAIN]
        return lax.ppermute(block, "z", route)

    def z_ring(block, step):
        return lax.ppermute(block, "z", [(i, (i + step) % CHAIN) for i in range(CHAIN)])

    def y_ring(block, step):
        return lax.ppermute(block, "y", [(i, (i + step) % pair) for i in range(pair)])

    def shifted(block, distance):
        route = [(i - distance, i) for i in range(count) if 0 <= i - distance < count]
        return lax.ppermute(block, ("z", "y"), route)

    first_row = seq_index * rows_dev
    positions = first_row + jnp.arange(rows_dev, dtype=jnp.int32)
    cosine, sine = rope_tables(positions, head)
    seg_pad = jnp.concatenate([jnp.full((reach * rows_dev,), -1, jnp.int32), segment_ids])
    key_seg = lax.dynamic_slice_in_dim(seg_pad, first_row, span, 0)[:, None]
    query_seg = lax.dynamic_slice_in_dim(segment_ids, first_row, rows_dev, 0)[None, :]

    def q_columns(array, group):
        return array[:, group * per_kv * head : (group + 1) * per_kv * head]

    key_raw, own, two, queries = [], [], [], []
    tables = (key_gain[None, :], cosine, sine)
    for group in groups:
        source = after(hidden_in, own[-1]) if own else hidden_in
        raw, packed = project(source, (key_proj, value_proj), group, head, tables)
        key_raw.append(raw)
        own.append(packed)
        if short:
            two.append(z_shift(own[group], 1))

    def neighbour(group, *earlier):
        block = jnp.where(across == 0, own[group], two[group])
        return y_ring(after(block, *earlier) if earlier else block, 1)

    def farthest(group, four, *earlier):
        back = after(two[group], *earlier)
        return y_ring(jnp.where(across == 0, back, four), 1)

    for group in groups:
        source = after(hidden_in, *own, *queries)
        queries.append(project(source, (query_proj,), group, per_kv * head, ())[0])

    hidden_rows = flip(after(hidden_in, *queries))
    windows, fours, ones = [], [], []
    if short:
        for group in groups:
            ones.append(neighbour(group))
        for group in groups:
            fours.append(z_shift(after(two[group], own[-1]), 1))
        for group in groups:
            three_back = farthest(group, fours[group], *ones, *fours[: group + 1], hidden_rows)
            windows.append([fours[group], three_back, two[group], ones[group], own[group]])
    else:
        for group in groups:
            windows.append([shifted(own[group], d) for d in range(reach, 0, -1)] + [own[group]])
    def sent_along(source, step):
        start = (along + step) % CHAIN * slab + member * piece
        return z_shift(lax.dynamic_slice_in_dim(source, start, piece, 0), step)

    from_above = [sent_along(hidden_rows, -step) for step in range(1, CHAIN)]

    chips = members // CORES
    chip, core = member // CORES, member % CORES

    def to_core(block):
        return lax.ppermute(block, "tensor", [(i, i ^ 1) for i in range(members)])

    def to_chip(block, step):
        route = [(i, (i + step * CORES) % members) for i in range(members)]
        return lax.ppermute(block, "tensor", route)

    def in_order(blocks, index, axis):
        size = blocks[0].shape[axis]
        both = jnp.concatenate(blocks + blocks[:-1], axis=axis)
        start = (len(blocks) - 1 - index) * size
        return lax.dynamic_slice_in_dim(both, start, len(blocks) * size, axis)

    attended, d_query, parts = [], [], []
    for group in groups:
        ready = attended or from_above
        out, d_q, d_kv = attention(
            after(queries[group], *ready),
            q_columns(grad_out, group),
            query_gain[None, :],
            cosine,
            sine,
            query_seg,
            key_seg,
            windows[group],
            per_kv,
        )
        attended.append(out)
        d_query.append(d_q)
        parts.append(d_kv)

    upward = after(hidden_rows, *attended[:1])
    from_below = [sent_along(upward, step) for step in range(1, CHAIN)]
    pieces = [
        jnp.where(along >= step, from_below[step - 1], from_above[CHAIN - 1 - step])
        for step in range(CHAIN - 1, 0, -1)
    ]
    mine = jnp.stack(pieces)
    chip_rows = in_order([to_core(mine), mine], core, 1)
    arrivals = [to_chip(chip_rows, step) for step in range(chips - 1, 0, -1)]
    others = in_order(arrivals + [chip_rows], chip, 1)
    own_slab = lax.dynamic_slice_in_dim(hidden_rows, along * slab, slab, 0)
    place = jnp.stack([along, across]).astype(jnp.int32)
    turned = turn(place, others, own_slab)

    strip = width // members
    turns = [(chip + step) % chips for step in range(chips)]
    theirs_at = jnp.stack([c * CORES + 1 - core for c in turns]).astype(jnp.int32)
    mine_at = jnp.stack([c * CORES + core for c in turns]).astype(jnp.int32)

    def query_strips(which):
        pieces = ((kv_local, 0, per_kv * head),)
        return input_strips(which, strip, (query_proj,), d_query, pieces, None)

    def kv_strips(which, partial):
        pieces = ((kv_local, 0, head), (kv_local, head, head))
        return input_strips(which, strip, (key_proj, value_proj), d_kv, pieces, partial)

    def product_of(ring, step, span=(0, 0)):
        return product(place, step, turned, ring, pair, span)

    def terms(ring, span=(0, 0)):
        return [product_of(ring, step, span) for step in range(pair - 1, 0, -1)]

    def exchange(sent):
        return [y_ring(term, pair - 1 - i) for i, term in enumerate(sent)]

    sent = []

    def follow(block, send, extra):
        earlier = sent[-2:-1] + list(extra)
        sent.append(send(after(block, *earlier) if earlier else block))
        return sent[-1]

    keep = jnp.where(across == 0, 1.0, 0.0).reshape(1, 1).astype(jnp.float32)
    q_rings = [[d] for d in d_query]
    d_kv, k_rings, held = [], [], []

    def q_hop(group, *extra):
        q_rings[group].append(follow(q_rings[group][-1], lambda b: z_ring(b, 1), extra))

    def k_hop(group, *extra):
        k_rings[group].append(follow(k_rings[group][-1], lambda b: z_ring(b, 1), extra))

    def far_return(group, *extra):
        four, three_back, two_back, one, mine = parts[group]
        from_three = y_ring(three_back, 1)
        from_one = y_ring(one, 1)
        block = four + jnp.where(across == 0, 0.0, from_three)
        got = follow(block, lambda b: z_shift(b, -1), extra)
        held.append((two_back + jnp.where(across == 0, from_three, from_one) + got, from_one))

    def near_return(group, extra, before):
        block, from_one = held[group]
        far = follow(block, lambda b: z_shift(b, -1), extra)
        far = after(far, *before) if before else far
        mine = parts[group][-1]
        d_kv.append(settle(mine, from_one, far, keep, key_raw[group], *tables))
        k_rings.append([d_kv[group]])

    if short and kv_local == 2:
        q_hop(0)
        far_return(0, q_rings[0][1], *attended)
        q_hop(0)
        near_return(0, [q_rings[0][2]], from_below)
        q_hop(1)
        theirs_q = query_strips(theirs_at)
        far_return(1, theirs_q, q_rings[1][1])
        q_hop(0)
        mine_q = query_strips(mine_at)
        q_hop(1)
        k_hop(0)
        near_return(1, [mine_q, q_rings[0][3]], [q_rings[1][2], k_rings[0][1], *turned])
        q_hop(1)
        q_terms = [terms(q_rings[0])]
        k_hop(0, *q_terms[0])
        theirs = kv_strips(theirs_at, theirs_q)
        q_sent = [exchange(q_terms[0])]
        k_hop(1, theirs)
        q_terms.append(terms(q_rings[1]))
        sums = kv_strips(mine_at, mine_q) + to_core(theirs)
        from_chips = [to_chip(sums[step], step) for step in range(1, chips)]
        k_hop(0, *q_terms[1])
        k_hop(1, *q_sent[0])
        k_terms = [terms(k_rings[0])]
        q_sent.append(exchange(q_terms[1]))
        last = after(k_rings[1][-1], sent[-2], *from_chips, *k_terms[0], *q_sent[1])
        tails = [z_ring(last[:, head:], 1), z_ring(last[:, :head], 1)]
        tail_rings = [k_rings[1] + [tail] for tail in tails]
        tail_spans = [(head, head), (0, head)]
    else:
        for group in groups:
            mine = parts[group][reach]
            total = jnp.zeros_like(mine)
            for distance in range(1, reach + 1):
                total = total + shifted(parts[group][reach - distance], -distance)
            d_kv.append(settle(mine, mine, total, 0.0 * keep, key_raw[group], *tables))
            k_rings.append([d_kv[group]])
            for _ in range(CHAIN - 1):
                q_hop(group)
            for _ in range(CHAIN - 1):
                k_hop(group)
        theirs = kv_strips(theirs_at, query_strips(theirs_at))
        sums = kv_strips(mine_at, query_strips(mine_at))
        q_sent = [exchange(terms(ring)) for ring in q_rings]
        sums = sums + to_core(theirs)
        from_chips = [to_chip(sums[step], step) for step in range(1, chips)]
        k_terms = [terms(ring) for ring in k_rings[:-1]]
        tail_rings, tail_spans = [k_rings[-1]], [(0, 2 * head)]

    grad_input = sums[0]
    for arrival in from_chips:
        grad_input = grad_input + arrival

    def finish(ring, arrived, span=(0, 0)):
        total = product_of(ring, 0, span)
        for term in arrived:
            total = total + term
        return total

    grad_query = [finish(ring, arrived) for ring, arrived in zip(q_rings, q_sent)]
    tail_terms = [terms(ring, span) for ring, span in zip(tail_rings, tail_spans)]
    tail_sent = [exchange(term) for term in tail_terms]
    grad_kv = [finish(ring, exchange(term)) for ring, term in zip(k_rings, k_terms)]
    ends = [finish(*each) for each in zip(tail_rings, tail_sent, tail_spans)]
    grad_kv.append(jnp.concatenate(ends[::-1], axis=1))

    return (
        jnp.concatenate(attended, axis=1),
        grad_input.T,
        jnp.concatenate(grad_query, axis=1),
        jnp.concatenate([g[:, :head] for g in grad_kv], axis=1),
        jnp.concatenate([g[:, head:] for g in grad_kv], axis=1),
    )


def solution(mesh):
    seq, members = mesh.devices.shape
    split = Mesh(mesh.devices.reshape(CHAIN, seq // CHAIN, members), ("z", "y", "tensor"))
    tokens = ("z", "y")
    return jax.shard_map(
        local,
        mesh=split,
        in_specs=(
            P(tokens, None),
            P(None, "tensor"),
            P(None, "tensor"),
            P(None, "tensor"),
            P(),
            P(),
            P(),
            P(tokens, "tensor"),
        ),
        out_specs=(
            P(tokens, "tensor"),
            P(tokens, "tensor"),
            P(tokens, "tensor"),
            P(tokens, "tensor"),
            P(tokens, "tensor"),
        ),
        check_vma=False,
    )
```

```python
import functools

import jax
import jax.numpy as jnp
from jax import lax
from jax.experimental import pallas as pl
from jax.experimental.pallas import tpu as pltpu
from jax.sharding import Mesh, PartitionSpec as P

WINDOW = 1024
CHAIN = 4
CORES = 2

MIB = 1024 * 1024
SOON = pl.CostEstimate(flops=1024, bytes_accessed=1024, transcendentals=0)
epsilon = 1e-06


def after(block, *earlier):
    return lax.optimization_barrier((block, earlier))[0]


def rope_tables(positions, head_width):
    middle = head_width // 2
    exponent = 2.0 * jnp.arange(middle).astype(jnp.float32) / head_width
    frequency = 10000.0 ** (-exponent)
    angles = positions.astype(jnp.float32)[:, None] * frequency[None, :]
    return jnp.cos(angles), jnp.sin(angles)


def inverse_rms(vector):
    return lax.rsqrt(jnp.mean(vector * vector, axis=-1, keepdims=True) + epsilon)


def norm_rotate(vector, scaling, cosine, sine):
    middle = vector.shape[-1] // 2
    normed = vector * inverse_rms(vector) * scaling
    low, high = normed[:, :middle], normed[:, middle:]
    return jnp.concatenate([low * cosine - high * sine, high * cosine + low * sine], axis=1)


def norm_rotate_back(grad, vector, scaling, cosine, sine):
    middle = vector.shape[-1] // 2
    low, high = grad[:, :middle], grad[:, middle:]
    d_normed = jnp.concatenate([low * cosine + high * sine, high * cosine - low * sine], axis=1)
    d_normed = d_normed * scaling
    inverse = inverse_rms(vector)
    unit = vector * inverse
    return inverse * (d_normed - unit * jnp.mean(d_normed * unit, axis=-1, keepdims=True))


def halves(array):
    high = array.astype(jnp.bfloat16)
    return high, (array - high.astype(jnp.float32)).astype(jnp.bfloat16)


def three(left, right, left_dim, right_dim):
    def once(a, b):
        return lax.dot_general(
            a, b, (((left_dim,), (right_dim,)), ((), ())), preferred_element_type=jnp.float32
        )

    return once(left[0], right[0]) + (once(left[0], right[1]) + once(left[1], right[0]))


def attention_kernel(blocks, per_kv, *refs):
    query_ref, grad_ref, gain_ref, cos_ref, sin_ref, seg_ref, key_seg_ref = refs[:7]
    kv_refs = refs[7 : 7 + blocks]
    out_ref, d_query_ref = refs[7 + blocks : 9 + blocks]
    d_kv_refs = refs[9 + blocks : 9 + 2 * blocks]
    weight_ref, d_share_ref, share_high, share_low, score_high, score_low = refs[9 + 2 * blocks :]
    rows = query_ref.shape[0]
    head = gain_ref.shape[1]
    factor = head ** (-0.5)
    gain, cosine, sine = gain_ref[...], cos_ref[...], sin_ref[...]
    raw = [query_ref[:, h * head : (h + 1) * head] for h in range(per_kv)]
    q_rot = halves(
        jnp.concatenate([norm_rotate(u, gain, cosine, sine) for u in raw], axis=0)
    )
    grad = halves(
        jnp.concatenate([grad_ref[:, h * head : (h + 1) * head] for h in range(per_kv)], axis=0)
    )
    total = jnp.zeros((1, per_kv * rows), jnp.float32)
    mixed = jnp.zeros((1, per_kv * rows), jnp.float32)
    seg = jnp.concatenate([seg_ref[...]] * per_kv, axis=1)
    turned_keys, turned_values = [], []
    lane = lax.broadcasted_iota(jnp.int32, (rows, rows), 1)
    lane = jnp.concatenate([lane] * per_kv, axis=1)
    row = lax.broadcasted_iota(jnp.int32, (rows, per_kv * rows), 0)
    for j in range(blocks):
        place = slice(j * rows, (j + 1) * rows)
        key, value = kv_refs[j][:, :head], kv_refs[j][:, head:]
        turned_keys.append(key.T)
        turned_values.append(value.T)
        scores = three(halves(key), q_rot, 1, 1) * factor
        distance = (blocks - 1 - j) * rows + lane - row
        allowed = (distance >= 0) & (distance < WINDOW) & (key_seg_ref[place, :] == seg)
        weights = jnp.where(allowed, jnp.exp(scores), 0.0)
        d_shares = three(halves(value), grad, 1, 1)
        weight_ref[place, :] = weights
        d_share_ref[place, :] = d_shares
        total = total + jnp.sum(weights, axis=0, keepdims=True)
        mixed = mixed + jnp.sum(weights * d_shares, axis=0, keepdims=True)
    scale = 1.0 / total
    delta = mixed * scale
    for j in range(blocks):
        place = slice(j * rows, (j + 1) * rows)
        shares = weight_ref[place, :] * scale
        d_scores = shares * (d_share_ref[place, :] - delta) * factor
        share_pair = halves(shares)
        score_pair = halves(d_scores)
        share_high[place, :], share_low[place, :] = share_pair
        score_high[place, :], score_low[place, :] = score_pair
        d_kv_refs[j][:, :head] = three(score_pair, q_rot, 1, 0)
        d_kv_refs[j][:, head:] = three(share_pair, grad, 1, 0)
    turned_out = three(
        halves(jnp.concatenate(turned_values, axis=1)), (share_high[...], share_low[...]), 1, 0
    )
    turned_query = three(
        halves(jnp.concatenate(turned_keys, axis=1)), (score_high[...], score_low[...]), 1, 0
    )
    for h in range(per_kv):
        place = slice(h * rows, (h + 1) * rows)
        columns = slice(h * head, (h + 1) * head)
        out_ref[:, columns] = turned_out[:, place].T
        d_query_ref[:, columns] = norm_rotate_back(
            turned_query[:, place].T, raw[h], gain, cosine, sine
        )


def attention(queries, grads, gain, cosine, sine, query_seg, key_seg, window, per_kv):
    rows, width = queries.shape
    blocks = len(window)
    span = blocks * rows
    flat = jax.ShapeDtypeStruct((rows, width), jnp.float32)
    part = jax.ShapeDtypeStruct(window[0].shape, jnp.float32)
    wide = per_kv * rows
    results = pl.pallas_call(
        functools.partial(attention_kernel, blocks, per_kv),
        out_shape=[flat, flat] + [part] * blocks,
        scratch_shapes=[
            pltpu.VMEM((span, wide), jnp.float32),
            pltpu.VMEM((span, wide), jnp.float32),
            pltpu.VMEM((span, wide), jnp.bfloat16),
            pltpu.VMEM((span, wide), jnp.bfloat16),
            pltpu.VMEM((span, wide), jnp.bfloat16),
            pltpu.VMEM((span, wide), jnp.bfloat16),
        ],
        compiler_params=pltpu.CompilerParams(vmem_limit_bytes=40 * 1024 * 1024),
        cost_estimate=SOON,
    )(queries, grads, gain, cosine, sine, query_seg, key_seg, *window)
    return results[0], results[1], results[2:]


def project_kernel(normed, lanes, source_ref, *refs):
    if normed:
        weight_refs, rest = refs[: 2 * lanes], refs[2 * lanes :]
        gain_ref, cos_ref, sin_ref, raw_ref, packed_ref, total_ref = rest
    else:
        weight_refs, (raw_ref, total_ref) = refs[:lanes], refs[lanes:]
    step = pl.program_id(0)
    stacked = [
        jnp.concatenate([ref[...] for ref in weight_refs[start : start + lanes]], axis=0)
        for start in range(0, len(weight_refs), lanes)
    ]
    weight = stacked[0] if len(stacked) == 1 else jnp.concatenate(stacked, axis=1)
    product = three(halves(source_ref[...]), halves(weight), 1, 0)

    @pl.when(step == 0)
    def _():
        total_ref[...] = product

    @pl.when(step > 0)
    def _():
        total_ref[...] += product

    @pl.when(step == pl.num_programs(0) - 1)
    def _():
        if normed:
            head = gain_ref.shape[1]
            raw = total_ref[:, :head]
            raw_ref[...] = raw
            packed_ref[:, :head] = norm_rotate(raw, gain_ref[...], cos_ref[...], sin_ref[...])
            packed_ref[:, head:] = total_ref[:, head:]
        else:
            raw_ref[...] = total_ref[...]


def project(source, weights, group, columns, extra):
    rows, width = source.shape
    steps, lanes = 5, 3
    tile = width // steps
    thin = tile // lanes
    normed = len(weights) > 1
    wide = columns * len(weights)
    whole = [pl.BlockSpec(e.shape, lambda k: (0, 0)) for e in extra]
    outs = [jax.ShapeDtypeStruct((rows, columns), jnp.float32)]
    if normed:
        outs.append(jax.ShapeDtypeStruct((rows, wide), jnp.float32))
    return pl.pallas_call(
        functools.partial(project_kernel, normed, lanes),
        grid=(steps,),
        out_shape=outs,
        in_specs=[pl.BlockSpec((rows, tile), lambda k: (0, k))]
        + [
            pl.BlockSpec((thin, columns), lambda k, lane=lane: (k * lanes + lane, group))
            for lane in range(lanes)
        ]
        * len(weights)
        + whole,
        out_specs=[pl.BlockSpec(o.shape, lambda k: (0, 0)) for o in outs],
        scratch_shapes=[pltpu.VMEM((rows, wide), jnp.float32)],
        compiler_params=pltpu.CompilerParams(vmem_limit_bytes=56 * MIB),
        cost_estimate=SOON
        if normed
        else pl.CostEstimate(
            flops=24 * rows * width * wide, bytes_accessed=1024, transcendentals=0
        ),
    )(source, *[w for w in weights for _ in range(lanes)], *extra)


def settle_kernel(mine_ref, one_ref, far_ref, keep_ref, raw_ref, gain_ref, cos_ref, sin_ref, out_ref):
    head = gain_ref.shape[1]
    total = mine_ref[...] + one_ref[...] * keep_ref[...] + far_ref[...]
    out_ref[:, :head] = norm_rotate_back(
        total[:, :head], raw_ref[...], gain_ref[...], cos_ref[...], sin_ref[...]
    )
    out_ref[:, head:] = total[:, head:]


def settle(mine, one, far, keep, raw, gain, cosine, sine):
    return pl.pallas_call(
        settle_kernel,
        out_shape=jax.ShapeDtypeStruct(mine.shape, jnp.float32),
        compiler_params=pltpu.CompilerParams(vmem_limit_bytes=16 * MIB),
        cost_estimate=SOON,
    )(mine, one, far, keep, raw, gain, cosine, sine)


def flip_kernel(source_ref, out_ref):
    out_ref[...] = source_ref[...].T


def flip(source):
    rows, width = source.shape
    tile = width // 5
    return pl.pallas_call(
        flip_kernel,
        grid=(5,),
        out_shape=jax.ShapeDtypeStruct((width, rows), jnp.float32),
        in_specs=[pl.BlockSpec((rows, tile), lambda k: (0, k))],
        out_specs=pl.BlockSpec((tile, rows), lambda k: (k, 0)),
        compiler_params=pltpu.CompilerParams(vmem_limit_bytes=16 * MIB),
        cost_estimate=SOON,
    )(source)


def turn_kernel(place_ref, others_ref, own_ref, high_ref, low_ref):
    step = pl.program_id(0)

    @pl.when(step < CHAIN - 1)
    def _():
        high_ref[0], low_ref[0] = halves(others_ref[0])

    @pl.when(step == CHAIN - 1)
    def _():
        high_ref[0], low_ref[0] = halves(own_ref[...])


def turn(place, others, own):
    slab, rows = own.shape
    half = jax.ShapeDtypeStruct((CHAIN, slab, rows), jnp.bfloat16)
    out_spec = pl.BlockSpec((1, slab, rows), lambda i, p: ((p[0] + 1 + i) % CHAIN, 0, 0))
    return pl.pallas_call(
        turn_kernel,
        grid_spec=pltpu.PrefetchScalarGridSpec(
            num_scalar_prefetch=1,
            grid=(CHAIN,),
            in_specs=[
                pl.BlockSpec((1, slab, rows), lambda i, p: (jnp.minimum(i, CHAIN - 2), 0, 0)),
                pl.BlockSpec((slab, rows), lambda i, p: (0, 0)),
            ],
            out_specs=[out_spec, out_spec],
        ),
        out_shape=[half, half],
        compiler_params=pltpu.CompilerParams(vmem_limit_bytes=24 * MIB),
        cost_estimate=SOON,
    )(place, others, own)


def product_kernel(start, place_ref, high_ref, low_ref, *refs):
    blocks, out_ref = refs[:-1], refs[-1]
    total = None
    for hop in range(CHAIN):
        slot = lax.rem(place_ref[0] + (CHAIN - hop), CHAIN)
        block = blocks[hop]
        if block.shape[1] == out_ref.shape[1]:
            block = block[...]
        else:
            block = block[:, start : start + out_ref.shape[1]]
        term = three((high_ref[slot], low_ref[slot]), halves(block), 1, 0)
        total = term if total is None else total + term
    out_ref[...] = total


def product(place, step, turned, blocks, pair, span):
    high, low = turned
    part = high.shape[1] // pair
    rows = high.shape[2]
    columns = span[1] or blocks[0].shape[1]
    spec = pl.BlockSpec((CHAIN, part, rows), lambda i, p: (0, (p[1] + step) % pair, 0))
    return pl.pallas_call(
        functools.partial(product_kernel, span[0]),
        grid_spec=pltpu.PrefetchScalarGridSpec(
            num_scalar_prefetch=1,
            grid=(1,),
            in_specs=[spec, spec] + [pl.BlockSpec(b.shape, lambda i, p: (0, 0)) for b in blocks],
            out_specs=pl.BlockSpec((part, columns), lambda i, p: (0, 0)),
        ),
        out_shape=jax.ShapeDtypeStruct((part, columns), jnp.float32),
        compiler_params=pltpu.CompilerParams(vmem_limit_bytes=28 * MIB),
        cost_estimate=SOON,
    )(place, high, low, *blocks)


def strip_kernel(pieces, added, strips_ref, *refs):
    weight_refs, left_refs = refs[: len(pieces)], refs[len(pieces) : -1]
    total = left_refs[-1][0] if added else None
    left_at = 0
    for ref, (count, start, wide) in zip(weight_refs, pieces):
        for group in range(count):
            left = left_refs[left_at + group][:, start : start + wide]
            right = ref[:, group * wide : (group + 1) * wide]
            term = three(halves(right), halves(left), 1, 1)
            total = term if total is None else total + term
        left_at = left_at if start == 0 and len(pieces) > 1 else left_at + count
    refs[-1][0] = total


def input_strips(strips, strip, weights, lefts, pieces, partial):
    count = strips.shape[0]
    rows = lefts[0].shape[0]
    wide = sum(w.shape[1] for w in weights)
    whole = [pl.BlockSpec(d.shape, lambda i, p: (0, 0)) for d in lefts]
    out_spec = pl.BlockSpec((1, strip, rows), lambda i, p: (i, 0, 0))
    return pl.pallas_call(
        functools.partial(strip_kernel, pieces, partial is not None),
        grid_spec=pltpu.PrefetchScalarGridSpec(
            num_scalar_prefetch=1,
            grid=(count,),
            in_specs=[pl.BlockSpec((strip, w.shape[1]), lambda i, p: (p[i], 0)) for w in weights]
            + whole
            + ([] if partial is None else [out_spec]),
            out_specs=out_spec,
        ),
        out_shape=jax.ShapeDtypeStruct((count, strip, rows), jnp.float32),
        compiler_params=pltpu.CompilerParams(vmem_limit_bytes=56 * MIB),
        cost_estimate=SOON,
    )(strips, *weights, *lefts, *([] if partial is None else [partial]))


def local(hidden_in, query_proj, key_proj, value_proj, query_gain, key_gain, segment_ids, grad_out):
    rows_dev, width = hidden_in.shape
    head = query_gain.shape[0]
    kv_local = key_proj.shape[1] // head
    per_kv = query_proj.shape[1] // key_proj.shape[1]
    pair = lax.axis_size("y")
    count = CHAIN * pair
    members = lax.axis_size("tensor")
    member = lax.axis_index("tensor")
    along = lax.axis_index("z")
    across = lax.axis_index("y")
    seq_index = along * pair + across
    reach = (WINDOW - 1) // rows_dev + 1
    span = (reach + 1) * rows_dev
    slab = width // CHAIN
    part = width // count
    piece = slab // members
    groups = range(kv_local)
    short = pair == 2 and reach == 4

    def z_shift(block, step):
        route = [(i, i + step) for i in range(CHAIN) if 0 <= i + step < CHAIN]
        return lax.ppermute(block, "z", route)

    def z_ring(block, step):
        return lax.ppermute(block, "z", [(i, (i + step) % CHAIN) for i in range(CHAIN)])

    def y_ring(block, step):
        return lax.ppermute(block, "y", [(i, (i + step) % pair) for i in range(pair)])

    def shifted(block, distance):
        route = [(i - distance, i) for i in range(count) if 0 <= i - distance < count]
        return lax.ppermute(block, ("z", "y"), route)

    first_row = seq_index * rows_dev
    positions = first_row + jnp.arange(rows_dev, dtype=jnp.int32)
    cosine, sine = rope_tables(positions, head)
    seg_pad = jnp.concatenate([jnp.full((reach * rows_dev,), -1, jnp.int32), segment_ids])
    key_seg = lax.dynamic_slice_in_dim(seg_pad, first_row, span, 0)[:, None]
    query_seg = lax.dynamic_slice_in_dim(segment_ids, first_row, rows_dev, 0)[None, :]

    def q_columns(array, group):
        return array[:, group * per_kv * head : (group + 1) * per_kv * head]

    key_raw, own, two, queries = [], [], [], []
    tables = (key_gain[None, :], cosine, sine)
    for group in groups:
        source = after(hidden_in, own[-1]) if own else hidden_in
        raw, packed = project(source, (key_proj, value_proj), group, head, tables)
        key_raw.append(raw)
        own.append(packed)
        if short:
            two.append(z_shift(own[group], 1))

    def neighbour(group, *earlier):
        block = jnp.where(across == 0, own[group], two[group])
        return y_ring(after(block, *earlier) if earlier else block, 1)

    def farthest(group, four, *earlier):
        back = after(two[group], *earlier)
        return y_ring(jnp.where(across == 0, back, four), 1)

    for group in groups:
        source = after(hidden_in, *own, *queries)
        queries.append(project(source, (query_proj,), group, per_kv * head, ())[0])

    hidden_rows = flip(after(hidden_in, *queries))
    windows, fours, ones = [], [], []
    if short:
        for group in groups:
            ones.append(neighbour(group))
        for group in groups:
            fours.append(z_shift(after(two[group], own[-1]), 1))
        for group in groups:
            three_back = farthest(group, fours[group], *ones, *fours, hidden_rows)
            windows.append([fours[group], three_back, two[group], ones[group], own[group]])
    else:
        for group in groups:
            windows.append([shifted(own[group], d) for d in range(reach, 0, -1)] + [own[group]])
    pieces = []
    for step in range(CHAIN - 1, 0, -1):
        target = (along + step) % CHAIN
        start = target * slab + member * piece
        pieces.append(z_ring(lax.dynamic_slice_in_dim(hidden_rows, start, piece, 0), step))
    chips = members // CORES
    chip, core = member // CORES, member % CORES

    def to_core(block):
        return lax.ppermute(block, "tensor", [(i, i ^ 1) for i in range(members)])

    def to_chip(block, step):
        route = [(i, (i + step * CORES) % members) for i in range(members)]
        return lax.ppermute(block, "tensor", route)

    def in_order(blocks, index, axis):
        size = blocks[0].shape[axis]
        both = jnp.concatenate(blocks + blocks[:-1], axis=axis)
        start = (len(blocks) - 1 - index) * size
        return lax.dynamic_slice_in_dim(both, start, len(blocks) * size, axis)

    mine = jnp.stack(pieces)
    chip_rows = in_order([to_core(mine), mine], core, 1)
    arrivals = [to_chip(chip_rows, step) for step in range(chips - 1, 0, -1)]
    others = in_order(arrivals + [chip_rows], chip, 1)
    own_slab = lax.dynamic_slice_in_dim(hidden_rows, along * slab, slab, 0)
    place = jnp.stack([along, across]).astype(jnp.int32)
    turned = turn(place, others, own_slab)

    attended, d_query, parts = [], [], []
    for group in groups:
        ready = attended or pieces
        out, d_q, d_kv = attention(
            after(queries[group], *ready),
            q_columns(grad_out, group),
            query_gain[None, :],
            cosine,
            sine,
            query_seg,
            key_seg,
            windows[group],
            per_kv,
        )
        attended.append(out)
        d_query.append(d_q)
        parts.append(d_kv)

    strip = width // members
    turns = [(chip + step) % chips for step in range(chips)]
    theirs_at = jnp.stack([c * CORES + 1 - core for c in turns]).astype(jnp.int32)
    mine_at = jnp.stack([c * CORES + core for c in turns]).astype(jnp.int32)

    def query_strips(which):
        pieces = ((kv_local, 0, per_kv * head),)
        return input_strips(which, strip, (query_proj,), d_query, pieces, None)

    def kv_strips(which, partial):
        pieces = ((kv_local, 0, head), (kv_local, head, head))
        return input_strips(which, strip, (key_proj, value_proj), d_kv, pieces, partial)

    def product_of(ring, step, span=(0, 0)):
        return product(place, step, turned, ring, pair, span)

    def terms(ring, span=(0, 0)):
        return [product_of(ring, step, span) for step in range(pair - 1, 0, -1)]

    def exchange(sent):
        return [y_ring(term, pair - 1 - i) for i, term in enumerate(sent)]

    sent = []

    def follow(block, send, extra):
        earlier = sent[-2:-1] + list(extra)
        sent.append(send(after(block, *earlier) if earlier else block))
        return sent[-1]

    keep = jnp.where(across == 0, 1.0, 0.0).reshape(1, 1).astype(jnp.float32)
    q_rings = [[d] for d in d_query]
    d_kv, k_rings, held = [], [], []

    def q_hop(group, *extra):
        q_rings[group].append(follow(q_rings[group][-1], lambda b: z_ring(b, 1), extra))

    def k_hop(group, *extra):
        k_rings[group].append(follow(k_rings[group][-1], lambda b: z_ring(b, 1), extra))

    def far_return(group, *extra):
        four, three_back, two_back, one, mine = parts[group]
        from_three = y_ring(three_back, 1)
        from_one = y_ring(one, 1)
        block = four + jnp.where(across == 0, 0.0, from_three)
        got = follow(block, lambda b: z_shift(b, -1), extra)
        held.append((two_back + jnp.where(across == 0, from_three, from_one) + got, from_one))

    def near_return(group, *extra):
        block, from_one = held[group]
        far = follow(block, lambda b: z_shift(b, -1), extra)
        mine = parts[group][-1]
        d_kv.append(settle(mine, from_one, far, keep, key_raw[group], *tables))
        k_rings.append([d_kv[group]])

    if short and kv_local == 2:
        q_hop(0)
        far_return(0, q_rings[0][1], *attended)
        q_hop(0)
        near_return(0, q_rings[0][2])
        q_hop(1)
        theirs_q = query_strips(theirs_at)
        far_return(1, theirs_q, q_rings[1][1])
        q_hop(0)
        mine_q = query_strips(mine_at)
        q_hop(1)
        near_return(1, mine_q, q_rings[0][3])
        k_hop(0)
        q_terms = [terms(q_rings[0])]
        q_hop(1, *q_terms[0])
        k_hop(0)
        theirs = kv_strips(theirs_at, theirs_q)
        q_sent = [exchange(q_terms[0])]
        k_hop(1, theirs)
        q_terms.append(terms(q_rings[1]))
        k_hop(0, *q_terms[1])
        sums = kv_strips(mine_at, mine_q)
        k_hop(1, sums, *q_sent[0])
        k_terms = [terms(k_rings[0])]
        q_sent.append(exchange(q_terms[1]))
        last = after(k_rings[1][-1], sent[-2], *k_terms[0], *q_sent[1])
        tails = [z_ring(last[:, head:], 1), z_ring(last[:, :head], 1)]
        tail_rings = [k_rings[1] + [tail] for tail in tails]
        tail_spans = [(head, head), (0, head)]
    else:
        for group in groups:
            mine = parts[group][reach]
            total = jnp.zeros_like(mine)
            for distance in range(1, reach + 1):
                total = total + shifted(parts[group][reach - distance], -distance)
            d_kv.append(settle(mine, mine, total, 0.0 * keep, key_raw[group], *tables))
            k_rings.append([d_kv[group]])
            for _ in range(CHAIN - 1):
                q_hop(group)
            for _ in range(CHAIN - 1):
                k_hop(group)
        theirs = kv_strips(theirs_at, query_strips(theirs_at))
        sums = kv_strips(mine_at, query_strips(mine_at))
        q_sent = [exchange(terms(ring)) for ring in q_rings]
        k_terms = [terms(ring) for ring in k_rings[:-1]]
        tail_rings, tail_spans = [k_rings[-1]], [(0, 2 * head)]

    sums = sums + to_core(theirs)
    grad_input = sums[0]
    for step in range(1, chips):
        grad_input = grad_input + to_chip(sums[step], step)

    def finish(ring, arrived, span=(0, 0)):
        total = product_of(ring, 0, span)
        for term in arrived:
            total = total + term
        return total

    grad_query = [finish(ring, arrived) for ring, arrived in zip(q_rings, q_sent)]
    tail_sent = [exchange(terms(ring, span)) for ring, span in zip(tail_rings, tail_spans)]
    grad_kv = [finish(ring, exchange(term)) for ring, term in zip(k_rings, k_terms)]
    ends = [finish(*each) for each in zip(tail_rings, tail_sent, tail_spans)]
    grad_kv.append(jnp.concatenate(ends[::-1], axis=1))

    return (
        jnp.concatenate(attended, axis=1),
        grad_input.T,
        jnp.concatenate(grad_query, axis=1),
        jnp.concatenate([g[:, :head] for g in grad_kv], axis=1),
        jnp.concatenate([g[:, head:] for g in grad_kv], axis=1),
    )


def solution(mesh):
    seq, members = mesh.devices.shape
    split = Mesh(mesh.devices.reshape(CHAIN, seq // CHAIN, members), ("z", "y", "tensor"))
    tokens = ("z", "y")
    return jax.shard_map(
        local,
        mesh=split,
        in_specs=(
            P(tokens, None),
            P(None, "tensor"),
            P(None, "tensor"),
            P(None, "tensor"),
            P(),
            P(),
            P(),
            P(tokens, "tensor"),
        ),
        out_specs=(
            P(tokens, "tensor"),
            P(tokens, "tensor"),
            P(tokens, "tensor"),
            P(tokens, "tensor"),
            P(tokens, "tensor"),
        ),
        check_vma=False,
    )
```
